256 devices in a mesh: section: 4 (over y), dp: 64 (over z, x, core).
Axes of the slice: x: 4, y: 4, z: 8, core: 2. Of those that a mesh axis runs over, the one named last changes fastest.
Arguments:
- saved_inputs: bfloat16 [4, 4, 8192, 2048], P('section', None, 'dp'), may hold values from -60 to 60, as said below
- out_cotangent: bfloat16 [4, 8192, 2048], P(None, 'dp'), may hold values from -16 to 16
- weights: bfloat16 [4, 2048, 2048], P('section', 'dp'), may hold values from -0.125 to 0.125
- gains: float32 [4, 2048], P('section'), may hold values from 0.5 to 1.5
- row_state: float32 [4, 2048], P('section', 'dp'), may hold values from 655.36 to 32768
- col_state: float32 [4, 2048], P('section'), may hold values from 655.36 to 32768
Outputs:
- input_grads: bfloat16 [4, 4, 8192, 2048], P('section', None, 'dp')
- weight_step: float32 [4, 2048, 2048], P('section', 'dp')
- row_new: float32 [4, 2048], P('section', 'dp')
- col_new: float32 [4, 2048], P('section')
- gain_grad: float32 [4, 2048], P('section')
The draws below stay inside these ranges and needn't reach their ends.
Inputs may be any that keep to these rules, and one draw needn't show every extreme that they name: `saved_inputs`: each section's inputs vary in scale from token to token and from feature to feature.
All inputs are finite; a program needn't handle non-finite values.
Results may differ from the reference program's by a relative error of at most 0.0059.
Values may be sent and summed in bfloat16 or wider, within the bound.
A program may use at most 128 MiB of HBM per device.

```python
import math
import jax
import jax.numpy as jnp
from jax import lax

D = 2048
MICRO = 4
SECTIONS = 4
TOKENS = 8192


def draw_saved_inputs(key, part):
    key = jax.random.fold_in(key, 11)
    first_key, second_key, third_key = jax.random.split(key, 3)
    full_shape = (SECTIONS, MICRO, TOKENS, D)
    base_values = jax.random.normal(first_key, full_shape, jnp.float32)
    log_spread = math.log(10.0)
    row_scale = jnp.exp(log_spread * jax.random.uniform(second_key, (SECTIONS, MICRO, TOKENS, 1), jnp.float32))
    column_scale = jnp.exp(log_spread * jax.random.uniform(third_key, (SECTIONS, 1, 1, D), jnp.float32))
    return jnp.clip(0.1 * base_values * row_scale * column_scale, -60.0, 60.0).astype(jnp.bfloat16)


def draw_out_cotangent(key, part):
    key = jax.random.fold_in(key, 23)
    first_key, second_key = jax.random.split(key, 2)
    full_shape = (MICRO, TOKENS, D)
    token_ramp = 0.6 * jnp.exp(math.log(3.0) * jnp.arange(TOKENS, dtype=jnp.float32) / TOKENS)[None, :, None]
    base_values = jax.random.normal(first_key, full_shape, jnp.float32)
    log_spread = math.log(10.0)
    row_scale = jnp.exp(log_spread * jax.random.uniform(second_key, (MICRO, TOKENS, 1), jnp.float32)) / 3.0
    return jnp.clip(base_values * token_ramp * row_scale, -16.0, 16.0).astype(jnp.bfloat16)


def shard_levels(stream_key, dims, pieces, least, high):
    factor_of = 1.0
    for position, blocks in pieces:
        steps = jax.random.uniform(jax.random.fold_in(jax.random.fold_in(stream_key, 6), position), (blocks,), jnp.float32, least / len(pieces), high / len(pieces))
        factor_of = factor_of * jnp.repeat(jnp.exp(steps), dims[position] // blocks).reshape((-1,) + (1,) * (len(dims) - 1 - position))
    return factor_of


def bell_draw(stream_key, shape, width, reach, cuts=(), kind=jnp.bfloat16):
    array = jax.random.normal(stream_key, shape, jnp.float32) * width
    if len(cuts) > 0:
        array = shard_levels(stream_key, shape, cuts, -0.22, 0.18) * array
    return jnp.clip(array, min=-reach, max=reach).astype(kind)


def setup_inputs(seed: int = 0) -> dict:
    key_list = jax.random.split(jax.random.key(seed), 7)
    saved_inputs = draw_saved_inputs(jax.random.fold_in(key_list[6], 71), 0)
    out_cotangent = draw_out_cotangent(jax.random.fold_in(key_list[6], 71), 0)
    weights = bell_draw(key_list[2], (SECTIONS, D, D), D ** -0.5, 0.125, ((0, 4), (1, 64)))
    gains = jnp.clip(1.0 + 0.1 * jax.random.normal(key_list[3], (SECTIONS, D), jnp.float32), 0.5, 1.5)
    row_state = jnp.clip(jnp.exp(math.log(32768.0) - 3.912023 * jax.random.uniform(key_list[4], (SECTIONS, D), jnp.float32) ** shard_levels(key_list[4], (SECTIONS, D), ((0, 4), (1, 64)), -0.2, 0.2)), 655.36, 32768.0)
    col_state = jnp.clip(jnp.exp(math.log(32768.0) - 3.912023 * jax.random.uniform(key_list[5], (SECTIONS, D), jnp.float32) ** shard_levels(key_list[5], (SECTIONS, D), ((0, 4),), -0.2, 0.2)), 655.36, 32768.0)
    return dict(saved_inputs=saved_inputs, out_cotangent=out_cotangent, weights=weights, gains=gains, row_state=row_state, col_state=col_state)


DECAY_RATE = 0.9
SQUARE_EPS = 1e-30
NORM_EPS = 1e-06

def section_back(saved_rows, grad_out, weight_mat, gain_row):
    inputs_float = saved_rows.astype(jnp.float32)
    inv_rms = lax.rsqrt(lax.optimization_barrier(jnp.mean(inputs_float * inputs_float, axis=-1, keepdims=True)) + NORM_EPS)
    whitened = inputs_float * inv_rms
    normed = (whitened * gain_row).astype(jnp.bfloat16)
    branch = jnp.dot(grad_out, weight_mat.T, preferred_element_type=jnp.float32)
    gained = branch * gain_row
    input_grad = grad_out.astype(jnp.float32) + inv_rms * (gained - whitened * lax.optimization_barrier(jnp.mean(gained * whitened, axis=-1, keepdims=True)))
    return (input_grad.astype(jnp.bfloat16), normed, lax.optimization_barrier(jnp.sum(branch * whitened, axis=0)))

def adafactor_step(weight_grad, row_old, col_old):
    squares = weight_grad * weight_grad + SQUARE_EPS
    row_fresh = DECAY_RATE * row_old + (1.0 - DECAY_RATE) * lax.optimization_barrier(jnp.mean(squares, axis=1))
    col_fresh = DECAY_RATE * col_old + (1.0 - DECAY_RATE) * lax.optimization_barrier(jnp.sum(squares, axis=0)) / D
    row_mean = jnp.mean(row_fresh)
    scaled = weight_grad / jnp.sqrt(row_fresh[:, None] * col_fresh[None, :] / row_mean)
    clip_factor = jnp.maximum(1.0, jnp.sqrt(jnp.mean(scaled * scaled)))
    return (scaled / clip_factor, row_fresh, col_fresh)

def reference(saved_inputs, out_cotangent, weights, gains, row_state, col_state):
    grads_down = out_cotangent
    section_grads = [None] * SECTIONS
    section_steps = [None] * SECTIONS
    section_rows = [None] * SECTIONS
    section_cols = [None] * SECTIONS
    section_gains = [None] * SECTIONS
    for section_idx in range(SECTIONS - 1, -1, -1):
        weight_grad = jnp.zeros((D, D), jnp.float32)
        gain_sum = jnp.zeros((D,), jnp.float32)
        section_outs = []
        for micro_idx in range(MICRO):
            grad_out = grads_down[micro_idx]
            input_grad, normed, gain_part = section_back(saved_inputs[section_idx, micro_idx], grad_out, weights[section_idx], gains[section_idx])
            section_outs.append(input_grad)
            gain_sum = gain_sum + gain_part
            weight_grad = weight_grad + jnp.dot(normed.T, grad_out, preferred_element_type=jnp.float32)
        grads_down = jnp.stack(section_outs)
        section_grads[section_idx] = grads_down
        step_now, row_fresh, col_fresh = adafactor_step(weight_grad, row_state[section_idx], col_state[section_idx])
        section_steps[section_idx] = step_now
        section_rows[section_idx] = row_fresh
        section_cols[section_idx] = col_fresh
        section_gains[section_idx] = gain_sum
    return (jnp.stack(section_grads), jnp.stack(section_steps), jnp.stack(section_rows), jnp.stack(section_cols), jnp.stack(section_gains))
```

```python
import functools

import jax
import jax.numpy as jnp
from jax import lax
from jax.experimental import pallas as pl
from jax.experimental.pallas import tpu as pltpu
from jax.sharding import PartitionSpec as P

DECAY_RATE = 0.9
SQUARE_EPS = 1e-30
NORM_EPS = 1e-06
X = 4
MESH = pl.DeviceIdType.MESH
NT = (((1,), (1,)), ((), ()))
NN = (((1,), (0,)), ((), ()))


def kernel(
    S, Z, R, CA,
    x_hbm, cot_hbm, w_ref, gain_ref, row_ref, col_ref,
    out_hbm, step_ref, rown_ref, coln_ref, gg_ref,
    xs, gs, outs, wg, nt, lt, acc, gained, invs, gacc, wgf, rbuf, sbuf, tv, t1, t2,
    in_sem, lsem, out_sem, ag_s, ag_r, d_s, d_r, own_s, own_r, l_s, l_r,
    y_s, y_r, f_s, f_r, rs_s, rs_r, t_s, t_r,
):
    MICRO, TR, D = xs.shape
    SR = w_ref.shape[0]
    NC = Z * X
    H = TR // R
    U = MICRO * H
    NZP, NZM = Z // 2, Z // 2 - 1
    HB, HS = SR, SR // 2
    QW = min(256, D)
    NQ = D // QW
    s = lax.axis_index("section")
    dp = lax.axis_index("dp")
    z, x, c = dp // (2 * X), (dp // 2) % X, dp % 2

    def chip(dz, dx):
        return ((z + dz + Z) % Z) * X + (x + dx + X) % X

    def dev(dz, dx, flip=0):
        return (s, chip(dz, dx) * 2 + (c + flip) % 2)

    partner = dev(0, 0, 1)

    def remote(src, dst, ss, rs, device):
        return pltpu.make_async_remote_copy(
            src_ref=src, dst_ref=dst, send_sem=ss, recv_sem=rs, device_id=device, device_id_type=MESH
        )

    def load_x():
        return pltpu.make_async_copy(x_hbm, xs, in_sem.at[0])

    def load_cot():
        return pltpu.make_async_copy(cot_hbm, gs.at[:, pl.ds(0, TR)], in_sem.at[1])

    load_x().start()

    @pl.when(s == S - 1)
    def _():
        load_cot().start()

    own_row = pl.multiple_of(c * SR, SR)
    wg[chip(0, 0), pl.ds(own_row, SR), :] = w_ref[...]
    acc[...] = jnp.zeros_like(acc)
    gacc[...] = jnp.zeros_like(gacc)

    barrier = pltpu.get_barrier_semaphore()
    peers = [dev(0, k // 2, k % 2) for k in range(1, 2 * X)] + [dev(k, 0) for k in range(1, Z)]
    for p in peers:
        pl.semaphore_signal(barrier, inc=1, device_id=p, device_id_type=MESH)

    for ds in (1, S - 1):
        pl.semaphore_signal(barrier, inc=1, device_id=((s + ds) % S, dp), device_id_type=MESH)
    pl.semaphore_wait(barrier, len(peers) + 2)

    def nt_send(m):
        return remote(nt.at[m, :, 1 - c], lt.at[m, :, :, pl.ds(TR, TR)], l_s.at[m], l_r.at[m], partner)

    def nt_local(m):
        return pltpu.make_async_copy(nt.at[m, :, c], lt.at[m, :, :, pl.ds(0, TR)], lsem.at[m])

    def prepare(m):
        if m == 0:
            load_x().wait()
        total = jnp.zeros((TR, 1), jnp.float32)
        for q in range(NQ):
            part = xs[m, :, pl.ds(q * QW, QW)].astype(jnp.float32)
            total = total + jnp.sum(part * part, axis=-1, keepdims=True)
        inv = lax.rsqrt(total / D + NORM_EPS)
        invs[m] = jnp.broadcast_to(inv, invs.shape[1:])
        for q in range(NQ):
            cols = pl.ds(q * QW, QW)
            whitened = xs[m, :, cols].astype(jnp.float32) * inv
            normed = whitened * gain_ref[:, cols]
            n = QW // (2 * SR)
            nt[m, pl.ds(q * n, n)] = normed.T.astype(jnp.bfloat16).reshape(n, 2, SR, TR)
        nt_local(m).start()
        nt_send(m).start()

    def own_copy():
        rows = wg.at[chip(0, 0), pl.ds(own_row, SR)]
        return remote(rows, rows, own_s.at[0], own_r.at[0], partner)

    def gather(first, cols, other_cols, order):
        sent = []

        def blk(dz, dx, rows=pl.ds(0, 2 * SR)):
            return wg.at[chip(dz, dx), rows, cols]

        lo, hi = pl.ds(0, HB), pl.ds(HB, HB)

        def put(view, sem, device):
            copy = remote(view, view, ag_s.at[len(sent)], ag_r.at[sem], device)
            copy.start()
            sent.append(copy)

        dsent = []

        def across(view):
            copy = remote(view, view, d_s.at[len(dsent)], d_r.at[0], partner)
            copy.start()
            dsent.append(copy)

        def got(view, sem):
            remote(view, view, ag_s.at[0], ag_r.at[sem], partner).wait_recv()

        right, left, up, down = dev(0, 1), dev(0, -1), dev(1, 0), dev(-1, 0)
        fill = iter(range(MICRO))

        def filler():
            m = next(fill, None)
            if m is not None:
                prepare(m)

        if first == "z":
            zp = lambda k: k - 1
            zm = lambda k: NZP + k - 1
            base = Z - 1

            def x_out(i, rel):
                put(blk(rel, 0), base + 4 * i, right)
                put(blk(rel, 0), base + 4 * i + 1, left)
                if i:
                    across(blk(rel, 0))

            def x_mid(i, rel):
                got(blk(rel, -1), base + 4 * i)
                put(blk(rel, -1, lo), base + 4 * i + 2, right)
                across(blk(rel, -1))
                got(blk(rel, 1), base + 4 * i + 1)
                put(blk(rel, 1, hi), base + 4 * i + 3, left)
                across(blk(rel, 1))

            def x_end(i, rel):
                got(blk(rel, 2, lo), base + 4 * i + 2)
                got(blk(rel, 2, hi), base + 4 * i + 3)
                across(blk(rel, 2))

            put(blk(0, 0), zp(1), up)
            if NZM:
                put(blk(0, 0), zm(1), down)
            x_out(0, 0)
            filler()
            mids, ends, i = [(0, 0)], [], 0
            for k in range(1, NZP + 1):
                fresh = []
                got(blk(-k, 0), zp(k))
                if k < NZP:
                    put(blk(-k, 0), zp(k + 1), up)
                i += 1
                x_out(i, -k)
                fresh.append((i, -k))
                if k <= NZM:
                    got(blk(k, 0), zm(k))
                    if k < NZM:
                        put(blk(k, 0), zm(k + 1), down)
                    i += 1
                    x_out(i, k)
                    fresh.append((i, k))
                for pair in mids:
                    x_mid(*pair)
                for pair in ends:
                    x_end(*pair)
                mids, ends = fresh, mids
                filler()
            for pair in mids:
                x_mid(*pair)
            for pair in ends + mids:
                x_end(*pair)
        else:
            rels = [0, -1, 1, 2]
            hops = [(NZP, NZM), (NZM, NZP), (NZP, NZM), (NZM, NZP)]
            zp = lambda xi, k: 4 + xi * Z + k - 1
            zm = lambda xi, k: 4 + xi * Z + NZP + k - 1

            def z_out(xi):
                put(blk(0, rels[xi]), zp(xi, 1), up)
                put(blk(0, rels[xi]), zm(xi, 1), down)

            put(blk(0, 0), 0, right)
            put(blk(0, 0), 1, left)
            z_out(0)
            filler()
            got(blk(0, -1), 0)
            put(blk(0, -1, lo), 2, right)
            z_out(1)
            across(blk(0, -1))
            got(blk(0, 1), 1)
            put(blk(0, 1, hi), 3, left)
            z_out(2)
            across(blk(0, 1))
            filler()
            got(blk(0, 2, lo), 2)
            got(blk(0, 2, hi), 3)
            z_out(3)
            across(blk(0, 2))
            for k in range(1, NZP + 1):
                for xi in range(4):
                    most_p, most_m = hops[xi]
                    if k <= most_p:
                        got(blk(-k, rels[xi]), zp(xi, k))
                        if k < most_p:
                            put(blk(-k, rels[xi]), zp(xi, k + 1), up)
                        across(blk(-k, rels[xi]))
                    if k <= most_m:
                        got(blk(k, rels[xi]), zm(xi, k))
                        if k < most_m:
                            put(blk(k, rels[xi]), zm(xi, k + 1), down)
                        across(blk(k, rels[xi]))
                filler()
        while True:
            m = next(fill, None)
            if m is None:
                break
            prepare(m)
        whole = wg.at[pl.ds(0, NC - 1), :, other_cols]
        remote(whole, whole, d_s.at[0], d_r.at[0], partner).wait_recv()
        for copy in sent + dsent:
            copy.wait_send()

    own_copy().start()
    own_copy().wait_recv()
    cols_a, cols_b = pl.ds(0, CA), pl.ds(CA, D - CA)

    @pl.when(c == 0)
    def _():
        gather("z", cols_a, cols_b, None)

    @pl.when(c == 1)
    def _():
        gather("x", cols_b, cols_a, None)

    own_copy().wait_send()

    @pl.when(s == S - 1)
    def _():
        load_cot().wait()

    def hand_down(m, rows, u):
        return remote(outs.at[m, rows], gs.at[m, rows], y_s.at[u], y_r.at[u], (s - 1, dp))

    def share(m, h, u):
        rows = pl.ds(pl.multiple_of(h * R, R), R)
        there = pl.ds(pl.multiple_of(TR + h * R, R), R)
        return remote(gs.at[m, rows], gs.at[m, there], f_s.at[u], f_r.at[u], partner)

    def save(m):
        return pltpu.make_async_copy(outs.at[m], out_hbm.at[m], out_sem.at[m])

    def unit(m, h):
        u = m * H + h
        rows = pl.ds(h * R, R)

        @pl.when(s < S - 1)
        def _():
            hand_down(m, rows, u).wait_recv()

        share(m, h, u).start()
        g = gs[m, rows, :]
        inv = invs[m, rows, 0:1]
        dots = jnp.zeros((R, 1), jnp.float32)
        for q in range(NQ):
            cols = pl.ds(q * QW, QW)
            n = QW // (2 * SR)
            w = wg[pl.ds(q * n, n)].reshape(QW, D)
            branch = lax.dot_general(g, w, NT, preferred_element_type=jnp.float32)
            whitened = xs[m, rows, cols].astype(jnp.float32) * inv
            both = branch * whitened
            gacc[:, cols] += jnp.sum(both, axis=0, keepdims=True)
            dots = dots + jnp.sum(both * gain_ref[:, cols], axis=-1, keepdims=True)
            gained[:, cols] = branch * gain_ref[:, cols]
        mean = dots / D
        for q in range(NQ):
            cols = pl.ds(q * QW, QW)
            whitened = xs[m, rows, cols].astype(jnp.float32) * inv
            fresh = gs[m, rows, cols].astype(jnp.float32) + inv * (gained[:, cols] - whitened * mean)
            outs[m, rows, cols] = fresh.astype(jnp.bfloat16)

        @pl.when(s > 0)
        def _():
            hand_down(m, rows, u).start()

    def micro(m, carry):
        for h in range(H):
            unit(m, h)
        save(m).start()
        nt_local(m).wait()
        nt_send(m).wait_recv()
        for h in range(H):
            share(m, h, m * H + h).wait_recv()
        quarter = max(SR, NC * SR // 4)

        def part(r, carry):
            rows = pl.ds(pl.multiple_of(r * quarter, quarter), quarter)
            n = quarter // SR
            lhs = lt[m, pl.ds(r * n, n)].reshape(quarter, 2 * TR)
            acc[rows, :] += lax.dot_general(lhs, gs[m], NN, preferred_element_type=jnp.float32)
            return carry

        lax.fori_loop(0, NC * SR // quarter, part, 0)
        return carry

    lax.fori_loop(0, MICRO, micro, 0)

    def mine(dz, dx):
        return acc[pl.ds(pl.multiple_of(chip(dz, dx) * SR, SR), SR), :]

    def reduce(first):
        sent = []
        right, left, up, down = dev(0, 1), dev(0, -1), dev(1, 0), dev(-1, 0)
        lo, hi, full = pl.ds(0, HS), pl.ds(HS, HS), pl.ds(0, SR)

        def put(i, slot, sem, device, rows=full):
            copy = remote(sbuf.at[i, rows], rbuf.at[slot, rows], rs_s.at[len(sent)], rs_r.at[sem], device)
            copy.start()
            sent.append(copy)

        def got(slot, sem, rows=full):
            view = rbuf.at[slot, rows]
            remote(view, view, rs_s.at[0], rs_r.at[sem], partner).wait_recv()

        def taken(slot, rows=full):
            return rbuf[slot, rows, :].astype(jnp.float32)

        if first == "x":
            rels = []
            for k in range(NZP, 0, -1):
                rels.append(k)
                if k > 1:
                    rels.append(-(k - 1))
            rels.append(0)
            zslot, zsem = 3 * Z, 4 * Z

            def one(i):
                sbuf[3 * i] = mine(rels[i], 2).astype(jnp.bfloat16)
                put(3 * i, 3 * i, 4 * i, right, lo)
                put(3 * i, 3 * i, 4 * i + 1, left, hi)

            def two(i):
                got(3 * i, 4 * i, lo)
                value = mine(rels[i], 1)
                sbuf[3 * i + 1, lo, :] = (value[:HS] + taken(3 * i, lo)).astype(jnp.bfloat16)
                sbuf[3 * i + 1, hi, :] = value[HS:].astype(jnp.bfloat16)
                put(3 * i + 1, 3 * i + 1, 4 * i + 2, right)
                got(3 * i, 4 * i + 1, hi)
                value = mine(rels[i], -1)
                sbuf[3 * i + 2, lo, :] = value[:HS].astype(jnp.bfloat16)
                sbuf[3 * i + 2, hi, :] = (value[HS:] + taken(3 * i, hi)).astype(jnp.bfloat16)
                put(3 * i + 2, 3 * i + 2, 4 * i + 3, left)

            def three(i):
                rel = rels[i]
                got(3 * i + 1, 4 * i + 2)
                got(3 * i + 2, 4 * i + 3)
                value = mine(rel, 0) + taken(3 * i + 1) + taken(3 * i + 2)
                if rel > 0:
                    slot = zslot + rel - 1
                    if rel < NZP:
                        got(slot + 1, zsem + rel)
                        value = value + taken(slot + 1)
                    sbuf[slot] = value.astype(jnp.bfloat16)
                    put(slot, slot, zsem + rel - 1, up)
                elif rel < 0:
                    slot = zslot + NZP - rel - 1
                    if -rel < NZM:
                        got(slot + 1, zsem + NZP - rel)
                        value = value + taken(slot + 1)
                    sbuf[slot] = value.astype(jnp.bfloat16)
                    put(slot, slot, zsem + NZP - rel - 1, down)
                else:
                    got(zslot, zsem)
                    value = value + taken(zslot)
                    if NZM:
                        got(zslot + NZP, zsem + NZP)
                        value = value + taken(zslot + NZP)
                    wgf[...] = value

            for i in range(Z + 4):
                if i < Z:
                    one(i)
                if 0 <= i - 2 < Z:
                    two(i - 2)
                if 0 <= i - 4 < Z:
                    three(i - 4)
        else:
            rels = [2, 1, -1, 0]
            hops = [(NZP, NZM), (NZM, NZP), (NZP, NZM), (NZM, NZP)]
            zs = lambda xi, j: xi * (Z - 1) + j - 1
            xslot = 4 * (Z - 1)

            def link(xi, j, most, base, sign, device):
                value = mine(sign * j, rels[xi])
                slot = base + j - 1
                if j < most:
                    got(slot + 1, slot + 1)
                    value = value + taken(slot + 1)
                sbuf[slot] = value.astype(jnp.bfloat16)
                put(slot, slot, slot, device)

            def total(xi):
                most_p, most_m = hops[xi]
                base = xi * (Z - 1)
                value = mine(0, rels[xi])
                if most_p:
                    got(base, base)
                    value = value + taken(base)
                if most_m:
                    got(base + most_p, base + most_p)
                    value = value + taken(base + most_p)
                return value

            for t in range(NZP):
                for xi in range(4):
                    most_p, most_m = hops[xi]
                    base = xi * (Z - 1)
                    if most_p - t >= 1:
                        link(xi, most_p - t, most_p, base, 1, up)
                    if most_m - t >= 1:
                        link(xi, most_m - t, most_m, base + most_p, -1, down)
            sbuf[xslot] = total(0).astype(jnp.bfloat16)
            put(xslot, xslot, xslot, right, lo)
            put(xslot, xslot, xslot + 1, left, hi)
            ahead, behind = total(1), total(2)
            sbuf[xslot + 1, hi, :] = ahead[HS:].astype(jnp.bfloat16)
            sbuf[xslot + 2, lo, :] = behind[:HS].astype(jnp.bfloat16)
            got(xslot, xslot, lo)
            sbuf[xslot + 1, lo, :] = (ahead[:HS] + taken(xslot, lo)).astype(jnp.bfloat16)
            put(xslot + 1, xslot + 1, xslot + 2, right)
            got(xslot, xslot + 1, hi)
            sbuf[xslot + 2, hi, :] = (behind[HS:] + taken(xslot, hi)).astype(jnp.bfloat16)
            put(xslot + 2, xslot + 2, xslot + 3, left)
            value = total(3)
            got(xslot + 1, xslot + 2)
            got(xslot + 2, xslot + 3)
            wgf[...] = value + taken(xslot + 1) + taken(xslot + 2)
        for copy in sent:
            copy.wait_send()

    @pl.when(c == 0)
    def _():
        reduce("x")

    @pl.when(c == 1)
    def _():
        reduce("z")

    grad = wgf[...]
    row_sum = jnp.sum(grad * grad + SQUARE_EPS, axis=-1, keepdims=True)
    eye = lax.broadcasted_iota(jnp.int32, (SR, SR), 0) == lax.broadcasted_iota(jnp.int32, (SR, SR), 1)
    row_old = jnp.sum(jnp.where(eye, jnp.broadcast_to(row_ref[...], (SR, SR)), 0.0), axis=-1, keepdims=True)
    row_new = DECAY_RATE * row_old + (1.0 - DECAY_RATE) * (row_sum / D)
    rown_ref[...] = jnp.sum(jnp.where(eye, jnp.broadcast_to(row_new, (SR, SR)), 0.0), axis=0, keepdims=True)
    per_row = 1.0 / row_new
    tv[:, pl.ds(0, D)] = jnp.sum(grad * grad + SQUARE_EPS, axis=0, keepdims=True)
    tv[:, pl.ds(D, D)] = jnp.sum(grad * grad * per_row, axis=0, keepdims=True)
    tv[:, pl.ds(2 * D, D)] = gacc[...]
    tv[:, pl.ds(3 * D, 128)] = jnp.broadcast_to(jnp.sum(row_new, axis=0, keepdims=True), (1, 128))

    def spread(src, dst, place, targets, sem0):
        copies = [remote(src, dst.at[place], t_s.at[sem0 + k], t_r.at[sem0 + k], t) for k, t in enumerate(targets)]
        for copy in copies:
            copy.start()
        dst[place] = src[...]
        for copy in copies:
            copy.wait()
        total = dst[0]
        for k in range(1, dst.shape[0]):
            total = total + dst[k]
        return total

    tv[...] = spread(tv, t1, x * 2 + c, peers[: 2 * X - 1], 0)
    t2_src = tv
    sums = spread(t2_src, t2, z, peers[2 * X - 1 :], 2 * X - 1)
    col_new = DECAY_RATE * col_ref[...] + (1.0 - DECAY_RATE) * sums[:, 0:D] / D
    coln_ref[...] = col_new
    gg_ref[...] = sums[:, 2 * D : 3 * D]
    row_mean = sums[:, 3 * D : 3 * D + 1] / D
    total_square = row_mean * jnp.sum(sums[:, D : 2 * D] / col_new, axis=-1, keepdims=True)
    clip = jnp.maximum(1.0, jnp.sqrt(total_square / (D * D)))
    step_ref[...] = grad / jnp.sqrt(row_new * col_new / row_mean) / clip

    for m in range(MICRO):
        save(m).wait()
        nt_send(m).wait_send()

    def settle(u, carry):
        m, h = u // H, u % H
        share(m, h, u).wait_send()

        @pl.when(s > 0)
        def _():
            hand_down(m, pl.ds(pl.multiple_of(h * R, R), R), u).wait_send()

        return carry

    lax.fori_loop(0, U, settle, 0)


def body(saved_inputs, out_cotangent, weights, gains, row_state, col_state):
    S, DP = lax.axis_size("section"), lax.axis_size("dp")
    Z = DP // (2 * X)
    _, MICRO, TR, D = saved_inputs.shape
    SR = weights.shape[1]
    NC = DP // 2
    R = TR // 2
    CA = D // 2
    U = MICRO * (TR // R)
    bf, f32 = jnp.bfloat16, jnp.float32
    dma = pltpu.SemaphoreType.DMA
    vmem = pl.BlockSpec(memory_space=pltpu.VMEM)
    hbm = pl.BlockSpec(memory_space=pl.ANY)
    V = pltpu.VMEM
    scratch = [
        V((MICRO, TR, D), bf),
        V((MICRO, 2 * TR, D), bf),
        V((MICRO, TR, D), bf),
        V((NC, 2 * SR, D), bf),
        V((MICRO, NC, 2, SR, TR), bf),
        V((MICRO, NC, SR, 2 * TR), bf),
        V((NC * SR, D), f32),
        V((R, D), f32),
        V((MICRO, TR, 128), f32),
        V((1, D), f32),
        V((SR, D), f32),
        V((NC - 1, SR, D), bf),
        V((NC - 1, SR, D), bf),
        V((1, 3 * D + 128), f32),
        V((2 * X, 1, 3 * D + 128), f32),
        V((Z, 1, 3 * D + 128), f32),
        dma((2,)),
        dma((MICRO,)),
        dma((MICRO,)),
        dma((5 * Z,)),
        dma((5 * Z,)),
        dma((NC,)),
        dma((1,)),
        dma((1,)),
        dma((1,)),
        dma((MICRO,)),
        dma((MICRO,)),
        dma((U,)),
        dma((U,)),
        dma((U,)),
        dma((U,)),
        dma((5 * Z,)),
        dma((5 * Z,)),
        dma((2 * X + Z,)),
        dma((2 * X + Z,)),
    ]
    outs = pl.pallas_call(
        functools.partial(kernel, S, Z, R, CA),
        out_shape=(
            jax.ShapeDtypeStruct((MICRO, TR, D), bf),
            jax.ShapeDtypeStruct((SR, D), f32),
            jax.ShapeDtypeStruct((1, SR), f32),
            jax.ShapeDtypeStruct((1, D), f32),
            jax.ShapeDtypeStruct((1, D), f32),
        ),
        in_specs=[hbm, hbm, vmem, vmem, vmem, vmem],
        out_specs=(hbm, vmem, vmem, vmem, vmem),
        scratch_shapes=scratch,
        compiler_params=pltpu.CompilerParams(
            collective_id=0, has_side_effects=True, vmem_limit_bytes=60 * 2**20
        ),
        name="relay_back",
    )(saved_inputs[0], out_cotangent, weights[0], gains, row_state, col_state)
    return (outs[0][None], outs[1][None], outs[2], outs[3], outs[4])


def solution(mesh):
    placed = (
        P("section", None, "dp", None),
        P(None, "dp", None),
        P("section", "dp", None),
        P("section", None),
        P("section", "dp"),
        P("section", None),
    )
    return jax.shard_map(
        body,
        mesh=mesh,
        in_specs=placed,
        out_specs=(
            P("section", None, "dp", None),
            P("section", "dp", None),
            P("section", "dp"),
            P("section", None),
            P("section", None),
        ),
        check_vma=False,
    )
```

```python
import functools

import jax
import jax.numpy as jnp
from jax import lax
from jax.experimental import pallas as pl
from jax.experimental.pallas import tpu as pltpu
from jax.sharding import PartitionSpec as P

DECAY_RATE = 0.9
SQUARE_EPS = 1e-30
NORM_EPS = 1e-06
X = 4
MESH = pl.DeviceIdType.MESH
NT = (((1,), (1,)), ((), ()))
NN = (((1,), (0,)), ((), ()))


def kernel(
    S, Z, R, CA,
    x_hbm, cot_hbm, w_ref, gain_ref, row_ref, col_ref,
    out_hbm, step_ref, rown_ref, coln_ref, gg_ref,
    xs, gs, outs, wg, wt, nt, lt, acc, gained, invs, gacc, wgf, rbuf, sbuf, tv, t1, t2, gv, g1, g2,
    in_sem, lsem, out_sem, ag_s, ag_r, d_s, d_r, own_s, own_r, l_s, l_r,
    y_s, y_r, f_s, f_r, rs_s, rs_r, t_s, t_r, g_s, g_r,
):
    MICRO, TR, D = xs.shape
    SR = w_ref.shape[0]
    NC = Z * X
    H = TR // R
    U = MICRO * H
    NZP, NZM = Z // 2, Z // 2 - 1
    HB, HS = SR, SR // 2
    QW = min(256, D)
    NQ = D // QW
    s = lax.axis_index("section")
    dp = lax.axis_index("dp")
    z, x, c = dp // (2 * X), (dp // 2) % X, dp % 2

    def chip(dz, dx):
        return ((z + dz + Z) % Z) * X + (x + dx + X) % X

    def dev(dz, dx, flip=0):
        return (s, chip(dz, dx) * 2 + (c + flip) % 2)

    partner = dev(0, 0, 1)

    def remote(src, dst, ss, rs, device):
        return pltpu.make_async_remote_copy(
            src_ref=src, dst_ref=dst, send_sem=ss, recv_sem=rs, device_id=device, device_id_type=MESH
        )

    def load_x():
        return pltpu.make_async_copy(x_hbm, xs, in_sem.at[0])

    def load_cot():
        return pltpu.make_async_copy(cot_hbm, gs.at[:, pl.ds(0, TR)], in_sem.at[1])

    load_x().start()

    @pl.when(s == S - 1)
    def _():
        load_cot().start()

    own_row = pl.multiple_of(c * SR, SR)
    wg[chip(0, 0), pl.ds(own_row, SR), :] = w_ref[...]

    barrier = pltpu.get_barrier_semaphore()
    peers = [dev(0, k // 2, k % 2) for k in range(1, 2 * X)] + [dev(k, 0) for k in range(1, Z)]
    for p in peers:
        pl.semaphore_signal(barrier, inc=1, device_id=p, device_id_type=MESH)

    for ds in (1, S - 1):
        pl.semaphore_signal(barrier, inc=1, device_id=((s + ds) % S, dp), device_id_type=MESH)
    pl.semaphore_wait(barrier, len(peers) + 2)

    def nt_send(m):
        return remote(nt.at[m, :, 1 - c], lt.at[m, :, :, pl.ds(TR, TR)], l_s.at[m], l_r.at[m], partner)

    def nt_local(m):
        return pltpu.make_async_copy(nt.at[m, :, c], lt.at[m, :, :, pl.ds(0, TR)], lsem.at[m])

    def prepare(m):
        if m == 0:
            load_x().wait()
        total = jnp.zeros((TR, 1), jnp.float32)
        for q in range(NQ):
            part = xs[m, :, pl.ds(q * QW, QW)].astype(jnp.float32)
            total = total + jnp.sum(part * part, axis=-1, keepdims=True)
        inv = lax.rsqrt(total / D + NORM_EPS)
        invs[m] = jnp.broadcast_to(inv, invs.shape[1:])
        for q in range(NQ):
            cols = pl.ds(q * QW, QW)
            whitened = xs[m, :, cols].astype(jnp.float32) * inv
            normed = whitened * gain_ref[:, cols]
            n = QW // (2 * SR)
            nt[m, pl.ds(q * n, n)] = normed.T.astype(jnp.bfloat16).reshape(n, 2, SR, TR)
        nt_local(m).start()
        nt_send(m).start()

    def own_copy():
        rows = wg.at[chip(0, 0), pl.ds(own_row, SR)]
        return remote(rows, rows, own_s.at[0], own_r.at[0], partner)

    def gather(first, cols, other_cols, order):
        def blk(dz, dx, rows=pl.ds(0, 2 * SR)):
            return wg.at[chip(dz, dx), rows, cols]

        lo, hi = pl.ds(0, HB), pl.ds(HB, HB)

        def put(view, sem, device):
            remote(view, view, ag_s.at[0], ag_r.at[sem], device).start()

        def across(view, i):
            remote(view, view, d_s.at[0], d_r.at[i], partner).start()

        def group(i):
            return 0 if i == 0 else (-(i + 1) // 2 if i % 2 else i // 2)

        def flip(i, part):
            first_chip = ((z + group(i) + Z) % Z) * X
            block = wg[pl.ds(first_chip, X), :, part].reshape(X * 2 * SR, part.size)
            width = X * 2 * SR
            wt[part, pl.ds(pl.multiple_of(first_chip * 2 * SR, width), width)] = block.T

        def flip_other(i):
            n = X if i else X - 1
            whole = wg.at[pl.ds(0, n), :, other_cols]
            remote(whole, whole, d_s.at[0], d_r.at[i], partner).wait_recv()
            flip(i, other_cols)

        def got(view, sem):
            remote(view, view, ag_s.at[0], ag_r.at[sem], partner).wait_recv()

        right, left, up, down = dev(0, 1), dev(0, -1), dev(1, 0), dev(-1, 0)
        fill = iter(range(MICRO))

        def filler():
            m = next(fill, None)
            if m is not None:
                prepare(m)
                rows = pl.ds(m * (NC * SR // MICRO), NC * SR // MICRO)
                acc[rows, :] = jnp.zeros((NC * SR // MICRO, D), jnp.float32)
            if m == 0:
                gacc[...] = jnp.zeros_like(gacc)

        if first == "z":
            zp = lambda k: k - 1
            zm = lambda k: NZP + k - 1
            base = Z - 1

            def x_out(i, rel):
                put(blk(rel, 0), base + 4 * i, right)
                put(blk(rel, 0), base + 4 * i + 1, left)
                if i:
                    across(blk(rel, 0), i)

            def x_mid(i, rel):
                got(blk(rel, -1), base + 4 * i)
                put(blk(rel, -1, lo), base + 4 * i + 2, right)
                across(blk(rel, -1), i)
                got(blk(rel, 1), base + 4 * i + 1)
                put(blk(rel, 1, hi), base + 4 * i + 3, left)
                across(blk(rel, 1), i)

            def x_end(i, rel):
                got(blk(rel, 2, lo), base + 4 * i + 2)
                got(blk(rel, 2, hi), base + 4 * i + 3)
                across(blk(rel, 2), i)
                flip(i, cols)

            put(blk(0, 0), zp(1), up)
            if NZM:
                put(blk(0, 0), zm(1), down)
            x_out(0, 0)
            filler()
            mids, ends, i = [(0, 0)], [], 0
            for k in range(1, NZP + 1):
                fresh = []
                got(blk(-k, 0), zp(k))
                if k < NZP:
                    put(blk(-k, 0), zp(k + 1), up)
                i += 1
                x_out(i, -k)
                fresh.append((i, -k))
                if k <= NZM:
                    got(blk(k, 0), zm(k))
                    if k < NZM:
                        put(blk(k, 0), zm(k + 1), down)
                    i += 1
                    x_out(i, k)
                    fresh.append((i, k))
                for pair in mids:
                    x_mid(*pair)
                for pair in ends:
                    x_end(*pair)
                mids, ends = fresh, mids
                filler()
            for pair in mids:
                x_mid(*pair)
            for pair in ends:
                x_end(*pair)
            for i in range(Z - 3):
                flip_other(i)
            for pair in mids:
                x_end(*pair)
            for i in range(Z - 3, Z):
                flip_other(i)
        else:
            rels = [0, -1, 1, 2]
            hops = [(NZP, NZM), (NZM, NZP), (NZP, NZM), (NZM, NZP)]
            zp = lambda xi, k: 4 + xi * Z + k - 1
            zm = lambda xi, k: 4 + xi * Z + NZP + k - 1

            def z_out(xi):
                put(blk(0, rels[xi]), zp(xi, 1), up)
                put(blk(0, rels[xi]), zm(xi, 1), down)

            put(blk(0, 0), 0, right)
            put(blk(0, 0), 1, left)
            z_out(0)
            filler()
            got(blk(0, -1), 0)
            put(blk(0, -1, lo), 2, right)
            z_out(1)
            across(blk(0, -1), 0)
            got(blk(0, 1), 1)
            put(blk(0, 1, hi), 3, left)
            z_out(2)
            across(blk(0, 1), 0)
            filler()
            got(blk(0, 2, lo), 2)
            got(blk(0, 2, hi), 3)
            z_out(3)
            across(blk(0, 2), 0)
            flip(0, cols)
            flipped = 0
            for k in range(1, NZP + 1):
                for xi in range(4):
                    most_p, most_m = hops[xi]
                    if k <= most_p:
                        got(blk(-k, rels[xi]), zp(xi, k))
                        if k < most_p:
                            put(blk(-k, rels[xi]), zp(xi, k + 1), up)
                        across(blk(-k, rels[xi]), 2 * k - 1)
                    if k <= most_m:
                        got(blk(k, rels[xi]), zm(xi, k))
                        if k < most_m:
                            put(blk(k, rels[xi]), zm(xi, k + 1), down)
                        across(blk(k, rels[xi]), 2 * k if k < NZP else 2 * k - 1)
                flip(2 * k - 1, cols)
                if k < NZP:
                    flip(2 * k, cols)
                if k > 2:
                    flip_other(flipped)
                    flip_other(flipped + 1)
                    flipped += 2
                filler()
            for i in range(flipped, Z):
                flip_other(i)
        for _ in range(MICRO):
            filler()
        everything = wg.at[pl.ds(0, NC - 1), :, cols]
        remote(everything, everything, ag_s.at[0], ag_r.at[0], partner).wait_send()
        remote(everything, everything, d_s.at[0], d_r.at[0], partner).wait_send()

    own_copy().start()
    own_copy().wait_recv()
    cols_a, cols_b = pl.ds(0, CA), pl.ds(CA, D - CA)

    @pl.when(c == 0)
    def _():
        gather("z", cols_a, cols_b, None)

    @pl.when(c == 1)
    def _():
        gather("x", cols_b, cols_a, None)

    own_copy().wait_send()

    @pl.when(s == S - 1)
    def _():
        load_cot().wait()

    def hand_down(m, rows, u):
        return remote(outs.at[m, rows], gs.at[m, rows], y_s.at[0], y_r.at[u], (s - 1, dp))

    def share(m, rows, there):
        return remote(gs.at[m, rows], gs.at[m, there], f_s.at[0], f_r.at[m], partner)

    def save():
        return pltpu.make_async_copy(outs, out_hbm, out_sem.at[0])

    def place(u, base=0):
        return u // H, pl.ds(pl.multiple_of(base + (u % H) * R, R), R)

    def differentiate(u):
        m, rows = place(u)
        g = gs[m, rows, :]
        inv = invs[m, rows, 0:1]
        dots = jnp.zeros((R, 1), jnp.float32)
        for q in range(NQ):
            cols = pl.ds(q * QW, QW)
            branch = lax.dot_general(g, wt[:, cols], NN, preferred_element_type=jnp.float32)
            whitened = xs[m, rows, cols].astype(jnp.float32) * inv
            both = branch * whitened
            gacc[:, cols] += jnp.sum(both.reshape(R // 8, 8, QW), axis=0)
            dots = dots + jnp.sum(both * gain_ref[:, cols], axis=-1, keepdims=True)
            gained[:, cols] = branch * gain_ref[:, cols]
        mean = dots / D
        for q in range(NQ):
            cols = pl.ds(q * QW, QW)
            whitened = xs[m, rows, cols].astype(jnp.float32) * inv
            fresh = gs[m, rows, cols].astype(jnp.float32) + inv * (gained[:, cols] - whitened * mean)
            outs[m, rows, cols] = fresh.astype(jnp.bfloat16)

    quarter = NC * SR // H

    def weigh(m, r):
        rows = pl.ds(pl.multiple_of(r * quarter, quarter), quarter)
        n = quarter // SR
        lhs = lt[m, pl.ds(r * n, n)].reshape(quarter, 2 * TR)
        acc[rows, :] += lax.dot_general(lhs, gs[m], NN, preferred_element_type=jnp.float32)

    def meet(m):
        nt_local(m).wait()
        nt_send(m).wait_recv()
        share(m, pl.ds(0, TR), pl.ds(TR, TR)).wait_recv()

    lag = jnp.where(s == 0, 1, 0)

    def tick(u, carry):
        m, rows = place(u)

        @pl.when(s < S - 1)
        def _():
            hand_down(m, rows, u).wait_recv()

        share(m, rows, place(u, TR)[1]).start()

        @pl.when(u >= lag)
        def _():
            differentiate(u - lag)

        @pl.when(s > 0)
        def _():
            hand_down(m, rows, u).start()

        @pl.when(u >= H)
        def _():
            @pl.when(u % H == 0)
            def _():
                meet(m - 1)

            weigh(m - 1, u % H)

        return carry

    lax.fori_loop(0, U, tick, 0)
    meet(MICRO - 1)

    def last(r, carry):
        weigh(MICRO - 1, r)
        return carry

    lax.fori_loop(0, H, last, 0)

    def spread(src, dst, place, targets, ss, rs, sem0):
        return [remote(src, dst.at[place], ss.at[sem0 + k], rs.at[sem0 + k], t) for k, t in enumerate(targets)]

    def added(dst):
        total = dst[0]
        for k in range(1, dst.shape[0]):
            total = total + dst[k]
        return total

    near, far = peers[: 2 * X - 1], peers[2 * X - 1 :]

    def gain_near():
        return spread(gv.at[0], g1, x * 2 + c, near, g_s, g_r, 0)

    def gain_far():
        return spread(gv.at[1], g2, z, far, g_s, g_r, 2 * X - 1)

    def hook_a():
        @pl.when(s == 0)
        def _():
            differentiate(U - 1)

        save().start()
        gv[0] = jnp.sum(gacc[...], axis=0, keepdims=True)
        for copy in gain_near():
            copy.start()
        g1[x * 2 + c] = gv[0]

    def hook_b():
        for copy in gain_near():
            copy.wait_recv()
        gv[1] = added(g1)
        for copy in gain_far():
            copy.start()
        g2[z] = gv[1]

    def mine(dz, dx):
        return acc[pl.ds(pl.multiple_of(chip(dz, dx) * SR, SR), SR), :]

    def reduce(first):
        right, left, up, down = dev(0, 1), dev(0, -1), dev(1, 0), dev(-1, 0)
        lo, hi, full = pl.ds(0, HS), pl.ds(HS, HS), pl.ds(0, SR)

        def put(i, slot, sem, device, rows=full):
            remote(sbuf.at[i, rows], rbuf.at[slot, rows], rs_s.at[0], rs_r.at[sem], device).start()

        def got(slot, sem, rows=full):
            view = rbuf.at[slot, rows]
            remote(view, view, rs_s.at[0], rs_r.at[sem], partner).wait_recv()

        def taken(slot, rows=full):
            return rbuf[slot, rows, :].astype(jnp.float32)

        if first == "x":
            rels = []
            for k in range(NZP, 0, -1):
                rels.append(k)
                if k > 1:
                    rels.append(-(k - 1))
            rels.append(0)
            zslot, zsem = 3 * Z, 4 * Z

            def one(i):
                sbuf[3 * i] = mine(rels[i], 2).astype(jnp.bfloat16)
                put(3 * i, 3 * i, 4 * i, right, lo)
                put(3 * i, 3 * i, 4 * i + 1, left, hi)

            def two(i):
                got(3 * i, 4 * i, lo)
                value = mine(rels[i], 1)
                sbuf[3 * i + 1, lo, :] = (value[:HS] + taken(3 * i, lo)).astype(jnp.bfloat16)
                sbuf[3 * i + 1, hi, :] = value[HS:].astype(jnp.bfloat16)
                put(3 * i + 1, 3 * i + 1, 4 * i + 2, right)
                got(3 * i, 4 * i + 1, hi)
                value = mine(rels[i], -1)
                sbuf[3 * i + 2, lo, :] = value[:HS].astype(jnp.bfloat16)
                sbuf[3 * i + 2, hi, :] = (value[HS:] + taken(3 * i, hi)).astype(jnp.bfloat16)
                put(3 * i + 2, 3 * i + 2, 4 * i + 3, left)

            def three(i):
                rel = rels[i]
                got(3 * i + 1, 4 * i + 2)
                got(3 * i + 2, 4 * i + 3)
                value = mine(rel, 0) + taken(3 * i + 1) + taken(3 * i + 2)
                if rel > 0:
                    slot = zslot + rel - 1
                    if rel < NZP:
                        got(slot + 1, zsem + rel)
                        value = value + taken(slot + 1)
                    sbuf[slot] = value.astype(jnp.bfloat16)
                    put(slot, slot, zsem + rel - 1, up)
                elif rel < 0:
                    slot = zslot + NZP - rel - 1
                    if -rel < NZM:
                        got(slot + 1, zsem + NZP - rel)
                        value = value + taken(slot + 1)
                    sbuf[slot] = value.astype(jnp.bfloat16)
                    put(slot, slot, zsem + NZP - rel - 1, down)
                else:
                    got(zslot, zsem)
                    value = value + taken(zslot)
                    if NZM:
                        got(zslot + NZP, zsem + NZP)
                        value = value + taken(zslot + NZP)
                    wgf[...] = value

            for i in range(Z + 4):
                if i < Z:
                    one(i)
                if 0 <= i - 2 < Z:
                    two(i - 2)
                if 0 <= i - 4 < Z:
                    three(i - 4)
                if i == 2:
                    hook_a()
                if i == Z:
                    hook_b()
        else:
            rels = [2, 1, -1, 0]
            hops = [(NZP, NZM), (NZM, NZP), (NZP, NZM), (NZM, NZP)]
            zs = lambda xi, j: xi * (Z - 1) + j - 1
            xslot = 4 * (Z - 1)

            def link(xi, j, most, base, sign, device):
                value = mine(sign * j, rels[xi])
                slot = base + j - 1
                if j < most:
                    got(slot + 1, slot + 1)
                    value = value + taken(slot + 1)
                sbuf[slot] = value.astype(jnp.bfloat16)
                put(slot, slot, slot, device)

            def total(xi):
                most_p, most_m = hops[xi]
                base = xi * (Z - 1)
                value = mine(0, rels[xi])
                if most_p:
                    got(base, base)
                    value = value + taken(base)
                if most_m:
                    got(base + most_p, base + most_p)
                    value = value + taken(base + most_p)
                return value

            for t in range(NZP):
                for xi in range(4):
                    most_p, most_m = hops[xi]
                    base = xi * (Z - 1)
                    if most_p - t >= 1:
                        link(xi, most_p - t, most_p, base, 1, up)
                    if most_m - t >= 1:
                        link(xi, most_m - t, most_m, base + most_p, -1, down)
                if t == 0:
                    hook_a()
                if t == NZP - 1:
                    hook_b()
            sbuf[xslot] = total(0).astype(jnp.bfloat16)
            put(xslot, xslot, xslot, right, lo)
            put(xslot, xslot, xslot + 1, left, hi)
            ahead, behind = total(1), total(2)
            sbuf[xslot + 1, hi, :] = ahead[HS:].astype(jnp.bfloat16)
            sbuf[xslot + 2, lo, :] = behind[:HS].astype(jnp.bfloat16)
            got(xslot, xslot, lo)
            sbuf[xslot + 1, lo, :] = (ahead[:HS] + taken(xslot, lo)).astype(jnp.bfloat16)
            put(xslot + 1, xslot + 1, xslot + 2, right)
            got(xslot, xslot + 1, hi)
            sbuf[xslot + 2, hi, :] = (behind[HS:] + taken(xslot, hi)).astype(jnp.bfloat16)
            put(xslot + 2, xslot + 2, xslot + 3, left)
            value = total(3)
            got(xslot + 1, xslot + 2)
            got(xslot + 2, xslot + 3)
            wgf[...] = value + taken(xslot + 1) + taken(xslot + 2)
        remote(sbuf, rbuf, rs_s.at[0], rs_r.at[0], partner).wait_send()

    @pl.when(c == 0)
    def _():
        reduce("x")

    @pl.when(c == 1)
    def _():
        reduce("z")

    grad = wgf[...]
    row_sum = jnp.sum(grad * grad + SQUARE_EPS, axis=-1, keepdims=True)
    eye = lax.broadcasted_iota(jnp.int32, (SR, SR), 0) == lax.broadcasted_iota(jnp.int32, (SR, SR), 1)
    row_old = jnp.sum(jnp.where(eye, jnp.broadcast_to(row_ref[...], (SR, SR)), 0.0), axis=-1, keepdims=True)
    row_new = DECAY_RATE * row_old + (1.0 - DECAY_RATE) * (row_sum / D)
    rown_ref[...] = jnp.sum(jnp.where(eye, jnp.broadcast_to(row_new, (SR, SR)), 0.0), axis=0, keepdims=True)
    per_row = 1.0 / row_new
    tv[0, :, pl.ds(0, D)] = jnp.sum(grad * grad + SQUARE_EPS, axis=0, keepdims=True)
    tv[0, :, pl.ds(D, D)] = jnp.sum(grad * grad * per_row, axis=0, keepdims=True)
    tv[0, :, pl.ds(2 * D, 128)] = jnp.broadcast_to(jnp.sum(row_new, axis=0, keepdims=True), (1, 128))

    def exchange(copies, dst, place, value):
        for copy in copies:
            copy.start()
        dst[place] = value
        for copy in copies:
            copy.wait_recv()
        return added(dst)

    near_copies = spread(tv.at[0], t1, x * 2 + c, near, t_s, t_r, 0)
    far_copies = spread(tv.at[1], t2, z, far, t_s, t_r, 2 * X - 1)
    tv[1] = exchange(near_copies, t1, x * 2 + c, tv[0])
    sums = exchange(far_copies, t2, z, tv[1])
    col_new = DECAY_RATE * col_ref[...] + (1.0 - DECAY_RATE) * sums[:, 0:D] / D
    coln_ref[...] = col_new
    row_mean = sums[:, 2 * D : 2 * D + 1] / D
    total_square = row_mean * jnp.sum(sums[:, D : 2 * D] / col_new, axis=-1, keepdims=True)
    clip = jnp.maximum(1.0, jnp.sqrt(total_square / (D * D)))
    step_ref[...] = grad / jnp.sqrt(row_new * col_new / row_mean) / clip
    for copy in gain_far():
        copy.wait_recv()
    gg_ref[...] = added(g2)

    for copy in near_copies + far_copies + gain_near() + gain_far():
        copy.wait_send()
    save().wait()
    for m in range(MICRO):
        nt_send(m).wait_send()
    shared = gs.at[:, pl.ds(0, TR)]
    remote(shared, shared, f_s.at[0], f_r.at[0], partner).wait_send()

    @pl.when(s > 0)
    def _():
        remote(outs, outs, y_s.at[0], y_r.at[0], partner).wait_send()


def deliver(*refs):
    n = len(refs) // 2
    sems = refs[-1]
    sources, results = refs[:n], refs[n : 2 * n]
    copies = []
    for src, dst in zip(sources, results):
        pieces = src.shape[0] if len(src.shape) == 3 else 1
        for k in range(pieces):
            a, b = (src.at[k], dst.at[k]) if pieces > 1 else (src, dst)
            copies.append(pltpu.make_async_copy(a, b, sems.at[len(copies)]))
    for copy in copies:
        copy.start()
    for copy in copies:
        copy.wait()


def body(saved_inputs, out_cotangent, weights, gains, row_state, col_state):
    S, DP = lax.axis_size("section"), lax.axis_size("dp")
    Z = DP // (2 * X)
    _, MICRO, TR, D = saved_inputs.shape
    SR = weights.shape[1]
    NC = DP // 2
    R = TR // 4
    CA = D * 9 // 16
    U = MICRO * (TR // R)
    bf, f32 = jnp.bfloat16, jnp.float32
    dma = pltpu.SemaphoreType.DMA
    vmem = pl.BlockSpec(memory_space=pltpu.VMEM)
    hbm = pl.BlockSpec(memory_space=pl.ANY)
    V = pltpu.VMEM
    scratch = [
        V((MICRO, TR, D), bf),
        V((MICRO, 2 * TR, D), bf),
        V((MICRO, TR, D), bf),
        V((NC, 2 * SR, D), bf),
        V((D, D), bf),
        V((MICRO, NC, 2, SR, TR), bf),
        V((MICRO, NC, SR, 2 * TR), bf),
        V((NC * SR, D), f32),
        V((R, D), f32),
        V((MICRO, TR, 128), f32),
        V((8, D), f32),
        V((SR, D), f32),
        V((NC - 1, SR, D), bf),
        V((NC - 1, SR, D), bf),
        V((2, 1, 2 * D + 128), f32),
        V((2 * X, 1, 2 * D + 128), f32),
        V((Z, 1, 2 * D + 128), f32),
        V((2, 1, D), f32),
        V((2 * X, 1, D), f32),
        V((Z, 1, D), f32),
        dma((2,)),
        dma((MICRO,)),
        dma((1,)),
        dma((1,)),
        dma((5 * Z,)),
        dma((1,)),
        dma((Z,)),
        dma((1,)),
        dma((1,)),
        dma((MICRO,)),
        dma((MICRO,)),
        dma((1,)),
        dma((U,)),
        dma((1,)),
        dma((MICRO,)),
        dma((1,)),
        dma((5 * Z,)),
        dma((2 * X + Z,)),
        dma((2 * X + Z,)),
        dma((2 * X + Z,)),
        dma((2 * X + Z,)),
    ]
    outs = pl.pallas_call(
        functools.partial(kernel, S, Z, R, CA),
        out_shape=(
            jax.ShapeDtypeStruct((MICRO, TR, D), bf),
            jax.ShapeDtypeStruct((SR, D), f32),
            jax.ShapeDtypeStruct((1, SR), f32),
            jax.ShapeDtypeStruct((1, D), f32),
            jax.ShapeDtypeStruct((1, D), f32),
        ),
        in_specs=[hbm, hbm, vmem, vmem, vmem, vmem],
        out_specs=(hbm, vmem, vmem, vmem, vmem),
        scratch_shapes=scratch,
        compiler_params=pltpu.CompilerParams(
            collective_id=0, has_side_effects=True, vmem_limit_bytes=60 * 2**20
        ),
        name="relay_back",
    )(saved_inputs[0], out_cotangent, weights[0], gains, row_state, col_state)
    outs = pl.pallas_call(
        deliver,
        out_shape=tuple(jax.ShapeDtypeStruct(o.shape, o.dtype) for o in outs),
        in_specs=[hbm] * 5,
        out_specs=(hbm,) * 5,
        scratch_shapes=[dma((MICRO + 4,))],
        name="deliver",
    )(*outs)
    return (outs[0][None], outs[1][None], outs[2], outs[3], outs[4])


def solution(mesh):
    placed = (
        P("section", None, "dp", None),
        P(None, "dp", None),
        P("section", "dp", None),
        P("section", None),
        P("section", "dp"),
        P("section", None),
    )
    return jax.shard_map(
        body,
        mesh=mesh,
        in_specs=placed,
        out_specs=(
            P("section", None, "dp", None),
            P("section", "dp", None),
            P("section", "dp"),
            P("section", None),
            P("section", None),
        ),
        check_vma=False,
    )
```

```python
import functools

import jax
import jax.numpy as jnp
from jax import lax
from jax.experimental import pallas as pl
from jax.experimental.pallas import tpu as pltpu
from jax.sharding import PartitionSpec as P

DECAY_RATE = 0.9
SQUARE_EPS = 1e-30
NORM_EPS = 1e-06
X = 4
MESH = pl.DeviceIdType.MESH
NT = (((1,), (1,)), ((), ()))
NN = (((1,), (0,)), ((), ()))


def kernel(
    S, Z, R, CA,
    x_hbm, cot_hbm, w_ref, gain_ref, row_ref, col_ref,
    out_hbm, step_ref, rown_ref, coln_ref, gg_ref,
    xs, gs, outs, wg, wt, nt, lt, acc, gained, invs, gacc, wgf, rbuf, sbuf, tv, t1, t2, gv, g1, g2,
    in_sem, lsem, out_sem, ag_s, ag_r, d_s, d_r, own_s, own_r, l_s, l_r,
    y_s, y_r, f_s, f_r, rs_s, rs_r, t_s, t_r, g_s, g_r,
):
    MICRO, TR, D = xs.shape
    SR = w_ref.shape[0]
    NC = Z * X
    H = TR // R
    U = MICRO * H
    NZP, NZM = Z // 2, Z // 2 - 1
    HB, HS = SR, SR // 2
    QW = min(256, D)
    NQ = D // QW
    s = lax.axis_index("section")
    dp = lax.axis_index("dp")
    z, x, c = dp // (2 * X), (dp // 2) % X, dp % 2

    def chip(dz, dx):
        return ((z + dz + Z) % Z) * X + (x + dx + X) % X

    def dev(dz, dx, flip=0):
        return (s, chip(dz, dx) * 2 + (c + flip) % 2)

    partner = dev(0, 0, 1)

    def remote(src, dst, ss, rs, device):
        return pltpu.make_async_remote_copy(
            src_ref=src, dst_ref=dst, send_sem=ss, recv_sem=rs, device_id=device, device_id_type=MESH
        )

    def load_x():
        return pltpu.make_async_copy(x_hbm, xs, in_sem.at[0])

    def load_cot():
        return pltpu.make_async_copy(cot_hbm, gs.at[:, pl.ds(0, TR)], in_sem.at[1])

    load_x().start()

    @pl.when(s == S - 1)
    def _():
        load_cot().start()

    own_row = pl.multiple_of(c * SR, SR)
    wg[chip(0, 0), pl.ds(own_row, SR), :] = w_ref[...]

    barrier = pltpu.get_barrier_semaphore()
    peers = [dev(0, k // 2, k % 2) for k in range(1, 2 * X)] + [dev(k, 0) for k in range(1, Z)]
    for p in peers:
        pl.semaphore_signal(barrier, inc=1, device_id=p, device_id_type=MESH)

    for ds in (1, S - 1):
        pl.semaphore_signal(barrier, inc=1, device_id=((s + ds) % S, dp), device_id_type=MESH)
    pl.semaphore_wait(barrier, len(peers) + 2)

    def nt_send(m):
        return remote(nt.at[m, :, 1 - c], lt.at[m, :, :, pl.ds(TR, TR)], l_s.at[m], l_r.at[m], partner)

    def nt_local(m):
        return pltpu.make_async_copy(nt.at[m, :, c], lt.at[m, :, :, pl.ds(0, TR)], lsem.at[m])

    def prepare(m):
        if m == 0:
            load_x().wait()
        total = jnp.zeros((TR, 1), jnp.float32)
        for q in range(NQ):
            part = xs[m, :, pl.ds(q * QW, QW)].astype(jnp.float32)
            total = total + jnp.sum(part * part, axis=-1, keepdims=True)
        inv = lax.rsqrt(total / D + NORM_EPS)
        invs[m] = jnp.broadcast_to(inv, invs.shape[1:])
        for q in range(NQ):
            cols = pl.ds(q * QW, QW)
            whitened = xs[m, :, cols].astype(jnp.float32) * inv
            normed = whitened * gain_ref[:, cols]
            n = QW // (2 * SR)
            nt[m, pl.ds(q * n, n)] = normed.T.astype(jnp.bfloat16).reshape(n, 2, SR, TR)
        nt_local(m).start()
        nt_send(m).start()

    def own_copy():
        rows = wg.at[chip(0, 0), pl.ds(own_row, SR)]
        return remote(rows, rows, own_s.at[0], own_r.at[0], partner)

    def gather(first, cols, other_cols, order):
        def blk(dz, dx, rows=pl.ds(0, 2 * SR)):
            return wg.at[chip(dz, dx), rows, cols]

        lo, hi = pl.ds(0, HB), pl.ds(HB, HB)

        def put(view, sem, device):
            remote(view, view, ag_s.at[0], ag_r.at[sem], device).start()

        def across(view, i):
            remote(view, view, d_s.at[0], d_r.at[i], partner).start()

        def group(i):
            return 0 if i == 0 else (-(i + 1) // 2 if i % 2 else i // 2)

        def flip(i, part):
            first_chip = ((z + group(i) + Z) % Z) * X
            block = wg[pl.ds(first_chip, X), :, part].reshape(X * 2 * SR, part.size)
            width = X * 2 * SR
            wt[part, pl.ds(pl.multiple_of(first_chip * 2 * SR, width), width)] = block.T

        def flip_other(i):
            n = X if i else X - 1
            whole = wg.at[pl.ds(0, n), :, other_cols]
            remote(whole, whole, d_s.at[0], d_r.at[i], partner).wait_recv()
            flip(i, other_cols)

        def got(view, sem):
            remote(view, view, ag_s.at[0], ag_r.at[sem], partner).wait_recv()

        right, left, up, down = dev(0, 1), dev(0, -1), dev(1, 0), dev(-1, 0)
        fill = iter(range(MICRO))

        def filler():
            m = next(fill, None)
            if m is not None:
                prepare(m)
                rows = pl.ds(m * (NC * SR // MICRO), NC * SR // MICRO)
                acc[rows, :] = jnp.zeros((NC * SR // MICRO, D), jnp.float32)
            if m == 0:
                gacc[...] = jnp.zeros_like(gacc)

        if first == "z":
            zp = lambda k: k - 1
            zm = lambda k: NZP + k - 1
            base = Z - 1

            def x_out(i, rel):
                put(blk(rel, 0), base + 4 * i, right)
                put(blk(rel, 0), base + 4 * i + 1, left)
                if i:
                    across(blk(rel, 0), i)

            def x_mid(i, rel):
                got(blk(rel, -1), base + 4 * i)
                put(blk(rel, -1, lo), base + 4 * i + 2, right)
                across(blk(rel, -1), i)
                got(blk(rel, 1), base + 4 * i + 1)
                put(blk(rel, 1, hi), base + 4 * i + 3, left)
                across(blk(rel, 1), i)

            def x_end(i, rel):
                got(blk(rel, 2, lo), base + 4 * i + 2)
                got(blk(rel, 2, hi), base + 4 * i + 3)
                across(blk(rel, 2), i)
                flip(i, cols)

            put(blk(0, 0), zp(1), up)
            if NZM:
                put(blk(0, 0), zm(1), down)
            x_out(0, 0)
            filler()
            mids, ends, i = [(0, 0)], [], 0
            for k in range(1, NZP + 1):
                fresh = []
                got(blk(-k, 0), zp(k))
                if k < NZP:
                    put(blk(-k, 0), zp(k + 1), up)
                i += 1
                x_out(i, -k)
                fresh.append((i, -k))
                if k <= NZM:
                    got(blk(k, 0), zm(k))
                    if k < NZM:
                        put(blk(k, 0), zm(k + 1), down)
                    i += 1
                    x_out(i, k)
                    fresh.append((i, k))
                for pair in mids:
                    x_mid(*pair)
                for pair in ends:
                    x_end(*pair)
                mids, ends = fresh, mids
                filler()
            for pair in mids:
                x_mid(*pair)
            for pair in ends:
                x_end(*pair)
            for i in range(Z - 3):
                flip_other(i)
            for pair in mids:
                x_end(*pair)
            for i in range(Z - 3, Z):
                flip_other(i)
        else:
            rels = [0, -1, 1, 2]
            hops = [(NZP, NZM), (NZM, NZP), (NZP, NZM), (NZM, NZP)]
            zp = lambda xi, k: 4 + xi * Z + k - 1
            zm = lambda xi, k: 4 + xi * Z + NZP + k - 1

            def z_out(xi):
                put(blk(0, rels[xi]), zp(xi, 1), up)
                put(blk(0, rels[xi]), zm(xi, 1), down)

            put(blk(0, 0), 0, right)
            put(blk(0, 0), 1, left)
            z_out(0)
            filler()
            got(blk(0, -1), 0)
            put(blk(0, -1, lo), 2, right)
            z_out(1)
            across(blk(0, -1), 0)
            got(blk(0, 1), 1)
            put(blk(0, 1, hi), 3, left)
            z_out(2)
            across(blk(0, 1), 0)
            filler()
            got(blk(0, 2, lo), 2)
            got(blk(0, 2, hi), 3)
            z_out(3)
            across(blk(0, 2), 0)
            flip(0, cols)
            flipped = 0
            for k in range(1, NZP + 1):
                for xi in range(4):
                    most_p, most_m = hops[xi]
                    if k <= most_p:
                        got(blk(-k, rels[xi]), zp(xi, k))
                        if k < most_p:
                            put(blk(-k, rels[xi]), zp(xi, k + 1), up)
                        across(blk(-k, rels[xi]), 2 * k - 1)
                    if k <= most_m:
                        got(blk(k, rels[xi]), zm(xi, k))
                        if k < most_m:
                            put(blk(k, rels[xi]), zm(xi, k + 1), down)
                        across(blk(k, rels[xi]), 2 * k if k < NZP else 2 * k - 1)
                flip(2 * k - 1, cols)
                if k < NZP:
                    flip(2 * k, cols)
                if k > 2:
                    flip_other(flipped)
                    flip_other(flipped + 1)
                    flipped += 2
                filler()
            for i in range(flipped, Z):
                flip_other(i)
        for _ in range(MICRO):
            filler()
        everything = wg.at[pl.ds(0, NC - 1), :, cols]
        remote(everything, everything, ag_s.at[0], ag_r.at[0], partner).wait_send()
        remote(everything, everything, d_s.at[0], d_r.at[0], partner).wait_send()

    own_copy().start()
    own_copy().wait_recv()
    cols_a, cols_b = pl.ds(0, CA), pl.ds(CA, D - CA)

    @pl.when(c == 0)
    def _():
        gather("z", cols_a, cols_b, None)

    @pl.when(c == 1)
    def _():
        gather("x", cols_b, cols_a, None)

    own_copy().wait_send()

    @pl.when(s == S - 1)
    def _():
        load_cot().wait()

    def hand_down(m, rows, u):
        return remote(outs.at[m, rows], gs.at[m, rows], y_s.at[0], y_r.at[u], (s - 1, dp))

    def share(m, rows, there):
        return remote(gs.at[m, rows], gs.at[m, there], f_s.at[0], f_r.at[m], partner)

    def save():
        return pltpu.make_async_copy(outs, out_hbm, out_sem.at[0])

    def place(u, base=0):
        return u // H, pl.ds(pl.multiple_of(base + (u % H) * R, R), R)

    def differentiate(u):
        m, rows = place(u)
        g = gs[m, rows, :]
        inv = invs[m, rows, 0:1]
        dots = jnp.zeros((R, 1), jnp.float32)
        for q in range(NQ):
            cols = pl.ds(q * QW, QW)
            branch = lax.dot_general(g, wt[:, cols], NN, preferred_element_type=jnp.float32)
            whitened = xs[m, rows, cols].astype(jnp.float32) * inv
            both = branch * whitened
            gacc[:, cols] += jnp.sum(both.reshape(R // 8, 8, QW), axis=0)
            dots = dots + jnp.sum(both * gain_ref[:, cols], axis=-1, keepdims=True)
            gained[:, cols] = branch * gain_ref[:, cols]
        mean = dots / D
        for q in range(NQ):
            cols = pl.ds(q * QW, QW)
            whitened = xs[m, rows, cols].astype(jnp.float32) * inv
            fresh = gs[m, rows, cols].astype(jnp.float32) + inv * (gained[:, cols] - whitened * mean)
            outs[m, rows, cols] = fresh.astype(jnp.bfloat16)

    quarter = NC * SR // H

    def weigh(m, r):
        rows = pl.ds(pl.multiple_of(r * quarter, quarter), quarter)
        n = quarter // SR
        lhs = lt[m, pl.ds(r * n, n)].reshape(quarter, 2 * TR)
        acc[rows, :] += lax.dot_general(lhs, gs[m], NN, preferred_element_type=jnp.float32)

    def meet(m):
        nt_local(m).wait()
        nt_send(m).wait_recv()
        share(m, pl.ds(0, TR), pl.ds(TR, TR)).wait_recv()

    lag = jnp.where(s == 0, 1, 0)

    def tick(u, carry):
        m, rows = place(u)

        @pl.when(s < S - 1)
        def _():
            hand_down(m, rows, u).wait_recv()

        share(m, rows, place(u, TR)[1]).start()

        @pl.when(u >= lag)
        def _():
            differentiate(u - lag)

        @pl.when(s > 0)
        def _():
            hand_down(m, rows, u).start()

        @pl.when(u >= H)
        def _():
            @pl.when(u % H == 0)
            def _():
                meet(m - 1)

            weigh(m - 1, u % H)

        return carry

    lax.fori_loop(0, U, tick, 0)
    meet(MICRO - 1)

    def last(r, carry):
        weigh(MICRO - 1, r)
        return carry

    lax.fori_loop(0, H, last, 0)

    def spread(src, dst, place, targets, ss, rs, sem0):
        return [remote(src, dst.at[place], ss.at[sem0 + k], rs.at[sem0 + k], t) for k, t in enumerate(targets)]

    def added(dst):
        total = dst[0]
        for k in range(1, dst.shape[0]):
            total = total + dst[k]
        return total

    near, far = peers[: 2 * X - 1], peers[2 * X - 1 :]

    def gain_near():
        return spread(gv.at[0], g1, x * 2 + c, near, g_s, g_r, 0)

    def gain_far():
        return spread(gv.at[1], g2, z, far, g_s, g_r, 2 * X - 1)

    def hook_a():
        @pl.when(s == 0)
        def _():
            differentiate(U - 1)

        save().start()
        gv[0] = jnp.sum(gacc[...], axis=0, keepdims=True)
        for copy in gain_near():
            copy.start()
        g1[x * 2 + c] = gv[0]

    def hook_b():
        for copy in gain_near():
            copy.wait_recv()
        gv[1] = added(g1)
        for copy in gain_far():
            copy.start()
        g2[z] = gv[1]

    def mine(dz, dx):
        return acc[pl.ds(pl.multiple_of(chip(dz, dx) * SR, SR), SR), :]

    def reduce(first):
        right, left, up, down = dev(0, 1), dev(0, -1), dev(1, 0), dev(-1, 0)
        lo, hi, full = pl.ds(0, HS), pl.ds(HS, HS), pl.ds(0, SR)

        def put(i, slot, sem, device, rows=full):
            remote(sbuf.at[i, rows], rbuf.at[slot, rows], rs_s.at[0], rs_r.at[sem], device).start()

        def got(slot, sem, rows=full):
            view = rbuf.at[slot, rows]
            remote(view, view, rs_s.at[0], rs_r.at[sem], partner).wait_recv()

        def taken(slot, rows=full):
            return rbuf[slot, rows, :].astype(jnp.float32)

        if first == "x":
            rels = []
            for k in range(NZP, 0, -1):
                rels.append(k)
                if k > 1:
                    rels.append(-(k - 1))
            rels.append(0)
            zslot, zsem = 3 * Z, 4 * Z

            def one(i):
                sbuf[3 * i] = mine(rels[i], 2).astype(jnp.bfloat16)
                put(3 * i, 3 * i, 4 * i, right, lo)
                put(3 * i, 3 * i, 4 * i + 1, left, hi)

            def two(i):
                got(3 * i, 4 * i, lo)
                value = mine(rels[i], 1)
                sbuf[3 * i + 1, lo, :] = (value[:HS] + taken(3 * i, lo)).astype(jnp.bfloat16)
                sbuf[3 * i + 1, hi, :] = value[HS:].astype(jnp.bfloat16)
                put(3 * i + 1, 3 * i + 1, 4 * i + 2, right)
                got(3 * i, 4 * i + 1, hi)
                value = mine(rels[i], -1)
                sbuf[3 * i + 2, lo, :] = value[:HS].astype(jnp.bfloat16)
                sbuf[3 * i + 2, hi, :] = (value[HS:] + taken(3 * i, hi)).astype(jnp.bfloat16)
                put(3 * i + 2, 3 * i + 2, 4 * i + 3, left)

            def three(i):
                rel = rels[i]
                got(3 * i + 1, 4 * i + 2)
                got(3 * i + 2, 4 * i + 3)
                value = mine(rel, 0) + taken(3 * i + 1) + taken(3 * i + 2)
                if rel > 0:
                    slot = zslot + rel - 1
                    if rel < NZP:
                        got(slot + 1, zsem + rel)
                        value = value + taken(slot + 1)
                    sbuf[slot] = value.astype(jnp.bfloat16)
                    put(slot, slot, zsem + rel - 1, up)
                elif rel < 0:
                    slot = zslot + NZP - rel - 1
                    if -rel < NZM:
                        got(slot + 1, zsem + NZP - rel)
                        value = value + taken(slot + 1)
                    sbuf[slot] = value.astype(jnp.bfloat16)
                    put(slot, slot, zsem + NZP - rel - 1, down)
                else:
                    got(zslot, zsem)
                    value = value + taken(zslot)
                    if NZM:
                        got(zslot + NZP, zsem + NZP)
                        value = value + taken(zslot + NZP)
                    wgf[...] = value

            for i in range(Z + 4):
                if i < Z:
                    one(i)
                if 0 <= i - 2 < Z:
                    two(i - 2)
                if 0 <= i - 4 < Z:
                    three(i - 4)
                if i == 2:
                    hook_a()
                if i == Z:
                    hook_b()
        else:
            rels = [2, 1, -1, 0]
            hops = [(NZP, NZM), (NZM, NZP), (NZP, NZM), (NZM, NZP)]
            zs = lambda xi, j: xi * (Z - 1) + j - 1
            xslot = 4 * (Z - 1)

            def link(xi, j, most, base, sign, device):
                value = mine(sign * j, rels[xi])
                slot = base + j - 1
                if j < most:
                    got(slot + 1, slot + 1)
                    value = value + taken(slot + 1)
                sbuf[slot] = value.astype(jnp.bfloat16)
                put(slot, slot, slot, device)

            def total(xi):
                most_p, most_m = hops[xi]
                base = xi * (Z - 1)
                value = mine(0, rels[xi])
                if most_p:
                    got(base, base)
                    value = value + taken(base)
                if most_m:
                    got(base + most_p, base + most_p)
                    value = value + taken(base + most_p)
                return value

            for t in range(NZP):
                for xi in range(4):
                    most_p, most_m = hops[xi]
                    base = xi * (Z - 1)
                    if most_p - t >= 1:
                        link(xi, most_p - t, most_p, base, 1, up)
                    if most_m - t >= 1:
                        link(xi, most_m - t, most_m, base + most_p, -1, down)
                if t == 0:
                    hook_a()
                if t == NZP - 1:
                    hook_b()
            sbuf[xslot] = total(0).astype(jnp.bfloat16)
            put(xslot, xslot, xslot, right, lo)
            put(xslot, xslot, xslot + 1, left, hi)
            ahead, behind = total(1), total(2)
            sbuf[xslot + 1, hi, :] = ahead[HS:].astype(jnp.bfloat16)
            sbuf[xslot + 2, lo, :] = behind[:HS].astype(jnp.bfloat16)
            got(xslot, xslot, lo)
            sbuf[xslot + 1, lo, :] = (ahead[:HS] + taken(xslot, lo)).astype(jnp.bfloat16)
            put(xslot + 1, xslot + 1, xslot + 2, right)
            got(xslot, xslot + 1, hi)
            sbuf[xslot + 2, hi, :] = (behind[HS:] + taken(xslot, hi)).astype(jnp.bfloat16)
            put(xslot + 2, xslot + 2, xslot + 3, left)
            value = total(3)
            got(xslot + 1, xslot + 2)
            got(xslot + 2, xslot + 3)
            wgf[...] = value + taken(xslot + 1) + taken(xslot + 2)
        remote(sbuf, rbuf, rs_s.at[0], rs_r.at[0], partner).wait_send()

    @pl.when(c == 0)
    def _():
        reduce("x")

    @pl.when(c == 1)
    def _():
        reduce("z")

    grad = wgf[...]
    row_sum = jnp.sum(grad * grad + SQUARE_EPS, axis=-1, keepdims=True)
    eye = lax.broadcasted_iota(jnp.int32, (SR, SR), 0) == lax.broadcasted_iota(jnp.int32, (SR, SR), 1)
    row_old = jnp.sum(jnp.where(eye, jnp.broadcast_to(row_ref[...], (SR, SR)), 0.0), axis=-1, keepdims=True)
    row_new = DECAY_RATE * row_old + (1.0 - DECAY_RATE) * (row_sum / D)
    rown_ref[...] = jnp.sum(jnp.where(eye, jnp.broadcast_to(row_new, (SR, SR)), 0.0), axis=0, keepdims=True)
    per_row = 1.0 / row_new
    tv[0, :, pl.ds(0, D)] = jnp.sum(grad * grad + SQUARE_EPS, axis=0, keepdims=True)
    tv[0, :, pl.ds(D, D)] = jnp.sum(grad * grad * per_row, axis=0, keepdims=True)
    tv[0, :, pl.ds(2 * D, 128)] = jnp.broadcast_to(jnp.sum(row_new, axis=0, keepdims=True), (1, 128))

    def exchange(copies, dst, place, value):
        for copy in copies:
            copy.start()
        dst[place] = value
        for copy in copies:
            copy.wait_recv()
        return added(dst)

    near_copies = spread(tv.at[0], t1, x * 2 + c, near, t_s, t_r, 0)
    far_copies = spread(tv.at[1], t2, z, far, t_s, t_r, 2 * X - 1)
    tv[1] = exchange(near_copies, t1, x * 2 + c, tv[0])
    sums = exchange(far_copies, t2, z, tv[1])
    col_new = DECAY_RATE * col_ref[...] + (1.0 - DECAY_RATE) * sums[:, 0:D] / D
    coln_ref[...] = col_new
    row_mean = sums[:, 2 * D : 2 * D + 1] / D
    total_square = row_mean * jnp.sum(sums[:, D : 2 * D] / col_new, axis=-1, keepdims=True)
    clip = jnp.maximum(1.0, jnp.sqrt(total_square / (D * D)))
    step_ref[...] = grad / jnp.sqrt(row_new * col_new / row_mean) / clip
    for copy in gain_far():
        copy.wait_recv()
    gg_ref[...] = added(g2)

    for copy in near_copies + far_copies + gain_near() + gain_far():
        copy.wait_send()
    save().wait()
    for m in range(MICRO):
        nt_send(m).wait_send()
    shared = gs.at[:, pl.ds(0, TR)]
    remote(shared, shared, f_s.at[0], f_r.at[0], partner).wait_send()

    @pl.when(s > 0)
    def _():
        remote(outs, outs, y_s.at[0], y_r.at[0], partner).wait_send()


def deliver(*refs):
    n = 5
    sources, results, held, sems = refs[:n], refs[n : 2 * n], refs[2 * n : 3 * n], refs[-1]
    ways = []
    for src, mid, dst in zip(sources, held, results):
        pieces = src.shape[0] if len(src.shape) == 3 else 1
        for k in range(pieces):
            a, m, b = (src.at[k], mid.at[k], dst.at[k]) if pieces > 1 else (src, mid, dst)
            i = len(ways)
            ways.append(
                (
                    pltpu.make_async_copy(a, m, sems.at[0, i]),
                    pltpu.make_async_copy(m, b, sems.at[1, i]),
                )
            )
    for into, _ in ways:
        into.start()
    for into, out in ways:
        into.wait()
        out.start()
    for _, out in ways:
        out.wait()


def body(saved_inputs, out_cotangent, weights, gains, row_state, col_state):
    S, DP = lax.axis_size("section"), lax.axis_size("dp")
    Z = DP // (2 * X)
    _, MICRO, TR, D = saved_inputs.shape
    SR = weights.shape[1]
    NC = DP // 2
    R = TR // 4
    CA = D * 9 // 16
    U = MICRO * (TR // R)
    bf, f32 = jnp.bfloat16, jnp.float32
    dma = pltpu.SemaphoreType.DMA
    vmem = pl.BlockSpec(memory_space=pltpu.VMEM)
    hbm = pl.BlockSpec(memory_space=pl.ANY)
    V = pltpu.VMEM
    scratch = [
        V((MICRO, TR, D), bf),
        V((MICRO, 2 * TR, D), bf),
        V((MICRO, TR, D), bf),
        V((NC, 2 * SR, D), bf),
        V((D, D), bf),
        V((MICRO, NC, 2, SR, TR), bf),
        V((MICRO, NC, SR, 2 * TR), bf),
        V((NC * SR, D), f32),
        V((R, D), f32),
        V((MICRO, TR, 128), f32),
        V((8, D), f32),
        V((SR, D), f32),
        V((NC - 1, SR, D), bf),
        V((NC - 1, SR, D), bf),
        V((2, 1, 2 * D + 128), f32),
        V((2 * X, 1, 2 * D + 128), f32),
        V((Z, 1, 2 * D + 128), f32),
        V((2, 1, D), f32),
        V((2 * X, 1, D), f32),
        V((Z, 1, D), f32),
        dma((2,)),
        dma((MICRO,)),
        dma((1,)),
        dma((1,)),
        dma((5 * Z,)),
        dma((1,)),
        dma((Z,)),
        dma((1,)),
        dma((1,)),
        dma((MICRO,)),
        dma((MICRO,)),
        dma((1,)),
        dma((U,)),
        dma((1,)),
        dma((MICRO,)),
        dma((1,)),
        dma((5 * Z,)),
        dma((2 * X + Z,)),
        dma((2 * X + Z,)),
        dma((2 * X + Z,)),
        dma((2 * X + Z,)),
    ]
    outs = pl.pallas_call(
        functools.partial(kernel, S, Z, R, CA),
        out_shape=(
            jax.ShapeDtypeStruct((MICRO, TR, D), bf),
            jax.ShapeDtypeStruct((SR, D), f32),
            jax.ShapeDtypeStruct((1, SR), f32),
            jax.ShapeDtypeStruct((1, D), f32),
            jax.ShapeDtypeStruct((1, D), f32),
        ),
        in_specs=[hbm, hbm, vmem, vmem, vmem, vmem],
        out_specs=(hbm, vmem, vmem, vmem, vmem),
        scratch_shapes=scratch,
        compiler_params=pltpu.CompilerParams(
            collective_id=0, has_side_effects=True, vmem_limit_bytes=60 * 2**20
        ),
        name="relay_back",
    )(saved_inputs[0], out_cotangent, weights[0], gains, row_state, col_state)
    outs = pl.pallas_call(
        deliver,
        out_shape=tuple(jax.ShapeDtypeStruct(o.shape, o.dtype) for o in outs),
        in_specs=[hbm] * 5,
        out_specs=(hbm,) * 5,
        scratch_shapes=[V(o.shape, o.dtype) for o in outs] + [dma((2, MICRO + 4))],
        name="deliver",
    )(*outs)
    return (outs[0][None], outs[1][None], outs[2], outs[3], outs[4])


def solution(mesh):
    placed = (
        P("section", None, "dp", None),
        P(None, "dp", None),
        P("section", "dp", None),
        P("section", None),
        P("section", "dp"),
        P("section", None),
    )
    return jax.shard_map(
        body,
        mesh=mesh,
        in_specs=placed,
        out_specs=(
            P("section", None, "dp", None),
            P("section", "dp", None),
            P("section", "dp"),
            P("section", None),
            P("section", None),
        ),
        check_vma=False,
    )
```

```python
import functools

import jax
import jax.numpy as jnp
from jax import lax
from jax.experimental import pallas as pl
from jax.experimental.pallas import tpu as pltpu
from jax.sharding import PartitionSpec as P

DECAY_RATE = 0.9
SQUARE_EPS = 1e-30
NORM_EPS = 1e-06
X = 4
MESH = pl.DeviceIdType.MESH
NT = (((1,), (1,)), ((), ()))
NN = (((1,), (0,)), ((), ()))


def kernel(
    S, Z, R, CA,
    x_hbm, cot_hbm, w_ref, gain_ref, row_ref, col_ref,
    out_hbm, step_ref, rown_ref, coln_ref, gg_ref,
    xs, gs, outs, wg, wt, nt, lt, acc, gained, invs, gacc, wgf, rbuf, sbuf, tv, t1, tu, t2, tw, t3, gv, g1, g2,
    in_sem, lsem, out_sem, ag_s, ag_r, d_s, d_r, own_s, own_r, l_s, l_r,
    y_s, y_r, f_s, f_r, rs_s, rs_r, t_s, t_r, g_s, g_r,
):
    MICRO, TR, D = xs.shape
    SR = w_ref.shape[0]
    NC = Z * X
    H = TR // R
    U = MICRO * H
    NZP, NZM = Z // 2, Z // 2 - 1
    HB, HS = SR, SR // 2
    QW = min(256, D)
    NQ = D // QW
    s = lax.axis_index("section")
    dp = lax.axis_index("dp")
    z, x, c = dp // (2 * X), (dp // 2) % X, dp % 2

    def chip(dz, dx):
        return ((z + dz + Z) % Z) * X + (x + dx + X) % X

    def dev(dz, dx, flip=0):
        return (s, chip(dz, dx) * 2 + (c + flip) % 2)

    partner = dev(0, 0, 1)

    def remote(src, dst, ss, rs, device):
        return pltpu.make_async_remote_copy(
            src_ref=src, dst_ref=dst, send_sem=ss, recv_sem=rs, device_id=device, device_id_type=MESH
        )

    def load_x():
        return pltpu.make_async_copy(x_hbm, xs, in_sem.at[0])

    def load_cot():
        return pltpu.make_async_copy(cot_hbm, gs.at[:, pl.ds(0, TR)], in_sem.at[1])

    load_x().start()

    @pl.when(s == S - 1)
    def _():
        load_cot().start()

    own_row = pl.multiple_of(c * SR, SR)
    other_row = pl.multiple_of((1 - c) * SR, SR)
    wg[chip(0, 0), pl.ds(own_row, SR), :] = w_ref[...]

    barrier = pltpu.get_barrier_semaphore()
    peers = [dev(0, k // 2, k % 2) for k in range(1, 2 * X)] + [dev(k, 0) for k in range(1, Z)]
    for p in peers:
        pl.semaphore_signal(barrier, inc=1, device_id=p, device_id_type=MESH)

    for ds in (1, S - 1):
        pl.semaphore_signal(barrier, inc=1, device_id=((s + ds) % S, dp), device_id_type=MESH)
    pl.semaphore_wait(barrier, len(peers) + 2)

    def nt_send(m):
        return remote(nt.at[m, :, 1 - c], lt.at[m, :, :, pl.ds(TR, TR)], l_s.at[m], l_r.at[m], partner)

    def nt_local(m):
        return pltpu.make_async_copy(nt.at[m, :, c], lt.at[m, :, :, pl.ds(0, TR)], lsem.at[m])

    def prepare(m):
        if m == 0:
            load_x().wait()
        total = jnp.zeros((TR, 1), jnp.float32)
        for q in range(NQ):
            part = xs[m, :, pl.ds(q * QW, QW)].astype(jnp.float32)
            total = total + jnp.sum(part * part, axis=-1, keepdims=True)
        inv = lax.rsqrt(total / D + NORM_EPS)
        invs[m] = jnp.broadcast_to(inv, invs.shape[1:])
        for q in range(NQ):
            cols = pl.ds(q * QW, QW)
            whitened = xs[m, :, cols].astype(jnp.float32) * inv
            normed = whitened * gain_ref[:, cols]
            n = QW // (2 * SR)
            nt[m, pl.ds(q * n, n)] = normed.T.astype(jnp.bfloat16).reshape(n, 2, SR, TR)
        nt_local(m).start()
        nt_send(m).start()

    def own_copy():
        rows = wg.at[chip(0, 0), pl.ds(own_row, SR)]
        return remote(rows, rows, own_s.at[0], own_r.at[0], partner)

    def gather(first, cols, other_cols, order):
        def blk(dz, dx, rows=pl.ds(0, 2 * SR)):
            return wg.at[chip(dz, dx), rows, cols]

        lo, hi = pl.ds(0, HB), pl.ds(HB, HB)

        def put(view, sem, device):
            remote(view, view, ag_s.at[0], ag_r.at[sem], device).start()

        def across(view, i):
            remote(view, view, d_s.at[0], d_r.at[i], partner).start()

        def put_own(base_rows, places):
            for sem, device in places:
                put(blk(0, 0, pl.ds(base_rows, SR)), sem, device)

        def group(i):
            return 0 if i == 0 else (-(i + 1) // 2 if i % 2 else i // 2)

        def flip(i, part):
            first_chip = ((z + group(i) + Z) % Z) * X
            block = wg[pl.ds(first_chip, X), :, part].reshape(X * 2 * SR, part.size)
            width = X * 2 * SR
            wt[part, pl.ds(pl.multiple_of(first_chip * 2 * SR, width), width)] = block.T

        def flip_other(i):
            n = X if i else X - 1
            whole = wg.at[pl.ds(0, n), :, other_cols]
            remote(whole, whole, d_s.at[0], d_r.at[i], partner).wait_recv()
            flip(i, other_cols)

        def got(view, sem):
            remote(view, view, ag_s.at[0], ag_r.at[sem], partner).wait_recv()

        right, left, up, down = dev(0, 1), dev(0, -1), dev(1, 0), dev(-1, 0)
        fill = iter(range(MICRO))

        def filler():
            m = next(fill, None)
            if m is not None:
                prepare(m)
                rows = pl.ds(m * (NC * SR // MICRO), NC * SR // MICRO)
                acc[rows, :] = jnp.zeros((NC * SR // MICRO, D), jnp.float32)
            if m == 0:
                gacc[...] = jnp.zeros_like(gacc)

        if first == "z":
            zp = lambda k: k - 1
            zm = lambda k: NZP + k - 1
            base = Z - 1

            def x_out(i, rel):
                put(blk(rel, 0), base + 4 * i, right)
                put(blk(rel, 0), base + 4 * i + 1, left)
                across(blk(rel, 0), i)

            def x_mid(i, rel):
                got(blk(rel, -1), base + 4 * i)
                put(blk(rel, -1, lo), base + 4 * i + 2, right)
                across(blk(rel, -1), i)
                got(blk(rel, 1), base + 4 * i + 1)
                put(blk(rel, 1, hi), base + 4 * i + 3, left)
                across(blk(rel, 1), i)

            def x_end(i, rel):
                got(blk(rel, 2, lo), base + 4 * i + 2)
                got(blk(rel, 2, hi), base + 4 * i + 3)
                across(blk(rel, 2), i)
                flip(i, cols)

            places = [(zp(1), up), (base, right), (base + 1, left)]
            if NZM:
                places.insert(1, (zm(1), down))
            put_own(own_row, places)
            own_copy().wait_recv()
            put_own(other_row, places)
            filler()
            mids, ends, i = [(0, 0)], [], 0
            for k in range(1, NZP + 1):
                fresh = []
                got(blk(-k, 0), zp(k))
                if k < NZP:
                    put(blk(-k, 0), zp(k + 1), up)
                i += 1
                x_out(i, -k)
                fresh.append((i, -k))
                if k <= NZM:
                    got(blk(k, 0), zm(k))
                    if k < NZM:
                        put(blk(k, 0), zm(k + 1), down)
                    i += 1
                    x_out(i, k)
                    fresh.append((i, k))
                for pair in mids:
                    x_mid(*pair)
                for pair in ends:
                    x_end(*pair)
                mids, ends = fresh, mids
                filler()
            for pair in mids:
                x_mid(*pair)
            for pair in ends:
                x_end(*pair)
            for i in range(Z - 3):
                flip_other(i)
            for pair in mids:
                x_end(*pair)
            for i in range(Z - 3, Z):
                flip_other(i)
        else:
            rels = [0, -1, 1, 2]
            hops = [(NZP, NZM), (NZM, NZP), (NZP, NZM), (NZM, NZP)]
            zp = lambda xi, k: 4 + xi * Z + k - 1
            zm = lambda xi, k: 4 + xi * Z + NZP + k - 1

            def z_out(xi):
                put(blk(0, rels[xi]), zp(xi, 1), up)
                put(blk(0, rels[xi]), zm(xi, 1), down)

            places = [(0, right), (1, left), (zp(0, 1), up), (zm(0, 1), down)]
            put_own(own_row, places)
            own_copy().wait_recv()
            put_own(other_row, places)
            filler()
            got(blk(0, -1), 0)
            put(blk(0, -1, lo), 2, right)
            z_out(1)
            across(blk(0, -1), 0)
            got(blk(0, 1), 1)
            put(blk(0, 1, hi), 3, left)
            z_out(2)
            across(blk(0, 1), 0)
            filler()
            got(blk(0, 2, lo), 2)
            got(blk(0, 2, hi), 3)
            z_out(3)
            across(blk(0, 2), 0)
            flip(0, cols)
            flipped = 0
            for k in range(1, NZP + 1):
                for xi in range(4):
                    most_p, most_m = hops[xi]
                    if k <= most_p:
                        got(blk(-k, rels[xi]), zp(xi, k))
                        if k < most_p:
                            put(blk(-k, rels[xi]), zp(xi, k + 1), up)
                        across(blk(-k, rels[xi]), 2 * k - 1)
                    if k <= most_m:
                        got(blk(k, rels[xi]), zm(xi, k))
                        if k < most_m:
                            put(blk(k, rels[xi]), zm(xi, k + 1), down)
                        across(blk(k, rels[xi]), 2 * k if k < NZP else 2 * k - 1)
                flip(2 * k - 1, cols)
                if k < NZP:
                    flip(2 * k, cols)
                if k > 2:
                    flip_other(flipped)
                    flip_other(flipped + 1)
                    flipped += 2
                filler()
            for i in range(flipped, Z):
                flip_other(i)
        for _ in range(MICRO):
            filler()

    own_copy().start()
    cols_a, cols_b = pl.ds(0, CA), pl.ds(CA, D - CA)

    @pl.when(c == 0)
    def _():
        gather("z", cols_a, cols_b, None)

    @pl.when(c == 1)
    def _():
        gather("x", cols_b, cols_a, None)

    def gathered(cols):
        everything = wg.at[pl.ds(0, NC - 1), :, cols]
        remote(everything, everything, ag_s.at[0], ag_r.at[0], partner).wait_send()
        remote(everything, everything, d_s.at[0], d_r.at[0], partner).wait_send()

    @pl.when(s == S - 1)
    def _():
        load_cot().wait()

    def hand_down(m, rows, u):
        return remote(outs.at[m, rows], gs.at[m, rows], y_s.at[0], y_r.at[u], (s - 1, dp))

    def share(m, rows, there):
        return remote(gs.at[m, rows], gs.at[m, there], f_s.at[0], f_r.at[m], partner)

    def save():
        return pltpu.make_async_copy(outs, out_hbm, out_sem.at[0])

    def place(u, base=0):
        return u // H, pl.ds(pl.multiple_of(base + (u % H) * R, R), R)

    def differentiate(m, rows):
        R = rows.size
        g = gs[m, rows, :]
        inv = invs[m, rows, 0:1]
        dots = jnp.zeros((R, 1), jnp.float32)
        for q in range(NQ):
            cols = pl.ds(q * QW, QW)
            branch = lax.dot_general(g, wt[:, cols], NN, preferred_element_type=jnp.float32)
            whitened = xs[m, rows, cols].astype(jnp.float32) * inv
            both = branch * whitened
            gacc[:, cols] += jnp.sum(both.reshape(R // 8, 8, QW), axis=0)
            dots = dots + jnp.sum(both * gain_ref[:, cols], axis=-1, keepdims=True)
            gained[pl.ds(0, R), cols] = branch * gain_ref[:, cols]
        mean = dots / D
        for q in range(NQ):
            cols = pl.ds(q * QW, QW)
            whitened = xs[m, rows, cols].astype(jnp.float32) * inv
            fresh = gs[m, rows, cols].astype(jnp.float32) + inv * (gained[pl.ds(0, R), cols] - whitened * mean)
            outs[m, rows, cols] = fresh.astype(jnp.bfloat16)

    quarter = NC * SR // H

    def weigh(m, r):
        rows = pl.ds(pl.multiple_of(r * quarter, quarter), quarter)
        n = quarter // SR
        lhs = lt[m, pl.ds(r * n, n)].reshape(quarter, 2 * TR)
        acc[rows, :] += lax.dot_general(lhs, gs[m], NN, preferred_element_type=jnp.float32)

    def meet(m):
        nt_local(m).wait()
        nt_send(m).wait_recv()
        share(m, pl.ds(0, TR), pl.ds(TR, TR)).wait_recv()

    lag = jnp.where(s == 0, 1, 0)

    def tick(u, carry):
        m, rows = place(u)

        @pl.when(s < S - 1)
        def _():
            hand_down(m, rows, u).wait_recv()

        share(m, rows, place(u, TR)[1]).start()

        @pl.when(u > lag)
        def _():
            differentiate(*place(u - lag))

        @pl.when(s > 0)
        def _():
            hand_down(m, rows, u).start()

        @pl.when(u >= H)
        def _():
            @pl.when(u % H == 0)
            def _():
                meet(m - 1)

            weigh(m - 1, u % H)

        return carry

    for k in range(2):
        rows, there = pl.ds(k * (R // 2), R // 2), pl.ds(TR + k * (R // 2), R // 2)
        sem = U if k else 0

        @pl.when(s < S - 1)
        def _():
            hand_down(0, rows, sem).wait_recv()

        share(0, rows, there).start()
        differentiate(0, rows)

        @pl.when(s > 0)
        def _():
            hand_down(0, rows, sem).start()

    lax.fori_loop(1, U, tick, 0)
    meet(MICRO - 1)

    far_part = (((z + NZP) % Z) * H) // Z

    def final(k):
        weigh(MICRO - 1, (far_part + k + H) % H)

    def spread(src, dst, place, targets, ss, rs, sem0):
        return [remote(src, dst.at[place], ss.at[sem0 + k], rs.at[sem0 + k], t) for k, t in enumerate(targets)]

    def added(dst):
        total = dst[0]
        for k in range(1, dst.shape[0]):
            total = total + dst[k]
        return total

    near, far = peers[: 2 * X - 1], peers[2 * X - 1 :]

    def gain_near():
        return spread(gv.at[0], g1, x * 2 + c, near, g_s, g_r, 0)

    def gain_far():
        return spread(gv.at[1], g2, z, far, g_s, g_r, 2 * X - 1)

    def hook_a():
        @pl.when(s == 0)
        def _():
            differentiate(*place(U - 1))

        save().start()
        gv[0] = jnp.sum(gacc[...], axis=0, keepdims=True)
        for copy in gain_near():
            copy.start()
        g1[x * 2 + c] = gv[0]

    def hook_b():
        for copy in gain_near():
            copy.wait_recv()
        gv[1] = added(g1)
        for copy in gain_far():
            copy.start()
        g2[z] = gv[1]

    def mine(dz, dx):
        return acc[pl.ds(pl.multiple_of(chip(dz, dx) * SR, SR), SR), :]

    def reduce(first):
        right, left, up, down = dev(0, 1), dev(0, -1), dev(1, 0), dev(-1, 0)
        lo, hi, full = pl.ds(0, HS), pl.ds(HS, HS), pl.ds(0, SR)

        def put(i, slot, sem, device, rows=full):
            remote(sbuf.at[i, rows], rbuf.at[slot, rows], rs_s.at[0], rs_r.at[sem], device).start()

        def got(slot, sem, rows=full):
            view = rbuf.at[slot, rows]
            remote(view, view, rs_s.at[0], rs_r.at[sem], partner).wait_recv()

        def taken(slot, rows=full):
            return rbuf[slot, rows, :].astype(jnp.float32)

        if first == "x":
            rels = []
            for k in range(NZP, 0, -1):
                rels.append(k)
                if k > 1:
                    rels.append(-(k - 1))
            rels.append(0)
            zslot, zsem = 3 * Z, 4 * Z

            def one(i):
                sbuf[3 * i] = mine(rels[i], 2).astype(jnp.bfloat16)
                put(3 * i, 3 * i, 4 * i, right, lo)
                put(3 * i, 3 * i, 4 * i + 1, left, hi)

            def two(i):
                got(3 * i, 4 * i, lo)
                value = mine(rels[i], 1)
                sbuf[3 * i + 1, lo, :] = (value[:HS] + taken(3 * i, lo)).astype(jnp.bfloat16)
                sbuf[3 * i + 1, hi, :] = value[HS:].astype(jnp.bfloat16)
                put(3 * i + 1, 3 * i + 1, 4 * i + 2, right)
                got(3 * i, 4 * i + 1, hi)
                value = mine(rels[i], -1)
                sbuf[3 * i + 2, lo, :] = value[:HS].astype(jnp.bfloat16)
                sbuf[3 * i + 2, hi, :] = (value[HS:] + taken(3 * i, hi)).astype(jnp.bfloat16)
                put(3 * i + 2, 3 * i + 2, 4 * i + 3, left)

            def three(i):
                rel = rels[i]
                got(3 * i + 1, 4 * i + 2)
                got(3 * i + 2, 4 * i + 3)
                value = mine(rel, 0) + taken(3 * i + 1) + taken(3 * i + 2)
                if rel > 0:
                    slot = zslot + rel - 1
                    if rel < NZP:
                        got(slot + 1, zsem + rel)
                        value = value + taken(slot + 1)
                    sbuf[slot] = value.astype(jnp.bfloat16)
                    put(slot, slot, zsem + rel - 1, up)
                elif rel < 0:
                    slot = zslot + NZP - rel - 1
                    if -rel < NZM:
                        got(slot + 1, zsem + NZP - rel)
                        value = value + taken(slot + 1)
                    sbuf[slot] = value.astype(jnp.bfloat16)
                    put(slot, slot, zsem + NZP - rel - 1, down)
                else:
                    got(zslot, zsem)
                    value = value + taken(zslot)
                    if NZM:
                        got(zslot + NZP, zsem + NZP)
                        value = value + taken(zslot + NZP)
                    wgf[...] = value

            final(0)
            final(1)
            for i in range(Z + 4):
                if i < Z:
                    one(i)
                if i == 1:
                    final(-1)
                    final(2)
                if 0 <= i - 2 < Z:
                    two(i - 2)
                if 0 <= i - 4 < Z:
                    three(i - 4)
                if i == 2:
                    hook_a()
                if i == Z:
                    hook_b()
        else:
            rels = [2, 1, -1, 0]
            hops = [(NZP, NZM), (NZM, NZP), (NZP, NZM), (NZM, NZP)]
            zs = lambda xi, j: xi * (Z - 1) + j - 1
            xslot = 4 * (Z - 1)

            def link(xi, j, most, base, sign, device):
                value = mine(sign * j, rels[xi])
                slot = base + j - 1
                if j < most:
                    got(slot + 1, slot + 1)
                    value = value + taken(slot + 1)
                sbuf[slot] = value.astype(jnp.bfloat16)
                put(slot, slot, slot, device)

            def total(xi):
                most_p, most_m = hops[xi]
                base = xi * (Z - 1)
                value = mine(0, rels[xi])
                if most_p:
                    got(base, base)
                    value = value + taken(base)
                if most_m:
                    got(base + most_p, base + most_p)
                    value = value + taken(base + most_p)
                return value

            for k in (0, 1, -1):
                final(k)
            for t in range(NZP):
                if t == 1:
                    final(2)
                for xi in range(4):
                    most_p, most_m = hops[xi]
                    base = xi * (Z - 1)
                    if most_p - t >= 1:
                        link(xi, most_p - t, most_p, base, 1, up)
                    if most_m - t >= 1:
                        link(xi, most_m - t, most_m, base + most_p, -1, down)
                if t == 0:
                    hook_a()
                if t == NZP - 1:
                    hook_b()
            sbuf[xslot] = total(0).astype(jnp.bfloat16)
            put(xslot, xslot, xslot, right, lo)
            put(xslot, xslot, xslot + 1, left, hi)
            ahead, behind = total(1), total(2)
            sbuf[xslot + 1, hi, :] = ahead[HS:].astype(jnp.bfloat16)
            sbuf[xslot + 2, lo, :] = behind[:HS].astype(jnp.bfloat16)
            got(xslot, xslot, lo)
            sbuf[xslot + 1, lo, :] = (ahead[:HS] + taken(xslot, lo)).astype(jnp.bfloat16)
            put(xslot + 1, xslot + 1, xslot + 2, right)
            got(xslot, xslot + 1, hi)
            sbuf[xslot + 2, hi, :] = (behind[HS:] + taken(xslot, hi)).astype(jnp.bfloat16)
            put(xslot + 2, xslot + 2, xslot + 3, left)
            value = total(3)
            got(xslot + 1, xslot + 2)
            got(xslot + 2, xslot + 3)
            wgf[...] = value + taken(xslot + 1) + taken(xslot + 2)
        remote(sbuf, rbuf, rs_s.at[0], rs_r.at[0], partner).wait_send()

    @pl.when(c == 0)
    def _():
        reduce("x")

    @pl.when(c == 1)
    def _():
        reduce("z")

    grad = wgf[...]
    row_sum = jnp.sum(grad * grad + SQUARE_EPS, axis=-1, keepdims=True)
    eye = lax.broadcasted_iota(jnp.int32, (SR, SR), 0) == lax.broadcasted_iota(jnp.int32, (SR, SR), 1)
    row_old = jnp.sum(jnp.where(eye, jnp.broadcast_to(row_ref[...], (SR, SR)), 0.0), axis=-1, keepdims=True)
    row_new = DECAY_RATE * row_old + (1.0 - DECAY_RATE) * (row_sum / D)
    rown_ref[...] = jnp.sum(jnp.where(eye, jnp.broadcast_to(row_new, (SR, SR)), 0.0), axis=0, keepdims=True)
    per_row = 1.0 / row_new
    E = 2 * X
    SL = D // E
    e = x * 2 + c
    col_sum = jnp.sum(grad * grad + SQUARE_EPS, axis=0, keepdims=True)
    col_part = jnp.sum(grad * grad * per_row, axis=0, keepdims=True)
    row_total = jnp.broadcast_to(jnp.sum(row_new, axis=0, keepdims=True), (1, 128))
    for k in range(E):
        cols = slice(k * SL, (k + 1) * SL)
        tv[k, :, pl.ds(0, SL)] = col_sum[:, cols]
        tv[k, :, pl.ds(SL, SL)] = col_part[:, cols]
        tv[k, :, pl.ds(2 * SL, 128)] = row_total

    def slice_of(k):
        return ((x + k // 2) % X) * 2 + (c + k) % 2

    first = [
        remote(tv.at[slice_of(k)], t1.at[e], t_s.at[k - 1], t_r.at[k - 1], p)
        for k, p in enumerate(near, start=1)
    ]
    second = spread(tu, t2, z, far, t_s, t_r, E - 1)
    third = spread(tw, t3, e, near, t_s, t_r, E + Z - 2)

    def exchange(copies, dst, place, value):
        for copy in copies:
            copy.start()
        dst[place] = value
        for copy in copies:
            copy.wait_recv()
        return added(dst)

    tu[...] = exchange(first, t1, e, tv[e])
    sums = exchange(second, t2, z, tu[...])
    col_old = col_ref[:, pl.ds(pl.multiple_of(e * SL, SL), SL)]
    fresh_cols = DECAY_RATE * col_old + (1.0 - DECAY_RATE) * sums[:, 0:SL] / D
    tw[:, pl.ds(0, SL)] = fresh_cols
    share_sum = jnp.sum(sums[:, SL : 2 * SL] / fresh_cols, axis=-1, keepdims=True)
    tw[:, pl.ds(SL, 128)] = jnp.broadcast_to(share_sum, (1, 128))
    shares = exchange(third, t3, e, tw[...])
    for k in range(E):
        coln_ref[:, pl.ds(k * SL, SL)] = t3[k, :, pl.ds(0, SL)]
    col_new = coln_ref[...]
    row_mean = sums[:, 2 * SL : 2 * SL + 1] / D
    total_square = row_mean * shares[:, SL : SL + 1]
    clip = jnp.maximum(1.0, jnp.sqrt(total_square / (D * D)))
    step_ref[...] = grad / jnp.sqrt(row_new * col_new / row_mean) / clip
    for copy in gain_far():
        copy.wait_recv()
    gg_ref[...] = added(g2)

    own_copy().wait_send()

    @pl.when(c == 0)
    def _():
        gathered(cols_a)

    @pl.when(c == 1)
    def _():
        gathered(cols_b)

    for copy in first + second + third + gain_near() + gain_far():
        copy.wait_send()
    save().wait()
    for m in range(MICRO):
        nt_send(m).wait_send()
    shared = gs.at[:, pl.ds(0, TR)]
    remote(shared, shared, f_s.at[0], f_r.at[0], partner).wait_send()

    @pl.when(s > 0)
    def _():
        remote(outs, outs, y_s.at[0], y_r.at[0], partner).wait_send()


def deliver(*refs):
    n = 5
    sources, results, held, sems = refs[:n], refs[n : 2 * n], refs[2 * n : 3 * n], refs[-1]
    ways = []
    for src, mid, dst in zip(sources, held, results):
        pieces = src.shape[0] if len(src.shape) == 3 else 1
        for k in range(pieces):
            a, m, b = (src.at[k], mid.at[k], dst.at[k]) if pieces > 1 else (src, mid, dst)
            i = len(ways)
            ways.append(
                (
                    pltpu.make_async_copy(a, m, sems.at[0, i]),
                    pltpu.make_async_copy(m, b, sems.at[1, i]),
                )
            )
    for into, _ in ways:
        into.start()
    for into, out in ways:
        into.wait()
        out.start()
    for _, out in ways:
        out.wait()


def body(saved_inputs, out_cotangent, weights, gains, row_state, col_state):
    S, DP = lax.axis_size("section"), lax.axis_size("dp")
    Z = DP // (2 * X)
    _, MICRO, TR, D = saved_inputs.shape
    SR = weights.shape[1]
    NC = DP // 2
    R = TR // 4
    CA = D * 9 // 16
    U = MICRO * (TR // R)
    SL = D // (2 * X)
    bf, f32 = jnp.bfloat16, jnp.float32
    dma = pltpu.SemaphoreType.DMA
    vmem = pl.BlockSpec(memory_space=pltpu.VMEM)
    hbm = pl.BlockSpec(memory_space=pl.ANY)
    V = pltpu.VMEM
    scratch = [
        V((MICRO, TR, D), bf),
        V((MICRO, 2 * TR, D), bf),
        V((MICRO, TR, D), bf),
        V((NC, 2 * SR, D), bf),
        V((D, D), bf),
        V((MICRO, NC, 2, SR, TR), bf),
        V((MICRO, NC, SR, 2 * TR), bf),
        V((NC * SR, D), f32),
        V((R, D), f32),
        V((MICRO, TR, 128), f32),
        V((8, D), f32),
        V((SR, D), f32),
        V((NC - 1, SR, D), bf),
        V((NC - 1, SR, D), bf),
        V((2 * X, 1, 2 * SL + 128), f32),
        V((2 * X, 1, 2 * SL + 128), f32),
        V((1, 2 * SL + 128), f32),
        V((Z, 1, 2 * SL + 128), f32),
        V((1, SL + 128), f32),
        V((2 * X, 1, SL + 128), f32),
        V((2, 1, D), f32),
        V((2 * X, 1, D), f32),
        V((Z, 1, D), f32),
        dma((2,)),
        dma((MICRO,)),
        dma((1,)),
        dma((1,)),
        dma((5 * Z,)),
        dma((1,)),
        dma((Z,)),
        dma((1,)),
        dma((1,)),
        dma((MICRO,)),
        dma((MICRO,)),
        dma((1,)),
        dma((U + 1,)),
        dma((1,)),
        dma((MICRO,)),
        dma((1,)),
        dma((5 * Z,)),
        dma((4 * X + Z,)),
        dma((4 * X + Z,)),
        dma((2 * X + Z,)),
        dma((2 * X + Z,)),
    ]
    outs = pl.pallas_call(
        functools.partial(kernel, S, Z, R, CA),
        out_shape=(
            jax.ShapeDtypeStruct((MICRO, TR, D), bf),
            jax.ShapeDtypeStruct((SR, D), f32),
            jax.ShapeDtypeStruct((1, SR), f32),
            jax.ShapeDtypeStruct((1, D), f32),
            jax.ShapeDtypeStruct((1, D), f32),
        ),
        in_specs=[hbm, hbm, vmem, vmem, vmem, vmem],
        out_specs=(hbm, vmem, vmem, vmem, vmem),
        scratch_shapes=scratch,
        compiler_params=pltpu.CompilerParams(
            collective_id=0, has_side_effects=True, vmem_limit_bytes=60 * 2**20
        ),
        name="relay_back",
    )(saved_inputs[0], out_cotangent, weights[0], gains, row_state, col_state)
    outs = pl.pallas_call(
        deliver,
        out_shape=tuple(jax.ShapeDtypeStruct(o.shape, o.dtype) for o in outs),
        in_specs=[hbm] * 5,
        out_specs=(hbm,) * 5,
        scratch_shapes=[V(o.shape, o.dtype) for o in outs] + [dma((2, MICRO + 4))],
        name="deliver",
    )(*outs)
    return (outs[0][None], outs[1][None], outs[2], outs[3], outs[4])


def solution(mesh):
    placed = (
        P("section", None, "dp", None),
        P(None, "dp", None),
        P("section", "dp", None),
        P("section", None),
        P("section", "dp"),
        P("section", None),
    )
    return jax.shard_map(
        body,
        mesh=mesh,
        in_specs=placed,
        out_specs=(
            P("section", None, "dp", None),
            P("section", "dp", None),
            P("section", "dp"),
            P("section", None),
            P("section", None),
        ),
        check_vma=False,
    )
```

```python
import functools

import jax
import jax.numpy as jnp
from jax import lax
from jax.experimental import pallas as pl
from jax.experimental.pallas import tpu as pltpu
from jax.sharding import PartitionSpec as P

DECAY_RATE = 0.9
SQUARE_EPS = 1e-30
NORM_EPS = 1e-06
X = 4
MESH = pl.DeviceIdType.MESH
NT = (((1,), (1,)), ((), ()))
NN = (((1,), (0,)), ((), ()))


def kernel(
    S, Z, R, CA,
    x_hbm, cot_hbm, w_ref, gain_ref, row_ref, col_ref,
    out_hbm, step_ref, rown_ref, coln_ref, gg_ref,
    xs, gs, outs, wg, wt, nt, lt, acc, gained, invs, gacc, wgf, pre, rbuf, sbuf, tv, t1, tu, t2, tw, t3, gv, g1, g2,
    in_sem, lsem, out_sem, ag_s, ag_r, d_s, d_r, own_s, own_r, l_s, l_r,
    y_s, y_r, f_s, f_r, rs_s, rs_r, t_s, t_r, g_s, g_r,
):
    MICRO, TR, D = xs.shape
    SR = w_ref.shape[0]
    NC = Z * X
    H = TR // R
    U = MICRO * H
    NZP, NZM = Z // 2, Z // 2 - 1
    HB, HS = SR, SR // 2
    QW = min(256, D)
    NQ = D // QW
    s = lax.axis_index("section")
    dp = lax.axis_index("dp")
    z, x, c = dp // (2 * X), (dp // 2) % X, dp % 2

    def chip(dz, dx):
        return ((z + dz + Z) % Z) * X + (x + dx + X) % X

    def dev(dz, dx, flip=0):
        return (s, chip(dz, dx) * 2 + (c + flip) % 2)

    partner = dev(0, 0, 1)

    def remote(src, dst, ss, rs, device):
        return pltpu.make_async_remote_copy(
            src_ref=src, dst_ref=dst, send_sem=ss, recv_sem=rs, device_id=device, device_id_type=MESH
        )

    def load_x():
        return pltpu.make_async_copy(x_hbm, xs, in_sem.at[0])

    def load_cot():
        return pltpu.make_async_copy(cot_hbm, gs.at[:, pl.ds(0, TR)], in_sem.at[1])

    load_x().start()

    @pl.when(s == S - 1)
    def _():
        load_cot().start()

    own_row = pl.multiple_of(c * SR, SR)
    other_row = pl.multiple_of((1 - c) * SR, SR)
    wg[chip(0, 0), pl.ds(own_row, SR), :] = w_ref[...]

    barrier = pltpu.get_barrier_semaphore()
    peers = [dev(0, k // 2, k % 2) for k in range(1, 2 * X)] + [dev(k, 0) for k in range(1, Z)]
    for p in peers:
        pl.semaphore_signal(barrier, inc=1, device_id=p, device_id_type=MESH)

    for ds in (1, S - 1):
        pl.semaphore_signal(barrier, inc=1, device_id=((s + ds) % S, dp), device_id_type=MESH)
    pl.semaphore_wait(barrier, len(peers) + 2)

    def nt_send(m):
        return remote(nt.at[m, :, 1 - c], lt.at[m, :, :, pl.ds(TR, TR)], l_s.at[m], l_r.at[m], partner)

    def nt_local(m):
        return pltpu.make_async_copy(nt.at[m, :, c], lt.at[m, :, :, pl.ds(0, TR)], lsem.at[m])

    def prepare(m):
        if m == 0:
            load_x().wait()
        total = jnp.zeros((TR, 1), jnp.float32)
        for q in range(NQ):
            part = xs[m, :, pl.ds(q * QW, QW)].astype(jnp.float32)
            total = total + jnp.sum(part * part, axis=-1, keepdims=True)
        inv = lax.rsqrt(total / D + NORM_EPS)
        invs[m] = jnp.broadcast_to(inv, invs.shape[1:])
        for q in range(NQ):
            cols = pl.ds(q * QW, QW)
            whitened = xs[m, :, cols].astype(jnp.float32) * inv
            normed = whitened * gain_ref[:, cols]
            n = QW // (2 * SR)
            nt[m, pl.ds(q * n, n)] = normed.T.astype(jnp.bfloat16).reshape(n, 2, SR, TR)
        nt_local(m).start()
        nt_send(m).start()

    def own_copy():
        rows = wg.at[chip(0, 0), pl.ds(own_row, SR)]
        return remote(rows, rows, own_s.at[0], own_r.at[0], partner)

    def gather(first, cols, other_cols, order):
        def blk(dz, dx, rows=pl.ds(0, 2 * SR)):
            return wg.at[chip(dz, dx), rows, cols]

        lo, hi = pl.ds(0, HB), pl.ds(HB, HB)

        def put(view, sem, device):
            remote(view, view, ag_s.at[0], ag_r.at[sem], device).start()

        def across(view, i):
            remote(view, view, d_s.at[0], d_r.at[i], partner).start()

        def put_own(base_rows, places):
            for sem, device in places:
                put(blk(0, 0, pl.ds(base_rows, SR)), sem, device)

        def group(i):
            return 0 if i == 0 else (-(i + 1) // 2 if i % 2 else i // 2)

        def flip(i, part):
            first_chip = ((z + group(i) + Z) % Z) * X
            block = wg[pl.ds(first_chip, X), :, part].reshape(X * 2 * SR, part.size)
            width = X * 2 * SR
            wt[part, pl.ds(pl.multiple_of(first_chip * 2 * SR, width), width)] = block.T

        def flip_other(i):
            n = X if i else X - 1
            whole = wg.at[pl.ds(0, n), :, other_cols]
            remote(whole, whole, d_s.at[0], d_r.at[i], partner).wait_recv()
            flip(i, other_cols)

            @pl.when(s == S - 1)
            def _():
                width = X * 2 * SR
                ready = pl.ds(pl.multiple_of(((z + group(i) + Z) % Z) * width, width), width)
                pre[:, ready] = lax.dot_general(
                    gs[0, pl.ds(0, TR), :], wt[:, ready], NN, preferred_element_type=jnp.float32
                )

        def got(view, sem):
            remote(view, view, ag_s.at[0], ag_r.at[sem], partner).wait_recv()

        right, left, up, down = dev(0, 1), dev(0, -1), dev(1, 0), dev(-1, 0)
        fill = iter(range(MICRO))

        def filler():
            m = next(fill, None)
            if m is not None:
                prepare(m)
                rows = pl.ds(m * (NC * SR // MICRO), NC * SR // MICRO)
                acc[rows, :] = jnp.zeros((NC * SR // MICRO, D), jnp.float32)
            if m == 0:
                gacc[...] = jnp.zeros_like(gacc)

        if first == "z":
            zp = lambda k: k - 1
            zm = lambda k: NZP + k - 1
            base = Z - 1

            def x_out(i, rel):
                put(blk(rel, 0), base + 4 * i, right)
                put(blk(rel, 0), base + 4 * i + 1, left)
                across(blk(rel, 0), i)

            def x_mid(i, rel):
                got(blk(rel, -1), base + 4 * i)
                put(blk(rel, -1, lo), base + 4 * i + 2, right)
                across(blk(rel, -1), i)
                got(blk(rel, 1), base + 4 * i + 1)
                put(blk(rel, 1, hi), base + 4 * i + 3, left)
                across(blk(rel, 1), i)

            def x_end(i, rel):
                got(blk(rel, 2, lo), base + 4 * i + 2)
                got(blk(rel, 2, hi), base + 4 * i + 3)
                across(blk(rel, 2), i)
                flip(i, cols)

            places = [(zp(1), up), (base, right), (base + 1, left)]
            if NZM:
                places.insert(1, (zm(1), down))
            put_own(own_row, places)
            own_copy().wait_recv()
            put_own(other_row, places)
            filler()
            mids, ends, i = [(0, 0)], [], 0
            for k in range(1, NZP + 1):
                fresh = []
                got(blk(-k, 0), zp(k))
                if k < NZP:
                    put(blk(-k, 0), zp(k + 1), up)
                i += 1
                x_out(i, -k)
                fresh.append((i, -k))
                if k <= NZM:
                    got(blk(k, 0), zm(k))
                    if k < NZM:
                        put(blk(k, 0), zm(k + 1), down)
                    i += 1
                    x_out(i, k)
                    fresh.append((i, k))
                for pair in mids:
                    x_mid(*pair)
                for pair in ends:
                    x_end(*pair)
                mids, ends = fresh, mids
                filler()
            for pair in mids:
                x_mid(*pair)
            for pair in ends:
                x_end(*pair)
            for i in range(Z - 3):
                flip_other(i)
            for pair in mids:
                x_end(*pair)
            for i in range(Z - 3, Z):
                flip_other(i)
        else:
            rels = [0, -1, 1, 2]
            hops = [(NZP, NZM), (NZM, NZP), (NZP, NZM), (NZM, NZP)]
            zp = lambda xi, k: 4 + xi * Z + k - 1
            zm = lambda xi, k: 4 + xi * Z + NZP + k - 1

            def z_out(xi):
                put(blk(0, rels[xi]), zp(xi, 1), up)
                put(blk(0, rels[xi]), zm(xi, 1), down)

            places = [(0, right), (1, left), (zp(0, 1), up), (zm(0, 1), down)]
            put_own(own_row, places)
            own_copy().wait_recv()
            put_own(other_row, places)
            filler()
            got(blk(0, -1), 0)
            put(blk(0, -1, lo), 2, right)
            z_out(1)
            across(blk(0, -1), 0)
            got(blk(0, 1), 1)
            put(blk(0, 1, hi), 3, left)
            z_out(2)
            across(blk(0, 1), 0)
            filler()
            got(blk(0, 2, lo), 2)
            got(blk(0, 2, hi), 3)
            z_out(3)
            across(blk(0, 2), 0)
            flip(0, cols)
            flipped = 0
            for k in range(1, NZP + 1):
                for xi in range(4):
                    most_p, most_m = hops[xi]
                    if k <= most_p:
                        got(blk(-k, rels[xi]), zp(xi, k))
                        if k < most_p:
                            put(blk(-k, rels[xi]), zp(xi, k + 1), up)
                        across(blk(-k, rels[xi]), 2 * k - 1)
                    if k <= most_m:
                        got(blk(k, rels[xi]), zm(xi, k))
                        if k < most_m:
                            put(blk(k, rels[xi]), zm(xi, k + 1), down)
                        across(blk(k, rels[xi]), 2 * k if k < NZP else 2 * k - 1)
                flip(2 * k - 1, cols)
                if k < NZP:
                    flip(2 * k, cols)
                if k > 2:
                    flip_other(flipped)
                    flip_other(flipped + 1)
                    flipped += 2
                filler()
            for i in range(flipped, Z):
                flip_other(i)
        for _ in range(MICRO):
            filler()

    own_copy().start()

    @pl.when(s == S - 1)
    def _():
        load_cot().wait()

    cols_a, cols_b = pl.ds(0, CA), pl.ds(CA, D - CA)

    @pl.when(c == 0)
    def _():
        gather("z", cols_a, cols_b, None)

    @pl.when(c == 1)
    def _():
        gather("x", cols_b, cols_a, None)

    def gathered(cols):
        everything = wg.at[pl.ds(0, NC - 1), :, cols]
        remote(everything, everything, ag_s.at[0], ag_r.at[0], partner).wait_send()
        remote(everything, everything, d_s.at[0], d_r.at[0], partner).wait_send()

    def hand_down(m, rows, u):
        return remote(outs.at[m, rows], gs.at[m, rows], y_s.at[0], y_r.at[u], (s - 1, dp))

    def share(m, rows, there):
        return remote(gs.at[m, rows], gs.at[m, there], f_s.at[0], f_r.at[m], partner)

    def save():
        return pltpu.make_async_copy(outs, out_hbm, out_sem.at[0])

    def place(u, base=0):
        return u // H, pl.ds(pl.multiple_of(base + (u % H) * R, R), R)

    def differentiate(m, rows, ready=False):
        R = rows.size
        g = gs[m, rows, :]
        inv = invs[m, rows, 0:1]
        dots = jnp.zeros((R, 1), jnp.float32)
        for q in range(NQ):
            cols = pl.ds(q * QW, QW)
            if ready:
                branch = pre[rows, cols]
            else:
                branch = lax.dot_general(g, wt[:, cols], NN, preferred_element_type=jnp.float32)
            whitened = xs[m, rows, cols].astype(jnp.float32) * inv
            both = branch * whitened
            gacc[:, cols] += jnp.sum(both.reshape(R // 8, 8, QW), axis=0)
            dots = dots + jnp.sum(both * gain_ref[:, cols], axis=-1, keepdims=True)
            gained[pl.ds(0, R), cols] = branch * gain_ref[:, cols]
        mean = dots / D
        for q in range(NQ):
            cols = pl.ds(q * QW, QW)
            whitened = xs[m, rows, cols].astype(jnp.float32) * inv
            fresh = gs[m, rows, cols].astype(jnp.float32) + inv * (gained[pl.ds(0, R), cols] - whitened * mean)
            outs[m, rows, cols] = fresh.astype(jnp.bfloat16)

    quarter = NC * SR // H

    def weigh(m, r):
        rows = pl.ds(pl.multiple_of(r * quarter, quarter), quarter)
        n = quarter // SR
        lhs = lt[m, pl.ds(r * n, n)].reshape(quarter, 2 * TR)
        acc[rows, :] += lax.dot_general(lhs, gs[m], NN, preferred_element_type=jnp.float32)

    def meet(m):
        nt_local(m).wait()
        nt_send(m).wait_recv()
        share(m, pl.ds(0, TR), pl.ds(TR, TR)).wait_recv()

    lag = jnp.where(s == 0, 1, 0)

    def tick(u, carry):
        m, rows = place(u)

        @pl.when(s < S - 1)
        def _():
            hand_down(m, rows, u).wait_recv()

        early = jnp.logical_and(s == S - 1, u < H)

        @pl.when(jnp.logical_and(u > lag, jnp.logical_not(early)))
        def _():
            differentiate(*place(u - lag))

        @pl.when(early)
        def _():
            differentiate(m, rows, True)

        @pl.when(s > 0)
        def _():
            hand_down(m, rows, u).start()

        share(m, rows, place(u, TR)[1]).start()

        @pl.when(u >= H)
        def _():
            @pl.when(u % H == 0)
            def _():
                meet(m - 1)

            weigh(m - 1, u % H)

        return carry

    for k in range(2):
        rows, there = pl.ds(k * (R // 2), R // 2), pl.ds(TR + k * (R // 2), R // 2)
        sem = U if k else 0

        @pl.when(s < S - 1)
        def _():
            hand_down(0, rows, sem).wait_recv()
            differentiate(0, rows)

        @pl.when(s == S - 1)
        def _():
            differentiate(0, rows, True)

        @pl.when(s > 0)
        def _():
            hand_down(0, rows, sem).start()

        share(0, rows, there).start()

    lax.fori_loop(1, U, tick, 0)
    meet(MICRO - 1)

    far_part = (((z + NZP) % Z) * H) // Z

    def final(k):
        weigh(MICRO - 1, (far_part + k + H) % H)

    def spread(src, dst, place, targets, ss, rs, sem0):
        return [remote(src, dst.at[place], ss.at[sem0 + k], rs.at[sem0 + k], t) for k, t in enumerate(targets)]

    def added(dst):
        total = dst[0]
        for k in range(1, dst.shape[0]):
            total = total + dst[k]
        return total

    near, far = peers[: 2 * X - 1], peers[2 * X - 1 :]

    def gain_near():
        return spread(gv.at[0], g1, x * 2 + c, near, g_s, g_r, 0)

    def gain_far():
        return spread(gv.at[1], g2, z, far, g_s, g_r, 2 * X - 1)

    def hook_a():
        @pl.when(s == 0)
        def _():
            differentiate(*place(U - 1))

        save().start()
        gv[0] = jnp.sum(gacc[...], axis=0, keepdims=True)
        for copy in gain_near():
            copy.start()
        g1[x * 2 + c] = gv[0]

    def hook_b():
        for copy in gain_near():
            copy.wait_recv()
        gv[1] = added(g1)
        for copy in gain_far():
            copy.start()
        g2[z] = gv[1]

    def mine(dz, dx):
        return acc[pl.ds(pl.multiple_of(chip(dz, dx) * SR, SR), SR), :]

    def reduce(first):
        right, left, up, down = dev(0, 1), dev(0, -1), dev(1, 0), dev(-1, 0)
        lo, hi, full = pl.ds(0, HS), pl.ds(HS, HS), pl.ds(0, SR)

        def put(i, slot, sem, device, rows=full):
            remote(sbuf.at[i, rows], rbuf.at[slot, rows], rs_s.at[0], rs_r.at[sem], device).start()

        def got(slot, sem, rows=full):
            view = rbuf.at[slot, rows]
            remote(view, view, rs_s.at[0], rs_r.at[sem], partner).wait_recv()

        def taken(slot, rows=full):
            return rbuf[slot, rows, :].astype(jnp.float32)

        if first == "x":
            rels = []
            for k in range(NZP, 0, -1):
                rels.append(k)
                if k > 1:
                    rels.append(-(k - 1))
            rels.append(0)
            zslot, zsem = 3 * Z, 4 * Z

            def one(i):
                sbuf[3 * i] = mine(rels[i], 2).astype(jnp.bfloat16)
                put(3 * i, 3 * i, 4 * i, right, lo)
                put(3 * i, 3 * i, 4 * i + 1, left, hi)

            def two(i):
                got(3 * i, 4 * i, lo)
                value = mine(rels[i], 1)
                sbuf[3 * i + 1, lo, :] = (value[:HS] + taken(3 * i, lo)).astype(jnp.bfloat16)
                sbuf[3 * i + 1, hi, :] = value[HS:].astype(jnp.bfloat16)
                put(3 * i + 1, 3 * i + 1, 4 * i + 2, right)
                got(3 * i, 4 * i + 1, hi)
                value = mine(rels[i], -1)
                sbuf[3 * i + 2, lo, :] = value[:HS].astype(jnp.bfloat16)
                sbuf[3 * i + 2, hi, :] = (value[HS:] + taken(3 * i, hi)).astype(jnp.bfloat16)
                put(3 * i + 2, 3 * i + 2, 4 * i + 3, left)

            def three(i):
                rel = rels[i]
                got(3 * i + 1, 4 * i + 2)
                got(3 * i + 2, 4 * i + 3)
                value = mine(rel, 0) + taken(3 * i + 1) + taken(3 * i + 2)
                if rel > 0:
                    slot = zslot + rel - 1
                    if rel < NZP:
                        got(slot + 1, zsem + rel)
                        value = value + taken(slot + 1)
                    sbuf[slot] = value.astype(jnp.bfloat16)
                    put(slot, slot, zsem + rel - 1, up)
                elif rel < 0:
                    slot = zslot + NZP - rel - 1
                    if -rel < NZM:
                        got(slot + 1, zsem + NZP - rel)
                        value = value + taken(slot + 1)
                    sbuf[slot] = value.astype(jnp.bfloat16)
                    put(slot, slot, zsem + NZP - rel - 1, down)
                else:
                    got(zslot, zsem)
                    value = value + taken(zslot)
                    if NZM:
                        got(zslot + NZP, zsem + NZP)
                        value = value + taken(zslot + NZP)
                    wgf[...] = value

            final(0)
            final(1)
            for i in range(Z + 4):
                if i < Z:
                    one(i)
                if i == 1:
                    final(-1)
                    final(2)
                if 0 <= i - 2 < Z:
                    two(i - 2)
                if 0 <= i - 4 < Z:
                    three(i - 4)
                if i == 2:
                    hook_a()
                if i == Z:
                    hook_b()
        else:
            rels = [2, 1, -1, 0]
            hops = [(NZP, NZM), (NZM, NZP), (NZP, NZM), (NZM, NZP)]
            zs = lambda xi, j: xi * (Z - 1) + j - 1
            xslot = 4 * (Z - 1)

            def link(xi, j, most, base, sign, device):
                value = mine(sign * j, rels[xi])
                slot = base + j - 1
                if j < most:
                    got(slot + 1, slot + 1)
                    value = value + taken(slot + 1)
                sbuf[slot] = value.astype(jnp.bfloat16)
                put(slot, slot, slot, device)

            def total(xi):
                most_p, most_m = hops[xi]
                base = xi * (Z - 1)
                value = mine(0, rels[xi])
                if most_p:
                    got(base, base)
                    value = value + taken(base)
                if most_m:
                    got(base + most_p, base + most_p)
                    value = value + taken(base + most_p)
                return value

            for k in (0, 1, -1):
                final(k)
            for t in range(NZP):
                if t == 1:
                    final(2)
                for xi in range(4):
                    most_p, most_m = hops[xi]
                    base = xi * (Z - 1)
                    if most_p - t >= 1:
                        link(xi, most_p - t, most_p, base, 1, up)
                    if most_m - t >= 1:
                        link(xi, most_m - t, most_m, base + most_p, -1, down)
                if t == 0:
                    hook_a()
                if t == NZP - 1:
                    hook_b()
            sbuf[xslot] = total(0).astype(jnp.bfloat16)
            put(xslot, xslot, xslot, right, lo)
            put(xslot, xslot, xslot + 1, left, hi)
            ahead, behind = total(1), total(2)
            sbuf[xslot + 1, hi, :] = ahead[HS:].astype(jnp.bfloat16)
            sbuf[xslot + 2, lo, :] = behind[:HS].astype(jnp.bfloat16)
            got(xslot, xslot, lo)
            sbuf[xslot + 1, lo, :] = (ahead[:HS] + taken(xslot, lo)).astype(jnp.bfloat16)
            put(xslot + 1, xslot + 1, xslot + 2, right)
            got(xslot, xslot + 1, hi)
            sbuf[xslot + 2, hi, :] = (behind[HS:] + taken(xslot, hi)).astype(jnp.bfloat16)
            put(xslot + 2, xslot + 2, xslot + 3, left)
            value = total(3)
            got(xslot + 1, xslot + 2)
            got(xslot + 2, xslot + 3)
            wgf[...] = value + taken(xslot + 1) + taken(xslot + 2)
        remote(sbuf, rbuf, rs_s.at[0], rs_r.at[0], partner).wait_send()

    @pl.when(c == 0)
    def _():
        reduce("x")

    @pl.when(c == 1)
    def _():
        reduce("z")

    grad = wgf[...]
    row_sum = jnp.sum(grad * grad + SQUARE_EPS, axis=-1, keepdims=True)
    eye = lax.broadcasted_iota(jnp.int32, (SR, SR), 0) == lax.broadcasted_iota(jnp.int32, (SR, SR), 1)
    row_old = jnp.sum(jnp.where(eye, jnp.broadcast_to(row_ref[...], (SR, SR)), 0.0), axis=-1, keepdims=True)
    row_new = DECAY_RATE * row_old + (1.0 - DECAY_RATE) * (row_sum / D)
    rown_ref[...] = jnp.sum(jnp.where(eye, jnp.broadcast_to(row_new, (SR, SR)), 0.0), axis=0, keepdims=True)
    per_row = 1.0 / row_new
    wgf[...] = grad * lax.rsqrt(row_new)
    E = 2 * X
    SL = D // E
    e = x * 2 + c
    col_sum = jnp.sum(grad * grad + SQUARE_EPS, axis=0, keepdims=True)
    col_part = jnp.sum(grad * grad * per_row, axis=0, keepdims=True)
    row_total = jnp.broadcast_to(jnp.sum(row_new, axis=0, keepdims=True), (1, 128))
    for k in range(E):
        cols = slice(k * SL, (k + 1) * SL)
        tv[k, :, pl.ds(0, SL)] = col_sum[:, cols]
        tv[k, :, pl.ds(SL, SL)] = col_part[:, cols]
        tv[k, :, pl.ds(2 * SL, 128)] = row_total

    def slice_of(k):
        return ((x + k // 2) % X) * 2 + (c + k) % 2

    first = [
        remote(tv.at[slice_of(k)], t1.at[e], t_s.at[k - 1], t_r.at[k - 1], p)
        for k, p in enumerate(near, start=1)
    ]
    second = spread(tu, t2, z, far, t_s, t_r, E - 1)
    third = spread(tw, t3, e, near, t_s, t_r, E + Z - 2)

    def exchange(copies, dst, place, value):
        for copy in copies:
            copy.start()
        dst[place] = value
        for copy in copies:
            copy.wait_recv()
        return added(dst)

    tu[...] = exchange(first, t1, e, tv[e])
    sums = exchange(second, t2, z, tu[...])
    col_old = col_ref[:, pl.ds(pl.multiple_of(e * SL, SL), SL)]
    fresh_cols = DECAY_RATE * col_old + (1.0 - DECAY_RATE) * sums[:, 0:SL] / D
    tw[:, pl.ds(0, SL)] = fresh_cols
    share_sum = jnp.sum(sums[:, SL : 2 * SL] / fresh_cols, axis=-1, keepdims=True)
    tw[:, pl.ds(SL, 128)] = jnp.broadcast_to(share_sum, (1, 128))
    shares = exchange(third, t3, e, tw[...])
    for k in range(E):
        coln_ref[:, pl.ds(k * SL, SL)] = t3[k, :, pl.ds(0, SL)]
    col_new = coln_ref[...]
    row_mean = sums[:, 2 * SL : 2 * SL + 1] / D
    total_square = row_mean * shares[:, SL : SL + 1]
    clip = jnp.maximum(1.0, jnp.sqrt(total_square / (D * D)))
    step_ref[...] = wgf[...] * (lax.rsqrt(col_new) * (jnp.sqrt(row_mean) / clip))
    for copy in gain_far():
        copy.wait_recv()
    gg_ref[...] = added(g2)

    own_copy().wait_send()

    @pl.when(c == 0)
    def _():
        gathered(cols_a)

    @pl.when(c == 1)
    def _():
        gathered(cols_b)

    for copy in first + second + third + gain_near() + gain_far():
        copy.wait_send()
    save().wait()
    for m in range(MICRO):
        nt_send(m).wait_send()
    shared = gs.at[:, pl.ds(0, TR)]
    remote(shared, shared, f_s.at[0], f_r.at[0], partner).wait_send()

    @pl.when(s > 0)
    def _():
        remote(outs, outs, y_s.at[0], y_r.at[0], partner).wait_send()


def deliver(*refs):
    n = 5
    sources, results, held, sems = refs[:n], refs[n : 2 * n], refs[2 * n : 3 * n], refs[-1]
    ways = []
    for src, mid, dst in zip(sources, held, results):
        pieces = src.shape[0] if len(src.shape) == 3 else 1
        for k in range(pieces):
            trio = (src.at[k], mid.at[k], dst.at[k]) if pieces > 1 else (src, mid, dst)
            half = trio[0].shape[0] // 2
            parts = [pl.ds(0, half), pl.ds(half, half)] if pieces > 1 else [None]
            for part in parts:
                a, m, b = trio if part is None else [ref.at[part] for ref in trio]
                i = len(ways)
                ways.append(
                    (
                        pltpu.make_async_copy(a, m, sems.at[0, i]),
                        pltpu.make_async_copy(m, b, sems.at[1, i]),
                    )
                )
    for into, _ in ways:
        into.start()
    for into, out in ways:
        into.wait()
        out.start()
    for _, out in ways:
        out.wait()


def body(saved_inputs, out_cotangent, weights, gains, row_state, col_state):
    S, DP = lax.axis_size("section"), lax.axis_size("dp")
    Z = DP // (2 * X)
    _, MICRO, TR, D = saved_inputs.shape
    SR = weights.shape[1]
    NC = DP // 2
    R = TR // 4
    CA = D * 9 // 16
    U = MICRO * (TR // R)
    SL = D // (2 * X)
    bf, f32 = jnp.bfloat16, jnp.float32
    dma = pltpu.SemaphoreType.DMA
    vmem = pl.BlockSpec(memory_space=pltpu.VMEM)
    hbm = pl.BlockSpec(memory_space=pl.ANY)
    V = pltpu.VMEM
    scratch = [
        V((MICRO, TR, D), bf),
        V((MICRO, 2 * TR, D), bf),
        V((MICRO, TR, D), bf),
        V((NC, 2 * SR, D), bf),
        V((D, D), bf),
        V((MICRO, NC, 2, SR, TR), bf),
        V((MICRO, NC, SR, 2 * TR), bf),
        V((NC * SR, D), f32),
        V((R, D), f32),
        V((MICRO, TR, 128), f32),
        V((8, D), f32),
        V((SR, D), f32),
        V((TR, D), f32),
        V((NC - 1, SR, D), bf),
        V((NC - 1, SR, D), bf),
        V((2 * X, 1, 2 * SL + 128), f32),
        V((2 * X, 1, 2 * SL + 128), f32),
        V((1, 2 * SL + 128), f32),
        V((Z, 1, 2 * SL + 128), f32),
        V((1, SL + 128), f32),
        V((2 * X, 1, SL + 128), f32),
        V((2, 1, D), f32),
        V((2 * X, 1, D), f32),
        V((Z, 1, D), f32),
        dma((2,)),
        dma((MICRO,)),
        dma((1,)),
        dma((1,)),
        dma((5 * Z,)),
        dma((1,)),
        dma((Z,)),
        dma((1,)),
        dma((1,)),
        dma((MICRO,)),
        dma((MICRO,)),
        dma((1,)),
        dma((U + 1,)),
        dma((1,)),
        dma((MICRO,)),
        dma((1,)),
        dma((5 * Z,)),
        dma((4 * X + Z,)),
        dma((4 * X + Z,)),
        dma((2 * X + Z,)),
        dma((2 * X + Z,)),
    ]
    outs = pl.pallas_call(
        functools.partial(kernel, S, Z, R, CA),
        out_shape=(
            jax.ShapeDtypeStruct((MICRO, TR, D), bf),
            jax.ShapeDtypeStruct((SR, D), f32),
            jax.ShapeDtypeStruct((1, SR), f32),
            jax.ShapeDtypeStruct((1, D), f32),
            jax.ShapeDtypeStruct((1, D), f32),
        ),
        in_specs=[hbm, hbm, vmem, vmem, vmem, vmem],
        out_specs=(hbm, vmem, vmem, vmem, vmem),
        scratch_shapes=scratch,
        compiler_params=pltpu.CompilerParams(
            collective_id=0, has_side_effects=True, vmem_limit_bytes=60 * 2**20
        ),
        name="relay_back",
    )(saved_inputs[0], out_cotangent, weights[0], gains, row_state, col_state)
    outs = pl.pallas_call(
        deliver,
        out_shape=tuple(jax.ShapeDtypeStruct(o.shape, o.dtype) for o in outs),
        in_specs=[hbm] * 5,
        out_specs=(hbm,) * 5,
        scratch_shapes=[V(o.shape, o.dtype) for o in outs] + [dma((2, 2 * MICRO + 4))],
        name="deliver",
    )(*outs)
    return (outs[0][None], outs[1][None], outs[2], outs[3], outs[4])


def solution(mesh):
    placed = (
        P("section", None, "dp", None),
        P(None, "dp", None),
        P("section", "dp", None),
        P("section", None),
        P("section", "dp"),
        P("section", None),
    )
    return jax.shard_map(
        body,
        mesh=mesh,
        in_specs=placed,
        out_specs=(
            P("section", None, "dp", None),
            P("section", "dp", None),
            P("section", "dp"),
            P("section", None),
            P("section", None),
        ),
        check_vma=False,
    )
```

```python
import functools

import jax
import jax.numpy as jnp
from jax import lax
from jax.experimental import pallas as pl
from jax.experimental.pallas import tpu as pltpu
from jax.sharding import PartitionSpec as P

DECAY_RATE = 0.9
SQUARE_EPS = 1e-30
NORM_EPS = 1e-06
X = 4
MESH = pl.DeviceIdType.MESH
NT = (((1,), (1,)), ((), ()))
NN = (((1,), (0,)), ((), ()))


def kernel(
    S, Z, R, CA,
    x_hbm, cot_hbm, w_ref, gain_ref, row_ref, col_ref,
    out_hbm, step_ref, rown_ref, coln_ref, gg_ref,
    xs, gs, outs, wg, wt, nt, lt, acc, gained, invs, gacc, wgf, rbuf, sbuf, tv, t1, tu, t2, tw, t3, gv, g1, g2,
    in_sem, lsem, out_sem, ag_s, ag_r, d_s, d_r, own_s, own_r, l_s, l_r,
    y_s, y_r, f_s, f_r, rs_s, rs_r, t_s, t_r, g_s, g_r,
):
    MICRO, TR, D = xs.shape
    SR = w_ref.shape[0]
    NC = Z * X
    H = TR // R
    U = MICRO * H
    NZP, NZM = Z // 2, Z // 2 - 1
    HB, HS = SR, SR // 2
    QW = min(256, D)
    NQ = D // QW
    s = lax.axis_index("section")
    dp = lax.axis_index("dp")
    z, x, c = dp // (2 * X), (dp // 2) % X, dp % 2

    def chip(dz, dx):
        return ((z + dz + Z) % Z) * X + (x + dx + X) % X

    def dev(dz, dx, flip=0):
        return (s, chip(dz, dx) * 2 + (c + flip) % 2)

    partner = dev(0, 0, 1)

    def remote(src, dst, ss, rs, device):
        return pltpu.make_async_remote_copy(
            src_ref=src, dst_ref=dst, send_sem=ss, recv_sem=rs, device_id=device, device_id_type=MESH
        )

    def load_x():
        return pltpu.make_async_copy(x_hbm, xs, in_sem.at[0])

    def load_cot():
        return pltpu.make_async_copy(cot_hbm, gs.at[:, pl.ds(0, TR)], in_sem.at[1])

    load_x().start()

    @pl.when(s == S - 1)
    def _():
        load_cot().start()

    own_row = pl.multiple_of(c * SR, SR)
    other_row = pl.multiple_of((1 - c) * SR, SR)
    wg[chip(0, 0), pl.ds(own_row, SR), :] = w_ref[...]

    barrier = pltpu.get_barrier_semaphore()
    peers = [dev(0, k // 2, k % 2) for k in range(1, 2 * X)] + [dev(k, 0) for k in range(1, Z)]
    for p in peers:
        pl.semaphore_signal(barrier, inc=1, device_id=p, device_id_type=MESH)

    for ds in (1, S - 1):
        pl.semaphore_signal(barrier, inc=1, device_id=((s + ds) % S, dp), device_id_type=MESH)
    pl.semaphore_wait(barrier, len(peers) + 2)

    def nt_send(m):
        return remote(nt.at[m, :, 1 - c], lt.at[m, :, :, pl.ds(TR, TR)], l_s.at[m], l_r.at[m], partner)

    def nt_local(m):
        return pltpu.make_async_copy(nt.at[m, :, c], lt.at[m, :, :, pl.ds(0, TR)], lsem.at[m])

    def prepare(m):
        if m == 0:
            load_x().wait()
        total = jnp.zeros((TR, 1), jnp.float32)
        for q in range(NQ):
            part = xs[m, :, pl.ds(q * QW, QW)].astype(jnp.float32)
            total = total + jnp.sum(part * part, axis=-1, keepdims=True)
        inv = lax.rsqrt(total / D + NORM_EPS)
        invs[m] = jnp.broadcast_to(inv, invs.shape[1:])
        for q in range(NQ):
            cols = pl.ds(q * QW, QW)
            whitened = xs[m, :, cols].astype(jnp.float32) * inv
            normed = whitened * gain_ref[:, cols]
            n = QW // (2 * SR)
            nt[m, pl.ds(q * n, n)] = normed.T.astype(jnp.bfloat16).reshape(n, 2, SR, TR)
        nt_local(m).start()
        nt_send(m).start()

    def own_copy():
        rows = wg.at[chip(0, 0), pl.ds(own_row, SR)]
        return remote(rows, rows, own_s.at[0], own_r.at[0], partner)

    def gather(first, cols, other_cols, order):
        def blk(dz, dx, rows=pl.ds(0, 2 * SR)):
            return wg.at[chip(dz, dx), rows, cols]

        lo, hi = pl.ds(0, HB), pl.ds(HB, HB)

        def put(view, sem, device):
            remote(view, view, ag_s.at[0], ag_r.at[sem], device).start()

        def across(view, i):
            remote(view, view, d_s.at[0], d_r.at[i], partner).start()

        def put_own(base_rows, places):
            for sem, device in places:
                put(blk(0, 0, pl.ds(base_rows, SR)), sem, device)

        def group(i):
            return 0 if i == 0 else (-(i + 1) // 2 if i % 2 else i // 2)

        def flip(i, part):
            first_chip = ((z + group(i) + Z) % Z) * X
            block = wg[pl.ds(first_chip, X), :, part].reshape(X * 2 * SR, part.size)
            width = X * 2 * SR
            wt[part, pl.ds(pl.multiple_of(first_chip * 2 * SR, width), width)] = block.T

        def flip_other(i):
            n = X if i else X - 1
            whole = wg.at[pl.ds(0, n), :, other_cols]
            remote(whole, whole, d_s.at[0], d_r.at[i], partner).wait_recv()
            flip(i, other_cols)

        def got(view, sem):
            remote(view, view, ag_s.at[0], ag_r.at[sem], partner).wait_recv()

        right, left, up, down = dev(0, 1), dev(0, -1), dev(1, 0), dev(-1, 0)
        fill = iter(range(MICRO))

        def filler():
            m = next(fill, None)
            if m is not None:
                prepare(m)
                rows = pl.ds(m * (NC * SR // MICRO), NC * SR // MICRO)
                acc[rows, :] = jnp.zeros((NC * SR // MICRO, D), jnp.float32)
            if m == 0:
                gacc[...] = jnp.zeros_like(gacc)

        if first == "z":
            zp = lambda k: k - 1
            zm = lambda k: NZP + k - 1
            base = Z - 1

            def x_out(i, rel):
                put(blk(rel, 0), base + 4 * i, right)
                put(blk(rel, 0), base + 4 * i + 1, left)
                across(blk(rel, 0), i)

            def x_mid(i, rel):
                got(blk(rel, -1), base + 4 * i)
                put(blk(rel, -1, lo), base + 4 * i + 2, right)
                across(blk(rel, -1), i)
                got(blk(rel, 1), base + 4 * i + 1)
                put(blk(rel, 1, hi), base + 4 * i + 3, left)
                across(blk(rel, 1), i)

            def x_end(i, rel):
                got(blk(rel, 2, lo), base + 4 * i + 2)
                got(blk(rel, 2, hi), base + 4 * i + 3)
                across(blk(rel, 2), i)
                flip(i, cols)

            places = [(zp(1), up), (base, right), (base + 1, left)]
            if NZM:
                places.insert(1, (zm(1), down))
            put_own(own_row, places)
            own_copy().wait_recv()
            put_own(other_row, places)
            filler()
            mids, ends, i = [(0, 0)], [], 0
            for k in range(1, NZP + 1):
                fresh = []
                got(blk(-k, 0), zp(k))
                if k < NZP:
                    put(blk(-k, 0), zp(k + 1), up)
                i += 1
                x_out(i, -k)
                fresh.append((i, -k))
                if k <= NZM:
                    got(blk(k, 0), zm(k))
                    if k < NZM:
                        put(blk(k, 0), zm(k + 1), down)
                    i += 1
                    x_out(i, k)
                    fresh.append((i, k))
                for pair in mids:
                    x_mid(*pair)
                for pair in ends:
                    x_end(*pair)
                mids, ends = fresh, mids
                filler()
            for pair in mids:
                x_mid(*pair)
            for pair in ends:
                x_end(*pair)
            for i in range(Z - 1):
                flip_other(i)
            for pair in mids:
                x_end(*pair)
            flip_other(Z - 1)
        else:
            rels = [0, -1, 1, 2]
            hops = [(NZP, NZM), (NZM, NZP), (NZP, NZM), (NZM, NZP)]
            zp = lambda xi, k: 4 + xi * Z + k - 1
            zm = lambda xi, k: 4 + xi * Z + NZP + k - 1

            def z_out(xi):
                put(blk(0, rels[xi]), zp(xi, 1), up)
                put(blk(0, rels[xi]), zm(xi, 1), down)

            places = [(0, right), (1, left), (zp(0, 1), up), (zm(0, 1), down)]
            put_own(own_row, places)
            own_copy().wait_recv()
            put_own(other_row, places)
            filler()
            got(blk(0, -1), 0)
            put(blk(0, -1, lo), 2, right)
            z_out(1)
            across(blk(0, -1), 0)
            got(blk(0, 1), 1)
            put(blk(0, 1, hi), 3, left)
            z_out(2)
            across(blk(0, 1), 0)
            filler()
            got(blk(0, 2, lo), 2)
            got(blk(0, 2, hi), 3)
            z_out(3)
            across(blk(0, 2), 0)
            flip(0, cols)
            flipped = 0
            for k in range(1, NZP + 1):
                for xi in range(4):
                    most_p, most_m = hops[xi]
                    if k <= most_p:
                        got(blk(-k, rels[xi]), zp(xi, k))
                        if k < most_p:
                            put(blk(-k, rels[xi]), zp(xi, k + 1), up)
                        across(blk(-k, rels[xi]), 2 * k - 1)
                    if k <= most_m:
                        got(blk(k, rels[xi]), zm(xi, k))
                        if k < most_m:
                            put(blk(k, rels[xi]), zm(xi, k + 1), down)
                        across(blk(k, rels[xi]), 2 * k if k < NZP else 2 * k - 1)
                flip(2 * k - 1, cols)
                if k < NZP:
                    flip(2 * k, cols)
                if k > 2:
                    flip_other(flipped)
                    flip_other(flipped + 1)
                    flipped += 2
                filler()
            for i in range(flipped, Z):
                flip_other(i)
        for _ in range(MICRO):
            filler()

    own_copy().start()

    @pl.when(s == S - 1)
    def _():
        load_cot().wait()

    cols_a, cols_b = pl.ds(0, CA), pl.ds(CA, D - CA)

    @pl.when(c == 0)
    def _():
        gather("z", cols_a, cols_b, None)

    @pl.when(c == 1)
    def _():
        gather("x", cols_b, cols_a, None)

    def gathered(cols):
        everything = wg.at[pl.ds(0, NC - 1), :, cols]
        remote(everything, everything, ag_s.at[0], ag_r.at[0], partner).wait_send()
        remote(everything, everything, d_s.at[0], d_r.at[0], partner).wait_send()

    def hand_down(m, rows, u):
        return remote(outs.at[m, rows], gs.at[m, rows], y_s.at[0], y_r.at[u], (s - 1, dp))

    def share(m, rows, there):
        return remote(gs.at[m, rows], gs.at[m, there], f_s.at[0], f_r.at[m], partner)

    def save():
        return pltpu.make_async_copy(outs, out_hbm, out_sem.at[0])

    def place(u, base=0):
        return u // H, pl.ds(pl.multiple_of(base + (u % H) * R, R), R)

    def differentiate(m, rows):
        R = rows.size
        g = gs[m, rows, :]
        inv = invs[m, rows, 0:1]
        dots = jnp.zeros((R, 1), jnp.float32)
        for q in range(NQ):
            cols = pl.ds(q * QW, QW)
            branch = lax.dot_general(g, wt[:, cols], NN, preferred_element_type=jnp.float32)
            whitened = xs[m, rows, cols].astype(jnp.float32) * inv
            both = branch * whitened
            gacc[:, cols] += jnp.sum(both.reshape(R // 8, 8, QW), axis=0)
            dots = dots + jnp.sum(both * gain_ref[:, cols], axis=-1, keepdims=True)
            gained[pl.ds(0, R), cols] = branch * gain_ref[:, cols]
        mean = dots / D
        for q in range(NQ):
            cols = pl.ds(q * QW, QW)
            whitened = xs[m, rows, cols].astype(jnp.float32) * inv
            fresh = gs[m, rows, cols].astype(jnp.float32) + inv * (gained[pl.ds(0, R), cols] - whitened * mean)
            outs[m, rows, cols] = fresh.astype(jnp.bfloat16)

    quarter = NC * SR // H

    def weigh(m, r):
        rows = pl.ds(pl.multiple_of(r * quarter, quarter), quarter)
        n = quarter // SR
        lhs = lt[m, pl.ds(r * n, n)].reshape(quarter, 2 * TR)
        acc[rows, :] += lax.dot_general(lhs, gs[m], NN, preferred_element_type=jnp.float32)

    def meet(m):
        nt_local(m).wait()
        nt_send(m).wait_recv()
        share(m, pl.ds(0, TR), pl.ds(TR, TR)).wait_recv()

    lag = jnp.where(s == 0, 1, 0)

    def tick(u, carry):
        m, rows = place(u)

        @pl.when(s < S - 1)
        def _():
            hand_down(m, rows, u).wait_recv()

        @pl.when(u > lag)
        def _():
            differentiate(*place(u - lag))

        @pl.when(s > 0)
        def _():
            hand_down(m, rows, u).start()

        share(m, rows, place(u, TR)[1]).start()

        @pl.when(u >= H)
        def _():
            @pl.when(u % H == 0)
            def _():
                meet(m - 1)

            weigh(m - 1, u % H)

        return carry

    for k in range(2):
        rows, there = pl.ds(k * (R // 2), R // 2), pl.ds(TR + k * (R // 2), R // 2)
        sem = U if k else 0

        @pl.when(s < S - 1)
        def _():
            hand_down(0, rows, sem).wait_recv()

        differentiate(0, rows)

        @pl.when(s > 0)
        def _():
            hand_down(0, rows, sem).start()

        share(0, rows, there).start()

    lax.fori_loop(1, U, tick, 0)
    meet(MICRO - 1)

    far_part = (((z + NZP) % Z) * H) // Z

    def final(k):
        weigh(MICRO - 1, (far_part + k + H) % H)

    def spread(src, dst, place, targets, ss, rs, sem0):
        return [remote(src, dst.at[place], ss.at[sem0 + k], rs.at[sem0 + k], t) for k, t in enumerate(targets)]

    def added(dst):
        total = dst[0]
        for k in range(1, dst.shape[0]):
            total = total + dst[k]
        return total

    near, far = peers[: 2 * X - 1], peers[2 * X - 1 :]

    def gain_near():
        return spread(gv.at[0], g1, x * 2 + c, near, g_s, g_r, 0)

    def gain_far():
        return spread(gv.at[1], g2, z, far, g_s, g_r, 2 * X - 1)

    def hook_a():
        @pl.when(s == 0)
        def _():
            differentiate(*place(U - 1))

        save().start()
        gv[0] = jnp.sum(gacc[...], axis=0, keepdims=True)
        for copy in gain_near():
            copy.start()
        g1[x * 2 + c] = gv[0]

    def hook_b():
        for copy in gain_near():
            copy.wait_recv()
        gv[1] = added(g1)
        for copy in gain_far():
            copy.start()
        g2[z] = gv[1]

    def mine(dz, dx):
        return acc[pl.ds(pl.multiple_of(chip(dz, dx) * SR, SR), SR), :]

    def reduce(first):
        right, left, up, down = dev(0, 1), dev(0, -1), dev(1, 0), dev(-1, 0)
        lo, hi, full = pl.ds(0, HS), pl.ds(HS, HS), pl.ds(0, SR)

        def put(i, slot, sem, device, rows=full):
            remote(sbuf.at[i, rows], rbuf.at[slot, rows], rs_s.at[0], rs_r.at[sem], device).start()

        def got(slot, sem, rows=full):
            view = rbuf.at[slot, rows]
            remote(view, view, rs_s.at[0], rs_r.at[sem], partner).wait_recv()

        def taken(slot, rows=full):
            return rbuf[slot, rows, :].astype(jnp.float32)

        if first == "x":
            rels = []
            for k in range(NZP, 0, -1):
                rels.append(k)
                if k > 1:
                    rels.append(-(k - 1))
            rels.append(0)
            zslot, zsem = 3 * Z, 4 * Z

            def one(i):
                sbuf[3 * i] = mine(rels[i], 2).astype(jnp.bfloat16)
                put(3 * i, 3 * i, 4 * i, right, lo)
                put(3 * i, 3 * i, 4 * i + 1, left, hi)

            def two(i):
                got(3 * i, 4 * i, lo)
                value = mine(rels[i], 1)
                sbuf[3 * i + 1, lo, :] = (value[:HS] + taken(3 * i, lo)).astype(jnp.bfloat16)
                sbuf[3 * i + 1, hi, :] = value[HS:].astype(jnp.bfloat16)
                put(3 * i + 1, 3 * i + 1, 4 * i + 2, right)
                got(3 * i, 4 * i + 1, hi)
                value = mine(rels[i], -1)
                sbuf[3 * i + 2, lo, :] = value[:HS].astype(jnp.bfloat16)
                sbuf[3 * i + 2, hi, :] = (value[HS:] + taken(3 * i, hi)).astype(jnp.bfloat16)
                put(3 * i + 2, 3 * i + 2, 4 * i + 3, left)

            def three(i):
                rel = rels[i]
                got(3 * i + 1, 4 * i + 2)
                got(3 * i + 2, 4 * i + 3)
                value = mine(rel, 0) + taken(3 * i + 1) + taken(3 * i + 2)
                if rel > 0:
                    slot = zslot + rel - 1
                    if rel < NZP:
                        got(slot + 1, zsem + rel)
                        value = value + taken(slot + 1)
                    sbuf[slot] = value.astype(jnp.bfloat16)
                    put(slot, slot, zsem + rel - 1, up)
                elif rel < 0:
                    slot = zslot + NZP - rel - 1
                    if -rel < NZM:
                        got(slot + 1, zsem + NZP - rel)
                        value = value + taken(slot + 1)
                    sbuf[slot] = value.astype(jnp.bfloat16)
                    put(slot, slot, zsem + NZP - rel - 1, down)
                else:
                    got(zslot, zsem)
                    value = value + taken(zslot)
                    if NZM:
                        got(zslot + NZP, zsem + NZP)
                        value = value + taken(zslot + NZP)
                    wgf[...] = value

            final(0)
            final(1)
            for i in range(Z + 4):
                if i < Z:
                    one(i)
                if i == 1:
                    final(-1)
                    final(2)
                if 0 <= i - 2 < Z:
                    two(i - 2)
                if 0 <= i - 4 < Z:
                    three(i - 4)
                if i == 2:
                    hook_a()
                if i == Z:
                    hook_b()
        else:
            rels = [2, 1, -1, 0]
            hops = [(NZP, NZM), (NZM, NZP), (NZP, NZM), (NZM, NZP)]
            zs = lambda xi, j: xi * (Z - 1) + j - 1
            xslot = 4 * (Z - 1)

            def link(xi, j, most, base, sign, device):
                value = mine(sign * j, rels[xi])
                slot = base + j - 1
                if j < most:
                    got(slot + 1, slot + 1)
                    value = value + taken(slot + 1)
                sbuf[slot] = value.astype(jnp.bfloat16)
                put(slot, slot, slot, device)

            def total(xi):
                most_p, most_m = hops[xi]
                base = xi * (Z - 1)
                value = mine(0, rels[xi])
                if most_p:
                    got(base, base)
                    value = value + taken(base)
                if most_m:
                    got(base + most_p, base + most_p)
                    value = value + taken(base + most_p)
                return value

            for k in (0, 1, -1):
                final(k)
            for t in range(NZP):
                if t == 1:
                    final(2)
                for xi in range(4):
                    most_p, most_m = hops[xi]
                    base = xi * (Z - 1)
                    if most_p - t >= 1:
                        link(xi, most_p - t, most_p, base, 1, up)
                    if most_m - t >= 1:
                        link(xi, most_m - t, most_m, base + most_p, -1, down)
                if t == 0:
                    hook_a()
                if t == NZP - 1:
                    hook_b()
            sbuf[xslot] = total(0).astype(jnp.bfloat16)
            put(xslot, xslot, xslot, right, lo)
            put(xslot, xslot, xslot + 1, left, hi)
            ahead, behind = total(1), total(2)
            sbuf[xslot + 1, hi, :] = ahead[HS:].astype(jnp.bfloat16)
            sbuf[xslot + 2, lo, :] = behind[:HS].astype(jnp.bfloat16)
            got(xslot, xslot, lo)
            sbuf[xslot + 1, lo, :] = (ahead[:HS] + taken(xslot, lo)).astype(jnp.bfloat16)
            put(xslot + 1, xslot + 1, xslot + 2, right)
            got(xslot, xslot + 1, hi)
            sbuf[xslot + 2, hi, :] = (behind[HS:] + taken(xslot, hi)).astype(jnp.bfloat16)
            put(xslot + 2, xslot + 2, xslot + 3, left)
            value = total(3)
            got(xslot + 1, xslot + 2)
            got(xslot + 2, xslot + 3)
            wgf[...] = value + taken(xslot + 1) + taken(xslot + 2)
        remote(sbuf, rbuf, rs_s.at[0], rs_r.at[0], partner).wait_send()

    @pl.when(c == 0)
    def _():
        reduce("x")

    @pl.when(c == 1)
    def _():
        reduce("z")

    grad = wgf[...]
    row_sum = jnp.sum(grad * grad + SQUARE_EPS, axis=-1, keepdims=True)
    eye = lax.broadcasted_iota(jnp.int32, (SR, SR), 0) == lax.broadcasted_iota(jnp.int32, (SR, SR), 1)
    row_old = jnp.sum(jnp.where(eye, jnp.broadcast_to(row_ref[...], (SR, SR)), 0.0), axis=-1, keepdims=True)
    row_new = DECAY_RATE * row_old + (1.0 - DECAY_RATE) * (row_sum / D)
    rown_ref[...] = jnp.sum(jnp.where(eye, jnp.broadcast_to(row_new, (SR, SR)), 0.0), axis=0, keepdims=True)
    per_row = 1.0 / row_new
    wgf[...] = grad * lax.rsqrt(row_new)
    E = 2 * X
    SL = D // E
    e = x * 2 + c
    col_sum = jnp.sum(grad * grad + SQUARE_EPS, axis=0, keepdims=True)
    col_part = jnp.sum(grad * grad * per_row, axis=0, keepdims=True)
    row_total = jnp.broadcast_to(jnp.sum(row_new, axis=0, keepdims=True), (1, 128))
    for k in range(E):
        cols = slice(k * SL, (k + 1) * SL)
        tv[k, :, pl.ds(0, SL)] = col_sum[:, cols]
        tv[k, :, pl.ds(SL, SL)] = col_part[:, cols]
        tv[k, :, pl.ds(2 * SL, 128)] = row_total

    def slice_of(k):
        return ((x + k // 2) % X) * 2 + (c + k) % 2

    first = [
        remote(tv.at[slice_of(k)], t1.at[e], t_s.at[k - 1], t_r.at[k - 1], p)
        for k, p in enumerate(near, start=1)
    ]
    second = spread(tu, t2, z, far, t_s, t_r, E - 1)
    third = spread(tw, t3, e, near, t_s, t_r, E + Z - 2)

    def exchange(copies, dst, place, value):
        for copy in copies:
            copy.start()
        dst[place] = value
        for copy in copies:
            copy.wait_recv()
        return added(dst)

    tu[...] = exchange(first, t1, e, tv[e])
    sums = exchange(second, t2, z, tu[...])
    col_old = col_ref[:, pl.ds(pl.multiple_of(e * SL, SL), SL)]
    fresh_cols = DECAY_RATE * col_old + (1.0 - DECAY_RATE) * sums[:, 0:SL] / D
    tw[:, pl.ds(0, SL)] = fresh_cols
    share_sum = jnp.sum(sums[:, SL : 2 * SL] / fresh_cols, axis=-1, keepdims=True)
    tw[:, pl.ds(SL, 128)] = jnp.broadcast_to(share_sum, (1, 128))
    shares = exchange(third, t3, e, tw[...])
    for k in range(E):
        coln_ref[:, pl.ds(k * SL, SL)] = t3[k, :, pl.ds(0, SL)]
    col_new = coln_ref[...]
    row_mean = sums[:, 2 * SL : 2 * SL + 1] / D
    total_square = row_mean * shares[:, SL : SL + 1]
    clip = jnp.maximum(1.0, jnp.sqrt(total_square / (D * D)))
    step_ref[...] = wgf[...] * (lax.rsqrt(col_new) * (jnp.sqrt(row_mean) / clip))
    for copy in gain_far():
        copy.wait_recv()
    gg_ref[...] = added(g2)

    own_copy().wait_send()

    @pl.when(c == 0)
    def _():
        gathered(cols_a)

    @pl.when(c == 1)
    def _():
        gathered(cols_b)

    for copy in first + second + third + gain_near() + gain_far():
        copy.wait_send()
    save().wait()
    for m in range(MICRO):
        nt_send(m).wait_send()
    shared = gs.at[:, pl.ds(0, TR)]
    remote(shared, shared, f_s.at[0], f_r.at[0], partner).wait_send()

    @pl.when(s > 0)
    def _():
        remote(outs, outs, y_s.at[0], y_r.at[0], partner).wait_send()


def deliver(*refs):
    n = 5
    sources, results, held, sems = refs[:n], refs[n : 2 * n], refs[2 * n : 3 * n], refs[-1]
    ways = []
    for src, mid, dst in zip(sources, held, results):
        pieces = src.shape[0] if len(src.shape) == 3 else 1
        for k in range(pieces):
            trio = (src.at[k], mid.at[k], dst.at[k]) if pieces > 1 else (src, mid, dst)
            half = trio[0].shape[0] // 2
            parts = [pl.ds(0, half), pl.ds(half, half)] if pieces > 1 else [None]
            for part in parts:
                a, m, b = trio if part is None else [ref.at[part] for ref in trio]
                i = len(ways)
                ways.append(
                    (
                        pltpu.make_async_copy(a, m, sems.at[0, i]),
                        pltpu.make_async_copy(m, b, sems.at[1, i]),
                    )
                )
    for into, _ in ways:
        into.start()
    for into, out in ways:
        into.wait()
        out.start()
    for _, out in ways:
        out.wait()


def body(saved_inputs, out_cotangent, weights, gains, row_state, col_state):
    S, DP = lax.axis_size("section"), lax.axis_size("dp")
    Z = DP // (2 * X)
    _, MICRO, TR, D = saved_inputs.shape
    SR = weights.shape[1]
    NC = DP // 2
    R = TR // 4
    CA = D * 9 // 16
    U = MICRO * (TR // R)
    SL = D // (2 * X)
    bf, f32 = jnp.bfloat16, jnp.float32
    dma = pltpu.SemaphoreType.DMA
    vmem = pl.BlockSpec(memory_space=pltpu.VMEM)
    hbm = pl.BlockSpec(memory_space=pl.ANY)
    V = pltpu.VMEM
    scratch = [
        V((MICRO, TR, D), bf),
        V((MICRO, 2 * TR, D), bf),
        V((MICRO, TR, D), bf),
        V((NC, 2 * SR, D), bf),
        V((D, D), bf),
        V((MICRO, NC, 2, SR, TR), bf),
        V((MICRO, NC, SR, 2 * TR), bf),
        V((NC * SR, D), f32),
        V((R, D), f32),
        V((MICRO, TR, 128), f32),
        V((8, D), f32),
        V((SR, D), f32),
        V((NC - 1, SR, D), bf),
        V((NC - 1, SR, D), bf),
        V((2 * X, 1, 2 * SL + 128), f32),
        V((2 * X, 1, 2 * SL + 128), f32),
        V((1, 2 * SL + 128), f32),
        V((Z, 1, 2 * SL + 128), f32),
        V((1, SL + 128), f32),
        V((2 * X, 1, SL + 128), f32),
        V((2, 1, D), f32),
        V((2 * X, 1, D), f32),
        V((Z, 1, D), f32),
        dma((2,)),
        dma((MICRO,)),
        dma((1,)),
        dma((1,)),
        dma((5 * Z,)),
        dma((1,)),
        dma((Z,)),
        dma((1,)),
        dma((1,)),
        dma((MICRO,)),
        dma((MICRO,)),
        dma((1,)),
        dma((U + 1,)),
        dma((1,)),
        dma((MICRO,)),
        dma((1,)),
        dma((5 * Z,)),
        dma((4 * X + Z,)),
        dma((4 * X + Z,)),
        dma((2 * X + Z,)),
        dma((2 * X + Z,)),
    ]
    outs = pl.pallas_call(
        functools.partial(kernel, S, Z, R, CA),
        out_shape=(
            jax.ShapeDtypeStruct((MICRO, TR, D), bf),
            jax.ShapeDtypeStruct((SR, D), f32),
            jax.ShapeDtypeStruct((1, SR), f32),
            jax.ShapeDtypeStruct((1, D), f32),
            jax.ShapeDtypeStruct((1, D), f32),
        ),
        in_specs=[hbm, hbm, vmem, vmem, vmem, vmem],
        out_specs=(hbm, vmem, vmem, vmem, vmem),
        scratch_shapes=scratch,
        compiler_params=pltpu.CompilerParams(
            collective_id=0, has_side_effects=True, vmem_limit_bytes=60 * 2**20
        ),
        name="relay_back",
    )(saved_inputs[0], out_cotangent, weights[0], gains, row_state, col_state)
    outs = pl.pallas_call(
        deliver,
        out_shape=tuple(jax.ShapeDtypeStruct(o.shape, o.dtype) for o in outs),
        in_specs=[hbm] * 5,
        out_specs=(hbm,) * 5,
        scratch_shapes=[V(o.shape, o.dtype) for o in outs] + [dma((2, 2 * MICRO + 4))],
        name="deliver",
    )(*outs)
    return (outs[0][None], outs[1][None], outs[2], outs[3], outs[4])


def solution(mesh):
    placed = (
        P("section", None, "dp", None),
        P(None, "dp", None),
        P("section", "dp", None),
        P("section", None),
        P("section", "dp"),
        P("section", None),
    )
    return jax.shard_map(
        body,
        mesh=mesh,
        in_specs=placed,
        out_specs=(
            P("section", None, "dp", None),
            P("section", "dp", None),
            P("section", "dp"),
            P("section", None),
            P("section", None),
        ),
        check_vma=False,
    )
```

```python
import functools

import jax
import jax.numpy as jnp
from jax import lax
from jax.experimental import pallas as pl
from jax.experimental.pallas import tpu as pltpu
from jax.sharding import PartitionSpec as P

DECAY_RATE = 0.9
SQUARE_EPS = 1e-30
NORM_EPS = 1e-06
X = 4
MESH = pl.DeviceIdType.MESH
NT = (((1,), (1,)), ((), ()))
NN = (((1,), (0,)), ((), ()))


def kernel(
    S, Z, R, CA,
    x_hbm, cot_hbm, w_ref, gain_ref, row_ref, col_ref,
    out_hbm, step_ref, rown_ref, coln_ref, gg_ref,
    xs, gs, outs, wg, wt, nt, lt, acc, gained, invs, gacc, wgf, rbuf, sbuf, tv, t1, t2, gv, g1, g2,
    in_sem, lsem, out_sem, ag_s, ag_r, d_s, d_r, own_s, own_r, l_s, l_r,
    y_s, y_r, f_s, f_r, rs_s, rs_r, t_s, t_r, g_s, g_r,
):
    MICRO, TR, D = xs.shape
    SR = w_ref.shape[0]
    NC = Z * X
    H = TR // R
    U = MICRO * H
    NZP, NZM = Z // 2, Z // 2 - 1
    HB, HS = SR, SR // 2
    QW = min(256, D)
    NQ = D // QW
    s = lax.axis_index("section")
    dp = lax.axis_index("dp")
    z, x, c = dp // (2 * X), (dp // 2) % X, dp % 2

    def chip(dz, dx):
        return ((z + dz + Z) % Z) * X + (x + dx + X) % X

    def dev(dz, dx, flip=0):
        return (s, chip(dz, dx) * 2 + (c + flip) % 2)

    partner = dev(0, 0, 1)

    def remote(src, dst, ss, rs, device):
        return pltpu.make_async_remote_copy(
            src_ref=src, dst_ref=dst, send_sem=ss, recv_sem=rs, device_id=device, device_id_type=MESH
        )

    def load_x():
        return pltpu.make_async_copy(x_hbm, xs, in_sem.at[0])

    def load_cot():
        return pltpu.make_async_copy(cot_hbm, gs.at[:, pl.ds(0, TR)], in_sem.at[1])

    load_x().start()

    @pl.when(s == S - 1)
    def _():
        load_cot().start()

    own_row = pl.multiple_of(c * SR, SR)
    other_row = pl.multiple_of((1 - c) * SR, SR)
    wg[chip(0, 0), pl.ds(own_row, SR), :] = w_ref[...]

    barrier = pltpu.get_barrier_semaphore()
    peers = [dev(0, k // 2, k % 2) for k in range(1, 2 * X)] + [dev(k, 0) for k in range(1, Z)]
    for p in peers:
        pl.semaphore_signal(barrier, inc=1, device_id=p, device_id_type=MESH)

    for ds in (1, S - 1):
        pl.semaphore_signal(barrier, inc=1, device_id=((s + ds) % S, dp), device_id_type=MESH)
    pl.semaphore_wait(barrier, len(peers) + 2)

    def nt_send(m):
        return remote(nt.at[m, :, 1 - c], lt.at[m, :, :, pl.ds(TR, TR)], l_s.at[m], l_r.at[m], partner)

    def nt_local(m):
        return pltpu.make_async_copy(nt.at[m, :, c], lt.at[m, :, :, pl.ds(0, TR)], lsem.at[m])

    def prepare(m):
        if m == 0:
            load_x().wait()
        total = jnp.zeros((TR, 1), jnp.float32)
        for q in range(NQ):
            part = xs[m, :, pl.ds(q * QW, QW)].astype(jnp.float32)
            total = total + jnp.sum(part * part, axis=-1, keepdims=True)
        inv = lax.rsqrt(total / D + NORM_EPS)
        invs[m] = jnp.broadcast_to(inv, invs.shape[1:])
        for q in range(NQ):
            cols = pl.ds(q * QW, QW)
            whitened = xs[m, :, cols].astype(jnp.float32) * inv
            normed = whitened * gain_ref[:, cols]
            n = QW // (2 * SR)
            nt[m, pl.ds(q * n, n)] = normed.T.astype(jnp.bfloat16).reshape(n, 2, SR, TR)
        nt_local(m).start()
        nt_send(m).start()

    def own_copy():
        rows = wg.at[chip(0, 0), pl.ds(own_row, SR)]
        return remote(rows, rows, own_s.at[0], own_r.at[0], partner)

    def gather(first, cols, other_cols, order):
        def blk(dz, dx, rows=pl.ds(0, 2 * SR)):
            return wg.at[chip(dz, dx), rows, cols]

        lo, hi = pl.ds(0, HB), pl.ds(HB, HB)

        def put(view, sem, device):
            remote(view, view, ag_s.at[0], ag_r.at[sem], device).start()

        def across(view, i):
            remote(view, view, d_s.at[0], d_r.at[i], partner).start()

        def put_own(base_rows, places):
            for sem, device in places:
                put(blk(0, 0, pl.ds(base_rows, SR)), sem, device)

        def group(i):
            return 0 if i == 0 else (-(i + 1) // 2 if i % 2 else i // 2)

        def flip(i, part):
            first_chip = ((z + group(i) + Z) % Z) * X
            block = wg[pl.ds(first_chip, X), :, part].reshape(X * 2 * SR, part.size)
            width = X * 2 * SR
            wt[part, pl.ds(pl.multiple_of(first_chip * 2 * SR, width), width)] = block.T

        def flip_other(i):
            n = X if i else X - 1
            whole = wg.at[pl.ds(0, n), :, other_cols]
            remote(whole, whole, d_s.at[0], d_r.at[i], partner).wait_recv()
            flip(i, other_cols)

        def got(view, sem):
            remote(view, view, ag_s.at[0], ag_r.at[sem], partner).wait_recv()

        right, left, up, down = dev(0, 1), dev(0, -1), dev(1, 0), dev(-1, 0)
        fill = iter(range(MICRO))

        def filler():
            m = next(fill, None)
            if m is not None:
                prepare(m)
                rows = pl.ds(m * (NC * SR // MICRO), NC * SR // MICRO)
                acc[rows, :] = jnp.zeros((NC * SR // MICRO, D), jnp.float32)
            if m == 0:
                gacc[...] = jnp.zeros_like(gacc)

        if first == "z":
            zp = lambda k: k - 1
            zm = lambda k: NZP + k - 1
            base = Z - 1

            def x_out(i, rel):
                put(blk(rel, 0), base + 4 * i, right)
                put(blk(rel, 0), base + 4 * i + 1, left)
                across(blk(rel, 0), i)

            def x_mid(i, rel):
                got(blk(rel, -1), base + 4 * i)
                put(blk(rel, -1, lo), base + 4 * i + 2, right)
                across(blk(rel, -1), i)
                got(blk(rel, 1), base + 4 * i + 1)
                put(blk(rel, 1, hi), base + 4 * i + 3, left)
                across(blk(rel, 1), i)

            def x_end(i, rel):
                got(blk(rel, 2, lo), base + 4 * i + 2)
                got(blk(rel, 2, hi), base + 4 * i + 3)
                across(blk(rel, 2), i)
                flip(i, cols)

            places = [(zp(1), up), (base, right), (base + 1, left)]
            if NZM:
                places.insert(1, (zm(1), down))
            put_own(own_row, places)
            own_copy().wait_recv()
            put_own(other_row, places)
            filler()
            mids, ends, i = [(0, 0)], [], 0
            for k in range(1, NZP + 1):
                fresh = []
                got(blk(-k, 0), zp(k))
                if k < NZP:
                    put(blk(-k, 0), zp(k + 1), up)
                i += 1
                x_out(i, -k)
                fresh.append((i, -k))
                if k <= NZM:
                    got(blk(k, 0), zm(k))
                    if k < NZM:
                        put(blk(k, 0), zm(k + 1), down)
                    i += 1
                    x_out(i, k)
                    fresh.append((i, k))
                for pair in mids:
                    x_mid(*pair)
                for pair in ends:
                    x_end(*pair)
                mids, ends = fresh, mids
                filler()
            for pair in mids:
                x_mid(*pair)
            for pair in ends:
                x_end(*pair)
            for i in range(Z - 1):
                flip_other(i)
            for pair in mids:
                x_end(*pair)
            flip_other(Z - 1)
        else:
            rels = [0, -1, 1, 2]
            hops = [(NZP, NZM), (NZM, NZP), (NZP, NZM), (NZM, NZP)]
            zp = lambda xi, k: 4 + xi * Z + k - 1
            zm = lambda xi, k: 4 + xi * Z + NZP + k - 1

            def z_out(xi):
                put(blk(0, rels[xi]), zp(xi, 1), up)
                put(blk(0, rels[xi]), zm(xi, 1), down)

            places = [(0, right), (1, left), (zp(0, 1), up), (zm(0, 1), down)]
            put_own(own_row, places)
            own_copy().wait_recv()
            put_own(other_row, places)
            filler()
            got(blk(0, -1), 0)
            put(blk(0, -1, lo), 2, right)
            z_out(1)
            across(blk(0, -1), 0)
            got(blk(0, 1), 1)
            put(blk(0, 1, hi), 3, left)
            z_out(2)
            across(blk(0, 1), 0)
            filler()
            got(blk(0, 2, lo), 2)
            got(blk(0, 2, hi), 3)
            z_out(3)
            across(blk(0, 2), 0)
            flip(0, cols)
            flipped = 0
            for k in range(1, NZP + 1):
                for xi in range(4):
                    most_p, most_m = hops[xi]
                    if k <= most_p:
                        got(blk(-k, rels[xi]), zp(xi, k))
                        if k < most_p:
                            put(blk(-k, rels[xi]), zp(xi, k + 1), up)
                        across(blk(-k, rels[xi]), 2 * k - 1)
                    if k <= most_m:
                        got(blk(k, rels[xi]), zm(xi, k))
                        if k < most_m:
                            put(blk(k, rels[xi]), zm(xi, k + 1), down)
                        across(blk(k, rels[xi]), 2 * k if k < NZP else 2 * k - 1)
                flip(2 * k - 1, cols)
                if k < NZP:
                    flip(2 * k, cols)
                if k > 2:
                    flip_other(flipped)
                    flip_other(flipped + 1)
                    flipped += 2
                filler()
            for i in range(flipped, Z):
                flip_other(i)
        for _ in range(MICRO):
            filler()

    own_copy().start()

    @pl.when(s == S - 1)
    def _():
        load_cot().wait()

    cols_a, cols_b = pl.ds(0, CA), pl.ds(CA, D - CA)

    @pl.when(c == 0)
    def _():
        gather("z", cols_a, cols_b, None)

    @pl.when(c == 1)
    def _():
        gather("x", cols_b, cols_a, None)

    def gathered(cols):
        everything = wg.at[pl.ds(0, NC - 1), :, cols]
        remote(everything, everything, ag_s.at[0], ag_r.at[0], partner).wait_send()
        remote(everything, everything, d_s.at[0], d_r.at[0], partner).wait_send()

    def hand_down(m, rows, u):
        return remote(outs.at[m, rows], gs.at[m, rows], y_s.at[0], y_r.at[u], (s - 1, dp))

    def share(m, rows, there):
        return remote(gs.at[m, rows], gs.at[m, there], f_s.at[0], f_r.at[m], partner)

    def save():
        return pltpu.make_async_copy(outs, out_hbm, out_sem.at[0])

    def place(u, base=0):
        return u // H, pl.ds(pl.multiple_of(base + (u % H) * R, R), R)

    def differentiate(m, rows):
        R = rows.size
        g = gs[m, rows, :]
        inv = invs[m, rows, 0:1]
        dots = jnp.zeros((R, 1), jnp.float32)
        for q in range(NQ):
            cols = pl.ds(q * QW, QW)
            branch = lax.dot_general(g, wt[:, cols], NN, preferred_element_type=jnp.float32)
            whitened = xs[m, rows, cols].astype(jnp.float32) * inv
            both = branch * whitened
            gacc[:, cols] += jnp.sum(both.reshape(R // 8, 8, QW), axis=0)
            dots = dots + jnp.sum(both * gain_ref[:, cols], axis=-1, keepdims=True)
            gained[pl.ds(0, R), cols] = branch * gain_ref[:, cols]
        mean = dots / D
        for q in range(NQ):
            cols = pl.ds(q * QW, QW)
            whitened = xs[m, rows, cols].astype(jnp.float32) * inv
            fresh = gs[m, rows, cols].astype(jnp.float32) + inv * (gained[pl.ds(0, R), cols] - whitened * mean)
            outs[m, rows, cols] = fresh.astype(jnp.bfloat16)

    quarter = NC * SR // H

    def weigh(m, r):
        rows = pl.ds(pl.multiple_of(r * quarter, quarter), quarter)
        n = quarter // SR
        lhs = lt[m, pl.ds(r * n, n)].reshape(quarter, 2 * TR)
        acc[rows, :] += lax.dot_general(lhs, gs[m], NN, preferred_element_type=jnp.float32)

    def meet(m):
        nt_local(m).wait()
        nt_send(m).wait_recv()
        share(m, pl.ds(0, TR), pl.ds(TR, TR)).wait_recv()

    lag = jnp.where(s == 0, 1, 0)

    def tick(u, carry):
        m, rows = place(u)

        @pl.when(s < S - 1)
        def _():
            hand_down(m, rows, u).wait_recv()

        share(m, rows, place(u, TR)[1]).start()

        @pl.when(u > lag)
        def _():
            differentiate(*place(u - lag))

        @pl.when(s > 0)
        def _():
            hand_down(m, rows, u).start()

        @pl.when(u >= H)
        def _():
            @pl.when(u % H == 0)
            def _():
                meet(m - 1)

            weigh(m - 1, u % H)

        return carry

    for k in range(2):
        rows, there = pl.ds(k * (R // 2), R // 2), pl.ds(TR + k * (R // 2), R // 2)
        sem = U if k else 0

        @pl.when(s < S - 1)
        def _():
            hand_down(0, rows, sem).wait_recv()

        share(0, rows, there).start()
        differentiate(0, rows)

        @pl.when(s > 0)
        def _():
            hand_down(0, rows, sem).start()

    lax.fori_loop(1, U, tick, 0)
    meet(MICRO - 1)

    far_part = (((z + NZP) % Z) * H) // Z

    def final(k):
        weigh(MICRO - 1, (far_part + k + H) % H)

    def spread(src, dst, place, targets, ss, rs, sem0):
        return [remote(src, dst.at[place], ss.at[sem0 + k], rs.at[sem0 + k], t) for k, t in enumerate(targets)]

    def added(dst):
        total = dst[0]
        for k in range(1, dst.shape[0]):
            total = total + dst[k]
        return total

    near, far = peers[: 2 * X - 1], peers[2 * X - 1 :]

    def gain_near():
        return spread(gv.at[0], g1, x * 2 + c, near, g_s, g_r, 0)

    def gain_far():
        return spread(gv.at[1], g2, z, far, g_s, g_r, 2 * X - 1)

    def hook_a():
        @pl.when(s == 0)
        def _():
            differentiate(*place(U - 1))

        save().start()
        gv[0] = jnp.sum(gacc[...], axis=0, keepdims=True)
        for copy in gain_near():
            copy.start()
        g1[x * 2 + c] = gv[0]

    def hook_b():
        for copy in gain_near():
            copy.wait_recv()
        gv[1] = added(g1)
        for copy in gain_far():
            copy.start()
        g2[z] = gv[1]

    def mine(dz, dx):
        return acc[pl.ds(pl.multiple_of(chip(dz, dx) * SR, SR), SR), :]

    def reduce(first):
        right, left, up, down = dev(0, 1), dev(0, -1), dev(1, 0), dev(-1, 0)
        lo, hi, full = pl.ds(0, HS), pl.ds(HS, HS), pl.ds(0, SR)

        def put(i, slot, sem, device, rows=full):
            remote(sbuf.at[i, rows], rbuf.at[slot, rows], rs_s.at[0], rs_r.at[sem], device).start()

        def got(slot, sem, rows=full):
            view = rbuf.at[slot, rows]
            remote(view, view, rs_s.at[0], rs_r.at[sem], partner).wait_recv()

        def taken(slot, rows=full):
            return rbuf[slot, rows, :].astype(jnp.float32)

        if first == "x":
            rels = []
            for k in range(NZP, 0, -1):
                rels.append(k)
                if k > 1:
                    rels.append(-(k - 1))
            rels.append(0)
            zslot, zsem = 3 * Z, 4 * Z

            def one(i):
                sbuf[3 * i] = mine(rels[i], 2).astype(jnp.bfloat16)
                put(3 * i, 3 * i, 4 * i, right, lo)
                put(3 * i, 3 * i, 4 * i + 1, left, hi)

            def two(i):
                got(3 * i, 4 * i, lo)
                value = mine(rels[i], 1)
                sbuf[3 * i + 1, lo, :] = (value[:HS] + taken(3 * i, lo)).astype(jnp.bfloat16)
                sbuf[3 * i + 1, hi, :] = value[HS:].astype(jnp.bfloat16)
                put(3 * i + 1, 3 * i + 1, 4 * i + 2, right)
                got(3 * i, 4 * i + 1, hi)
                value = mine(rels[i], -1)
                sbuf[3 * i + 2, lo, :] = value[:HS].astype(jnp.bfloat16)
                sbuf[3 * i + 2, hi, :] = (value[HS:] + taken(3 * i, hi)).astype(jnp.bfloat16)
                put(3 * i + 2, 3 * i + 2, 4 * i + 3, left)

            def three(i):
                rel = rels[i]
                got(3 * i + 1, 4 * i + 2)
                got(3 * i + 2, 4 * i + 3)
                value = mine(rel, 0) + taken(3 * i + 1) + taken(3 * i + 2)
                if rel > 0:
                    slot = zslot + rel - 1
                    if rel < NZP:
                        got(slot + 1, zsem + rel)
                        value = value + taken(slot + 1)
                    sbuf[slot] = value.astype(jnp.bfloat16)
                    put(slot, slot, zsem + rel - 1, up)
                elif rel < 0:
                    slot = zslot + NZP - rel - 1
                    if -rel < NZM:
                        got(slot + 1, zsem + NZP - rel)
                        value = value + taken(slot + 1)
                    sbuf[slot] = value.astype(jnp.bfloat16)
                    put(slot, slot, zsem + NZP - rel - 1, down)
                else:
                    got(zslot, zsem)
                    value = value + taken(zslot)
                    if NZM:
                        got(zslot + NZP, zsem + NZP)
                        value = value + taken(zslot + NZP)
                    wgf[...] = value

            final(0)
            final(1)
            for i in range(Z + 4):
                if i < Z:
                    one(i)
                if i == 1:
                    final(-1)
                    final(2)
                if 0 <= i - 2 < Z:
                    two(i - 2)
                if 0 <= i - 4 < Z:
                    three(i - 4)
                if i == 2:
                    hook_a()
                if i == Z:
                    hook_b()
        else:
            rels = [2, 1, -1, 0]
            hops = [(NZP, NZM), (NZM, NZP), (NZP, NZM), (NZM, NZP)]
            zs = lambda xi, j: xi * (Z - 1) + j - 1
            xslot = 4 * (Z - 1)

            def link(xi, j, most, base, sign, device):
                value = mine(sign * j, rels[xi])
                slot = base + j - 1
                if j < most:
                    got(slot + 1, slot + 1)
                    value = value + taken(slot + 1)
                sbuf[slot] = value.astype(jnp.bfloat16)
                put(slot, slot, slot, device)

            def total(xi):
                most_p, most_m = hops[xi]
                base = xi * (Z - 1)
                value = mine(0, rels[xi])
                if most_p:
                    got(base, base)
                    value = value + taken(base)
                if most_m:
                    got(base + most_p, base + most_p)
                    value = value + taken(base + most_p)
                return value

            for k in (0, 1, -1):
                final(k)
            for t in range(NZP):
                if t == 1:
                    final(2)
                for xi in range(4):
                    most_p, most_m = hops[xi]
                    base = xi * (Z - 1)
                    if most_p - t >= 1:
                        link(xi, most_p - t, most_p, base, 1, up)
                    if most_m - t >= 1:
                        link(xi, most_m - t, most_m, base + most_p, -1, down)
                if t == 0:
                    hook_a()
                if t == NZP - 1:
                    hook_b()
            sbuf[xslot] = total(0).astype(jnp.bfloat16)
            put(xslot, xslot, xslot, right, lo)
            put(xslot, xslot, xslot + 1, left, hi)
            ahead, behind = total(1), total(2)
            sbuf[xslot + 1, hi, :] = ahead[HS:].astype(jnp.bfloat16)
            sbuf[xslot + 2, lo, :] = behind[:HS].astype(jnp.bfloat16)
            got(xslot, xslot, lo)
            sbuf[xslot + 1, lo, :] = (ahead[:HS] + taken(xslot, lo)).astype(jnp.bfloat16)
            put(xslot + 1, xslot + 1, xslot + 2, right)
            got(xslot, xslot + 1, hi)
            sbuf[xslot + 2, hi, :] = (behind[HS:] + taken(xslot, hi)).astype(jnp.bfloat16)
            put(xslot + 2, xslot + 2, xslot + 3, left)
            value = total(3)
            got(xslot + 1, xslot + 2)
            got(xslot + 2, xslot + 3)
            wgf[...] = value + taken(xslot + 1) + taken(xslot + 2)
        remote(sbuf, rbuf, rs_s.at[0], rs_r.at[0], partner).wait_send()

    @pl.when(c == 0)
    def _():
        reduce("x")

    @pl.when(c == 1)
    def _():
        reduce("z")

    grad = wgf[...]
    row_sum = jnp.sum(grad * grad + SQUARE_EPS, axis=-1, keepdims=True)
    eye = lax.broadcasted_iota(jnp.int32, (SR, SR), 0) == lax.broadcasted_iota(jnp.int32, (SR, SR), 1)
    row_old = jnp.sum(jnp.where(eye, jnp.broadcast_to(row_ref[...], (SR, SR)), 0.0), axis=-1, keepdims=True)
    row_new = DECAY_RATE * row_old + (1.0 - DECAY_RATE) * (row_sum / D)
    rown_ref[...] = jnp.sum(jnp.where(eye, jnp.broadcast_to(row_new, (SR, SR)), 0.0), axis=0, keepdims=True)
    per_row = 1.0 / row_new
    wgf[...] = grad * lax.rsqrt(row_new)
    tv[0, :, pl.ds(0, D)] = jnp.sum(grad * grad + SQUARE_EPS, axis=0, keepdims=True)
    tv[0, :, pl.ds(D, D)] = jnp.sum(grad * grad * per_row, axis=0, keepdims=True)
    tv[0, :, pl.ds(2 * D, 128)] = jnp.broadcast_to(jnp.sum(row_new, axis=0, keepdims=True), (1, 128))

    def exchange(copies, dst, place, value):
        for copy in copies:
            copy.start()
        dst[place] = value
        for copy in copies:
            copy.wait_recv()
        return added(dst)

    first = spread(tv.at[0], t1, x * 2 + c, near, t_s, t_r, 0)
    second = spread(tv.at[1], t2, z, far, t_s, t_r, 2 * X - 1)
    tv[1] = exchange(first, t1, x * 2 + c, tv[0])
    sums = exchange(second, t2, z, tv[1])
    col_new = DECAY_RATE * col_ref[...] + (1.0 - DECAY_RATE) * sums[:, 0:D] / D
    coln_ref[...] = col_new
    row_mean = sums[:, 2 * D : 2 * D + 1] / D
    total_square = row_mean * jnp.sum(sums[:, D : 2 * D] / col_new, axis=-1, keepdims=True)
    clip = jnp.maximum(1.0, jnp.sqrt(total_square / (D * D)))
    step_ref[...] = wgf[...] * (lax.rsqrt(col_new) * (jnp.sqrt(row_mean) / clip))
    for copy in gain_far():
        copy.wait_recv()
    gg_ref[...] = added(g2)

    own_copy().wait_send()

    @pl.when(c == 0)
    def _():
        gathered(cols_a)

    @pl.when(c == 1)
    def _():
        gathered(cols_b)

    for copy in first + second + gain_near() + gain_far():
        copy.wait_send()
    save().wait()
    for m in range(MICRO):
        nt_send(m).wait_send()
    shared = gs.at[:, pl.ds(0, TR)]
    remote(shared, shared, f_s.at[0], f_r.at[0], partner).wait_send()

    @pl.when(s > 0)
    def _():
        remote(outs, outs, y_s.at[0], y_r.at[0], partner).wait_send()


def deliver(*refs):
    n = 5
    sources, results, held, sems = refs[:n], refs[n : 2 * n], refs[2 * n : 3 * n], refs[-1]
    ways = []
    for src, mid, dst in zip(sources, held, results):
        pieces = src.shape[0] if len(src.shape) == 3 else 1
        for k in range(pieces):
            trio = (src.at[k], mid.at[k], dst.at[k]) if pieces > 1 else (src, mid, dst)
            half = trio[0].shape[0] // 2
            parts = [pl.ds(0, half), pl.ds(half, half)] if pieces > 1 else [None]
            for part in parts:
                a, m, b = trio if part is None else [ref.at[part] for ref in trio]
                i = len(ways)
                ways.append(
                    (
                        pltpu.make_async_copy(a, m, sems.at[0, i]),
                        pltpu.make_async_copy(m, b, sems.at[1, i]),
                    )
                )
    for into, _ in ways:
        into.start()
    for into, out in ways:
        into.wait()
        out.start()
    for _, out in ways:
        out.wait()


def body(saved_inputs, out_cotangent, weights, gains, row_state, col_state):
    S, DP = lax.axis_size("section"), lax.axis_size("dp")
    Z = DP // (2 * X)
    _, MICRO, TR, D = saved_inputs.shape
    SR = weights.shape[1]
    NC = DP // 2
    R = TR // 4
    CA = D * 9 // 16
    U = MICRO * (TR // R)
    bf, f32 = jnp.bfloat16, jnp.float32
    dma = pltpu.SemaphoreType.DMA
    vmem = pl.BlockSpec(memory_space=pltpu.VMEM)
    hbm = pl.BlockSpec(memory_space=pl.ANY)
    V = pltpu.VMEM
    scratch = [
        V((MICRO, TR, D), bf),
        V((MICRO, 2 * TR, D), bf),
        V((MICRO, TR, D), bf),
        V((NC, 2 * SR, D), bf),
        V((D, D), bf),
        V((MICRO, NC, 2, SR, TR), bf),
        V((MICRO, NC, SR, 2 * TR), bf),
        V((NC * SR, D), f32),
        V((R, D), f32),
        V((MICRO, TR, 128), f32),
        V((8, D), f32),
        V((SR, D), f32),
        V((NC - 1, SR, D), bf),
        V((NC - 1, SR, D), bf),
        V((2, 1, 2 * D + 128), f32),
        V((2 * X, 1, 2 * D + 128), f32),
        V((Z, 1, 2 * D + 128), f32),
        V((2, 1, D), f32),
        V((2 * X, 1, D), f32),
        V((Z, 1, D), f32),
        dma((2,)),
        dma((MICRO,)),
        dma((1,)),
        dma((1,)),
        dma((5 * Z,)),
        dma((1,)),
        dma((Z,)),
        dma((1,)),
        dma((1,)),
        dma((MICRO,)),
        dma((MICRO,)),
        dma((1,)),
        dma((U + 1,)),
        dma((1,)),
        dma((MICRO,)),
        dma((1,)),
        dma((5 * Z,)),
        dma((2 * X + Z,)),
        dma((2 * X + Z,)),
        dma((2 * X + Z,)),
        dma((2 * X + Z,)),
    ]
    outs = pl.pallas_call(
        functools.partial(kernel, S, Z, R, CA),
        out_shape=(
            jax.ShapeDtypeStruct((MICRO, TR, D), bf),
            jax.ShapeDtypeStruct((SR, D), f32),
            jax.ShapeDtypeStruct((1, SR), f32),
            jax.ShapeDtypeStruct((1, D), f32),
            jax.ShapeDtypeStruct((1, D), f32),
        ),
        in_specs=[hbm, hbm, vmem, vmem, vmem, vmem],
        out_specs=(hbm, vmem, vmem, vmem, vmem),
        scratch_shapes=scratch,
        compiler_params=pltpu.CompilerParams(
            collective_id=0, has_side_effects=True, vmem_limit_bytes=60 * 2**20
        ),
        name="relay_back",
    )(saved_inputs[0], out_cotangent, weights[0], gains, row_state, col_state)
    outs = pl.pallas_call(
        deliver,
        out_shape=tuple(jax.ShapeDtypeStruct(o.shape, o.dtype) for o in outs),
        in_specs=[hbm] * 5,
        out_specs=(hbm,) * 5,
        scratch_shapes=[V(o.shape, o.dtype) for o in outs] + [dma((2, 2 * MICRO + 4))],
        name="deliver",
    )(*outs)
    return (outs[0][None], outs[1][None], outs[2], outs[3], outs[4])


def solution(mesh):
    placed = (
        P("section", None, "dp", None),
        P(None, "dp", None),
        P("section", "dp", None),
        P("section", None),
        P("section", "dp"),
        P("section", None),
    )
    return jax.shard_map(
        body,
        mesh=mesh,
        in_specs=placed,
        out_specs=(
            P("section", None, "dp", None),
            P("section", "dp", None),
            P("section", "dp"),
            P("section", None),
            P("section", None),
        ),
        check_vma=False,
    )
```
